32 devices in a mesh: exp: 8 (over y, x, core), seq: 4 (over z).
Axes of the slice: x: 2, y: 2, z: 4, core: 2. Of those that a mesh axis runs over, the one named last changes fastest.
Arguments:
- tokens: bfloat16 [16, 1024, 768], P('exp', 'seq'), may hold values from -6 to 6
- cotangent: bfloat16 [16, 1024, 768], P('exp', 'seq'), may hold values from -6 to 6
- token_ids: int32 [16, 1024], P('exp', 'seq'), may hold values from 0 to 50256, as said below
- segments: int32 [16, 1024], P('exp'), may hold values from 0 to 4, as said below
- hash_table: int32 [50257], replicated, may hold values from 0 to 7
- w_qkv: bfloat16 [768, 2304], P(('exp', 'seq')), may hold values from -0.21875 to 0.21875
- w_attn_out: bfloat16 [768, 768], P(('exp', 'seq')), may hold values from -1.75 to 1.75
- norm_scale: bfloat16 [768, 2], P(('exp', 'seq')), may hold values from 0.099609375 to 1.8984375
- norm_shift: bfloat16 [768, 2], P(('exp', 'seq')), may hold values from -3 to 3
- w_in: bfloat16 [8, 768, 3072], P('exp'), may hold values from -0.21875 to 0.21875
- w_out: bfloat16 [8, 3072, 768], P('exp'), may hold values from -0.109375 to 0.109375
Outputs:
- layer_out: bfloat16 [16, 1024, 768], P('exp', 'seq')
- grad_tokens: float32 [16, 1024, 768], P('exp', 'seq')
- grad_w_qkv: float32 [768, 2304], P(('exp', 'seq'))
- grad_w_attn_out: float32 [768, 768], P(('exp', 'seq'))
- grad_norm_scale: float32 [768, 2], P(('exp', 'seq'))
- grad_norm_shift: float32 [768, 2], P(('exp', 'seq'))
- grad_w_in: float32 [8, 768, 3072], P('exp', None, 'seq')
- grad_w_out: float32 [8, 3072, 768], P('exp', 'seq')
The draws below stay inside these ranges and needn't reach their ends.
Inputs may be any that keep to these rules, and one draw needn't show every extreme that they name: `token_ids`: the rows of one device name at most 192 tokens that the table sends to one expert, and one expert gets exactly 192 from every device. `segments`: never falling along a sequence; in each sequence one document begins within the first 256 positions and ends within the last 256.
All inputs are finite; a program needn't handle non-finite values.
Results may differ from the reference program's by a relative error of at most 0.012.
Values may be sent and summed in bfloat16 or wider, within the bound.
No kernel may reach another device: no remote copies, remote signals or barrier semaphores. Data moves between devices by JAX's collectives and lax.ppermute only.
A program may use at most 256 MiB of HBM per device.

```python
import jax
import jax.numpy as jnp
from jax import lax

D = 768
HEADS = 12
HEAD_DIM = 64
HIDDEN_SIZE = 3072
VOCAB = 50257
LEN = 1024
SEQ_DEV = 2
EXPERTS = 8
SEQS = 16
ROWS_SEQ = 256
TOK_DEV = 512
SLOT = 192
TOKENS = 16384


def shared_shuffle(key):
    return jax.random.permutation(key, VOCAB)


def draw_hash_table(key, part):
    shuffled = shared_shuffle(key)
    return (shuffled % EXPERTS).astype(jnp.int32)


def draw_token_ids(key, part):
    shuffled = shared_shuffle(key)
    key = jax.random.fold_in(key, 3)
    inverse = jnp.argsort(shuffled)
    blocks = EXPERTS * (LEN // ROWS_SEQ)
    key_hot, key_order, key_pick = jax.random.split(key, 3)
    hot_expert = jax.random.randint(key_hot, (), 0, EXPERTS)
    row_index = jnp.arange(TOK_DEV, dtype=jnp.int32)
    other = (hot_expert + 1 + (row_index - SLOT) % (EXPERTS - 1)) % EXPERTS
    expert_base = jnp.where(row_index < SLOT, hot_expert, other)
    orders = jax.vmap(lambda sub_key: jax.random.permutation(sub_key, TOK_DEV))(jax.random.split(key_order, blocks))
    chosen = expert_base[orders]
    pick_index = jax.random.randint(key_pick, (blocks, TOK_DEV), 0, VOCAB // EXPERTS)
    token_all = inverse[chosen + EXPERTS * pick_index]
    token_all = token_all.reshape(EXPERTS, LEN // ROWS_SEQ, SEQ_DEV, ROWS_SEQ).transpose(0, 2, 1, 3).reshape(SEQS, LEN)
    return token_all.astype(jnp.int32)


def draw_segments(key, part):
    key = jax.random.fold_in(key, 5)
    key_first, key_before, key_late, key_last = jax.random.split(key, 4)
    first = jax.random.randint(key_first, (SEQS, 1), 2, ROWS_SEQ)
    before = jax.random.randint(key_before, (SEQS, 1), 1, first)
    late = jax.random.randint(key_late, (SEQS, 1), LEN - ROWS_SEQ, LEN - 1)
    ending = jax.random.randint(key_last, (SEQS, 1), late + 1, LEN)
    position = jnp.arange(LEN, dtype=jnp.int32)[None, :]
    counted = (position >= before).astype(jnp.int32) + (position >= first).astype(jnp.int32)
    counted = counted + (position >= late).astype(jnp.int32) + (position >= ending).astype(jnp.int32)
    return counted.astype(jnp.int32)


def block_levels(own_key, dims, cuts, least, top_value):
    loudness, own = 1.0, jax.random.fold_in(own_key, 6)
    for dim, shards_of in cuts:
        draws = jnp.exp(jax.random.uniform(jax.random.fold_in(own, dim), (shards_of,), jnp.float32, least / len(cuts), top_value / len(cuts)))
        loudness = loudness * jnp.repeat(draws, dims[dim] // shards_of).reshape([-1 if axis == dim else 1 for axis in range(len(dims))])
    return loudness


def bell_draw(key, shape, scale, bound, cuts=(), kind=jnp.bfloat16):
    loudness = block_levels(key, shape, cuts, -0.22, 0.18) if cuts else 1.0
    values = jax.random.normal(key, shape, jnp.float32) * scale * loudness
    return jnp.minimum(jnp.maximum(values, -bound), bound).astype(kind)


def setup_inputs(seed: int = 0) -> dict:
    streams_of = jax.random.split(jax.random.key(seed), 12)
    tokens = bell_draw(streams_of[0], (SEQS, LEN, D), 1.0, 6.0, ((0, 8), (1, 4)))
    cotangent = bell_draw(streams_of[1], (SEQS, LEN, D), 1.0, 6.0, ((0, 8), (1, 4)))
    token_ids = draw_token_ids(jax.random.fold_in(streams_of[11], 71), 0)
    segments = draw_segments(jax.random.fold_in(streams_of[11], 71), 0)
    hash_table = draw_hash_table(jax.random.fold_in(streams_of[11], 71), 0)
    w_qkv = bell_draw(streams_of[5], (D, 3 * D), D ** -0.5, 0.21875, ((0, 32),))
    w_attn_out = bell_draw(streams_of[6], (D, D), (D // 64) ** -0.5, 1.75, ((0, 32),))
    norm_scale = jnp.clip(1.0 + 0.18 * jax.random.normal(streams_of[7], (D, 2), jnp.float32), 0.099609375, 1.8984375).astype(jnp.bfloat16)
    norm_shift = bell_draw(streams_of[8], (D, 2), 0.5, 3.0, ((0, 32),))
    w_in = bell_draw(streams_of[9], (EXPERTS, D, HIDDEN_SIZE), D ** -0.5, 0.21875, ((0, 8),))
    w_out = bell_draw(streams_of[10], (EXPERTS, HIDDEN_SIZE, D), HIDDEN_SIZE ** -0.5, 0.109375, ((0, 8),))
    return dict(tokens=tokens, cotangent=cotangent, token_ids=token_ids, segments=segments, hash_table=hash_table, w_qkv=w_qkv, w_attn_out=w_attn_out, norm_scale=norm_scale, norm_shift=norm_shift, w_in=w_in, w_out=w_out)


@jax.custom_vjp
def low(v):
    return lax.optimization_barrier(v.astype(jnp.bfloat16)).astype(jnp.float32)

@jax.custom_vjp
def low_back(v):
    return v

def low_keep(v):
    return (low(v), None)

def low_pass(kept, grad):
    return (grad,)

def back_keep(v):
    return (v, None)

def back_low(kept, grad):
    return (low(grad),)
low.defvjp(low_keep, low_pass)
low_back.defvjp(back_keep, back_low)
epsilon = 1e-05
precise = lax.Precision.HIGHEST

def layer_norm(feature, gain_col, bias_col):
    center = feature - lax.optimization_barrier(jnp.mean(feature, axis=-1, keepdims=True))
    spread = lax.optimization_barrier(jnp.mean(center * center, axis=-1, keepdims=True))
    return center * lax.rsqrt(spread + epsilon) * gain_col + bias_col

def attend_group(queries, key_full, value_full, seg_ids):
    scores = jnp.einsum('sqhd,skhd->shqk', queries, key_full, precision=precise) * HEAD_DIM ** (-0.5)
    scores = low_back(scores)
    position = jnp.arange(LEN, dtype=jnp.int32)
    causal = position[:, None] >= position[None, :]
    allowed = causal[None] & (seg_ids[:, :, None] == seg_ids[:, None, :])
    scores = jnp.where(allowed[:, None], scores, -1e+30)
    weights = low(jax.nn.softmax(scores, axis=-1))
    return jnp.einsum('shqk,skhd->sqhd', weights, value_full, precision=precise)

def attend_entry(entry):
    shaped, seg_ids = entry
    return jax.checkpoint(attend_group)(shaped[:, :, 0], shaped[:, :, 1], shaped[:, :, 2], seg_ids)

def expert_ffn(packed, weight_in, weight_out):
    hidden_pre = low_back(jnp.dot(packed, weight_in, precision=precise))
    hidden_act = low(jax.nn.gelu(hidden_pre, approximate=True))
    return low_back(low(jnp.dot(hidden_act, weight_out, precision=precise)))

def expert_entry(entry):
    return jax.checkpoint(expert_ffn)(entry[0], entry[1], entry[2])

def forward(tokens, w_qkv, w_attn_out, norm_scale, norm_shift, w_in, w_out, token_ids, segments, hash_table):
    tok_rows = tokens.reshape(TOKENS, D)
    normed = low(layer_norm(tok_rows, norm_scale[:, 0], norm_shift[:, 0]))
    qkv = low_back(low(jnp.dot(normed, w_qkv, precision=precise)))
    group = 4 if SEQS % 4 == 0 else 1
    shaped = qkv.reshape(SEQS // group, group, LEN, 3, HEADS, HEAD_DIM)
    seg_groups = segments.reshape(SEQS // group, group, LEN)
    attended = lax.map(attend_entry, (shaped, seg_groups))
    mixed = low_back(low(attended.reshape(TOKENS, D)))
    middle = tok_rows + low_back(jnp.dot(mixed, w_attn_out, precision=precise))
    sent = low_back(low(layer_norm(middle, norm_scale[:, 1], norm_shift[:, 1])))
    expert = hash_table[token_ids.reshape(-1)].astype(jnp.int32)
    onehot = (expert[:, None] == jnp.arange(EXPERTS, dtype=jnp.int32)[None, :]).astype(jnp.int32)
    slot_rank = lax.optimization_barrier(jnp.sum(jnp.cumsum(onehot, axis=0) * onehot, axis=1)) - 1
    capacity = SLOT * EXPERTS * (LEN // ROWS_SEQ)
    slot_index = (expert * capacity + slot_rank).astype(jnp.int32)
    packed = jnp.zeros((EXPERTS * capacity, D), tok_rows.dtype).at[slot_index].set(sent)
    returned = lax.map(expert_entry, (packed.reshape(EXPERTS, capacity, D), w_in, w_out))
    result = middle + returned.reshape(EXPERTS * capacity, D)[slot_index]
    return result.reshape(SEQS, LEN, D)

def reference(tokens, cotangent, token_ids, segments, hash_table, w_qkv, w_attn_out, norm_scale, norm_shift, w_in, w_out):

    def closed(tok_f, qkv_f, out_f, gain_f, bias_f, inner_f, outer_f):
        return forward(tok_f, qkv_f, out_f, gain_f, bias_f, inner_f, outer_f, token_ids, segments, hash_table)
    result, pull = jax.vjp(closed, tokens.astype(jnp.float32), w_qkv.astype(jnp.float32), w_attn_out.astype(jnp.float32), norm_scale.astype(jnp.float32), norm_shift.astype(jnp.float32), w_in.astype(jnp.float32), w_out.astype(jnp.float32))
    grads = pull(cotangent.astype(jnp.float32))
    return (result.astype(jnp.bfloat16), grads[0], grads[1], grads[2], grads[3], grads[4], grads[5], grads[6])
```

```python
import functools

import jax
import jax.numpy as jnp
from jax import lax
from jax.experimental import pallas as pl
from jax.experimental.pallas import tpu as pltpu
from jax.sharding import PartitionSpec as P

HEAD_DIM = 64
LANES = 128
BOTH = ("exp", "seq")
epsilon = 1e-05
f32 = jnp.float32
bf16 = jnp.bfloat16


def gelu_tanh(feature):
    return jax.nn.gelu(feature, approximate=True)


def norm_parts(feature):
    center = feature - jnp.mean(feature, axis=-1, keepdims=True)
    spread = jnp.mean(center * center, axis=-1, keepdims=True)
    rstd = lax.rsqrt(spread + epsilon)
    return center * rstd, rstd


def norm_pull(grad_hat, hat, rstd):
    first = jnp.mean(grad_hat, axis=-1, keepdims=True)
    second = jnp.mean(grad_hat * hat, axis=-1, keepdims=True)
    return rstd * (grad_hat - first - hat * second)


def pick(array, index, axis=0):
    return lax.dynamic_index_in_dim(array, index, axis, keepdims=False)


def order_by_xor(parts, index):
    bit = 0
    while (1 << bit) < len(parts):
        flag = ((index >> bit) & 1) == 1
        parts = [
            jnp.where(flag, parts[place ^ (1 << bit)], parts[place]) for place in range(len(parts))
        ]
        bit += 1
    return parts


def nt(a, b):
    return lax.dot_general(a, b, (((1,), (1,)), ((), ())), preferred_element_type=f32)


def nn(a, b):
    return lax.dot_general(a, b, (((1,), (0,)), ((), ())), preferred_element_type=f32)


def tn(a, b):
    return lax.dot_general(a, b, (((0,), (0,)), ((), ())), preferred_element_type=f32)


def allowed_keys(segc_ref, segr_ref, start, block):
    width = start + block
    keys = lax.broadcasted_iota(jnp.int32, (width, block), 0)
    queries = lax.broadcasted_iota(jnp.int32, (width, block), 1) + start
    same = segc_ref[0:width, :] == segr_ref[:, start : start + block]
    return same & (keys <= queries)


def attend_kernel(q_ref, k_ref, v_ref, segc_ref, segr_ref, att_ref, lse_ref, *, block):
    total = q_ref.shape[0]
    values_t = v_ref[...].astype(f32).T.astype(bf16)
    lane = lax.broadcasted_iota(jnp.int32, (block, LANES), 1)
    for start in range(0, total, block):
        width = start + block
        allowed = allowed_keys(segc_ref, segr_ref, start, block)
        queries = q_ref[start:width, :] * 0.125
        outs = []
        for head in range(2):
            own = (lane >= HEAD_DIM) if head else (lane < HEAD_DIM)
            q_head = jnp.where(own, queries, 0.0).astype(bf16)
            scores = jnp.where(allowed, nt(k_ref[0:width, :], q_head), -1e30)
            top = jnp.max(scores, axis=0, keepdims=True)
            expo = jnp.exp(scores - top)
            total_row = jnp.sum(expo, axis=0, keepdims=True)
            out = nn(values_t[head * HEAD_DIM : (head + 1) * HEAD_DIM, 0:width], expo.astype(bf16))
            outs.append(out / total_row)
            lse_ref[0, head : head + 1, start:width] = top + jnp.log(total_row)
        att_ref[start:width, :] = jnp.concatenate(outs, axis=0).T.astype(bf16)


def attend(qkv, seg_col, seg_row):
    total, width = qkv.shape
    pairs = width // 3 // LANES
    block = min(256, total)
    column = lambda part: pl.BlockSpec((total, LANES), lambda h: (0, part * pairs + h))
    return pl.pallas_call(
        functools.partial(attend_kernel, block=block),
        grid=(pairs,),
        in_specs=[
            column(0),
            column(1),
            column(2),
            pl.BlockSpec((total, 1), lambda h: (0, 0)),
            pl.BlockSpec((1, total), lambda h: (0, 0)),
        ],
        out_specs=[
            pl.BlockSpec((total, LANES), lambda h: (0, h)),
            pl.BlockSpec((1, 8, total), lambda h: (h, 0, 0)),
        ],
        out_shape=[
            jax.ShapeDtypeStruct((total, pairs * LANES), bf16),
            jax.ShapeDtypeStruct((pairs, 8, total), f32),
        ],
        compiler_params=pltpu.CompilerParams(vmem_limit_bytes=48 << 20),
        cost_estimate=pl.CostEstimate(
            flops=4 * total * total * width // 6,
            bytes_accessed=2 * total * width * 2,
            transcendentals=total * total * width // 3 // HEAD_DIM // 2,
        ),
        name="attend",
    )(qkv, qkv, qkv, seg_col, seg_row)


def attend_back_kernel(
    q_ref,
    k_ref,
    v_ref,
    att_ref,
    datt_ref,
    lse_ref,
    segc_ref,
    segr_ref,
    out_ref,
    dk_ref,
    dv_ref,
    *,
    block,
):
    total = q_ref.shape[0]
    pairs = pl.num_programs(0)
    pair = pl.program_id(0)
    lane = lax.broadcasted_iota(jnp.int32, (block, LANES), 1)
    lane_all = lax.broadcasted_iota(jnp.int32, (total, LANES), 1)
    dk_ref[...] = jnp.zeros_like(dk_ref)
    dv_ref[...] = jnp.zeros_like(dv_ref)
    row8 = lax.broadcasted_iota(jnp.int32, (8, LANES), 0)
    lane8 = lax.broadcasted_iota(jnp.int32, (8, LANES), 1)
    head_rows = jnp.where(row8 == lane8 // HEAD_DIM, 1.0, 0.0)

    def column(part):
        return pl.ds(pl.multiple_of((part * pairs + pair) * LANES, LANES), LANES)

    for start in range(0, total, block):
        width = start + block
        allowed = allowed_keys(segc_ref, segr_ref, start, block)
        queries = q_ref[start:width, :] * 0.125
        grads = datt_ref[start:width, :]
        product = grads.astype(f32) * att_ref[start:width, :].astype(f32)
        delta = lax.dot_general(
            head_rows,
            product,
            (((1,), (1,)), ((), ())),
            precision=lax.Precision.HIGHEST,
            preferred_element_type=f32,
        )
        dq = jnp.zeros((block, LANES), f32)
        for head in range(2):
            own = (lane >= HEAD_DIM) if head else (lane < HEAD_DIM)
            own_all = (lane_all >= HEAD_DIM) if head else (lane_all < HEAD_DIM)
            q_head = jnp.where(own, queries, 0.0).astype(bf16)
            g_head = jnp.where(own, grads, 0.0).astype(bf16)
            k_head = jnp.where(own_all[0:width], k_ref[0:width, :], 0.0).astype(bf16)
            scores = nt(k_ref[0:width, :], q_head)
            probs = jnp.where(allowed, jnp.exp(scores - lse_ref[0, head : head + 1, start:width]), 0.0)
            dprobs = nt(v_ref[0:width, :], g_head)
            dscores = (probs * (dprobs - delta[head : head + 1, :])).astype(bf16)
            dv_ref[0:width, :] += nn(probs.astype(bf16), g_head)
            dk_ref[0:width, :] += nn(dscores, q_head)
            dq = dq + tn(dscores, k_head)
        out_ref[start:width, column(0)] = (dq * 0.125).astype(bf16)
    out_ref[:, column(1)] = dk_ref[...].astype(bf16)
    out_ref[:, column(2)] = dv_ref[...].astype(bf16)


def attend_back(qkv, att, datt, lse, seg_col, seg_row):
    total, width = qkv.shape
    pairs = width // 3 // LANES
    block = min(256, total)
    column = lambda part: pl.BlockSpec((total, LANES), lambda h: (0, part * pairs + h))
    return pl.pallas_call(
        functools.partial(attend_back_kernel, block=block),
        grid=(pairs,),
        in_specs=[
            column(0),
            column(1),
            column(2),
            column(0),
            column(0),
            pl.BlockSpec((1, 8, total), lambda h: (h, 0, 0)),
            pl.BlockSpec((total, 1), lambda h: (0, 0)),
            pl.BlockSpec((1, total), lambda h: (0, 0)),
        ],
        out_specs=pl.BlockSpec((total, width), lambda h: (0, 0)),
        out_shape=jax.ShapeDtypeStruct((total, width), bf16),
        scratch_shapes=[pltpu.VMEM((total, LANES), f32), pltpu.VMEM((total, LANES), f32)],
        compiler_params=pltpu.CompilerParams(vmem_limit_bytes=48 << 20),
        cost_estimate=pl.CostEstimate(
            flops=10 * total * total * width // 6,
            bytes_accessed=3 * total * width * 2,
            transcendentals=total * total * width // 3 // HEAD_DIM // 2,
        ),
        name="attend_back",
    )(qkv, qkv, qkv, att, datt, lse, seg_col, seg_row)


def make_local(exp_size, seq_size):
    cols = exp_size // 2
    col_bits = cols.bit_length() - 1

    def flat_perm(target):
        pairs = []
        for exp in range(exp_size):
            for seq in range(seq_size):
                col, core = exp >> 1, exp & 1
                new_col, new_core, new_seq = target(col, core, seq)
                pairs.append((exp * seq_size + seq, (new_col * 2 + new_core) * seq_size + new_seq))
        return pairs

    def send(array, target):
        return lax.ppermute(array, BOTH, flat_perm(target))

    def to_core(array):
        return send(array, lambda c, k, z: (c, 1 - k, z))

    def to_seq(array, shift):
        return send(array, lambda c, k, z: (c, k, z ^ shift))

    def to_col(array, bit):
        return send(array, lambda c, k, z: (c ^ (1 << bit), k, z))

    def home_of(i):
        return lambda c, k, z: (c, z >> 1, (2 * k + (z & 1)) ^ i)

    def worker_of(i):
        return lambda c, k, z: (c, (z ^ i) >> 1, 2 * k + ((z ^ i) & 1))

    def local(
        tokens,
        cotangent,
        token_ids,
        segments,
        hash_table,
        w_qkv,
        w_attn_out,
        norm_scale,
        norm_shift,
        w_in,
        w_out,
    ):
        seq_dev, rows_seq, width = tokens.shape
        rows = seq_dev * rows_seq
        slot_rows = 3 * rows // exp_size
        full_len = rows_seq * seq_size
        half = width // 2
        part_rows = w_qkv.shape[0]
        exp_at = lax.axis_index("exp")
        z = lax.axis_index("seq")
        k = exp_at & 1
        c = exp_at >> 1

        norms = jnp.concatenate([norm_scale, norm_shift], axis=1)
        norms = jnp.pad(norms, ((0, 0), (0, LANES - norms.shape[1])))
        qkv_parts = w_qkv.reshape(part_rows, 3, 2, half)
        packs = [
            jnp.concatenate(
                [qkv_parts[:, i, core] for i in range(3)]
                + [w_attn_out[:, core * half : (core + 1) * half], norms],
                axis=1,
            )
            for core in range(2)
        ]
        is_one = k == 1
        keep = jnp.where(is_one, packs[1], packs[0])
        away = to_core(jnp.where(is_one, packs[0], packs[1]))
        pair = jnp.stack([jnp.where(is_one, away, keep), jnp.where(is_one, keep, away)])
        got = [pair] + [to_seq(pair, i) for i in range(1, seq_size)]
        gathered = jnp.stack(order_by_xor(got, z), axis=1)
        wide = gathered.shape[-1]
        halves = []
        for kk in range(2):
            block = gathered[kk]
            bits = list(range(col_bits))
            if kk:
                bits = bits[::-1]
            done = []
            for bit in bits:
                other = to_col(block, bit)
                flag = ((c >> bit) & 1) == 1
                place = sum(1 for b in done if b > bit)
                block = jnp.stack(
                    [jnp.where(flag, other, block), jnp.where(flag, block, other)], axis=place
                )
                done.append(bit)
            halves.append(block.reshape(cols, seq_size * part_rows, wide))
        weights = jnp.stack(halves, axis=1).reshape(width, wide)
        wq = weights[:, : 3 * half]
        wo_own = weights[:, 3 * half : 4 * half]
        wo_other = to_core(wo_own)
        wo = jnp.concatenate(
            [jnp.where(is_one, wo_other, wo_own), jnp.where(is_one, wo_own, wo_other)], axis=1
        )
        norm_rows = weights[:, 4 * half : 4 * half + 4].astype(f32).T
        gain_one, gain_two, bias_one, bias_two = (norm_rows[i : i + 1] for i in range(4))

        z0 = z & 1
        here_a = send(pick(tokens, z0), home_of(0))
        here_b = send(pick(tokens, 1 - z0), home_of(1))
        flip = z0 == 1
        x_half = jnp.concatenate(
            [jnp.where(flip, here_b, here_a), jnp.where(flip, here_a, here_b)], axis=0
        )
        x_other = to_core(x_half)
        x_seq = jnp.concatenate(
            [jnp.where(is_one, x_other, x_half), jnp.where(is_one, x_half, x_other)], axis=0
        )
        seg_other = to_core(segments)
        seg_pair = jnp.where((z >> 1) == k, segments, seg_other)
        seg_row = pick(seg_pair, z0)[None, :]
        seg_col = seg_row.reshape(full_len, 1)

        expert = hash_table[token_ids.reshape(-1)]
        order = jnp.arange(rows, dtype=jnp.int32)
        earlier = (expert[None, :] == expert[:, None]) & (order[None, :] < order[:, None])
        slot_rank = jnp.sum(earlier.astype(jnp.int32), axis=1)
        slot_index = expert * slot_rows + slot_rank
        slots = exp_size * slot_rows
        spread = (jnp.arange(slots, dtype=jnp.int32)[:, None] == slot_index[None, :]).astype(bf16)

        def swap(array):
            return lax.all_to_all(
                array.reshape(exp_size, slot_rows, width),
                "exp",
                split_axis=0,
                concat_axis=0,
                tiled=True,
            ).reshape(slots, width)

        grad_low = cotangent.reshape(rows, width)
        grad_arrived = swap(nn(spread, grad_low).astype(bf16))

        hat_seq, _ = norm_parts(x_seq.astype(f32))
        normed = (hat_seq * gain_one + bias_one).astype(bf16)
        qkv = nn(normed, wq).astype(bf16)
        att, lse = attend(qkv, seg_col, seg_row)

        chunk_at = 2 * k + z0
        att_chunks = att.reshape(seq_size, rows_seq, half)
        came = [send(pick(att_chunks, chunk_at ^ i), home_of(i)) for i in range(4)]
        quads = order_by_xor(came, z)
        att_home = jnp.concatenate(
            [
                jnp.concatenate([quads[0], quads[2]], axis=1),
                jnp.concatenate([quads[1], quads[3]], axis=1),
            ],
            axis=0,
        )
        tok_rows = tokens.reshape(rows, width).astype(f32)
        middle = tok_rows + nn(att_home, wo)
        hat_two, rstd_two = norm_parts(middle)
        sent = (hat_two * gain_two + bias_two).astype(bf16)

        arrived = swap(nn(spread, sent).astype(bf16))
        hidden_pre = nn(arrived, w_in[0])
        hidden_act = gelu_tanh(hidden_pre).astype(bf16)
        grad_outer = tn(hidden_act, grad_arrived).astype(bf16)
        grad_w_out = lax.psum_scatter(grad_outer, "seq", scatter_dimension=0, tiled=True)
        grad_act = nt(grad_arrived, w_out[0])
        grad_pre = jax.vjp(gelu_tanh, hidden_pre)[1](grad_act)[0].astype(bf16)
        grad_sent = nt(grad_pre, w_in[0]).astype(bf16)
        grad_back = swap(grad_sent)
        grad_inner = tn(arrived, grad_pre).astype(bf16)
        grad_w_in = lax.psum_scatter(grad_inner, "seq", scatter_dimension=1, tiled=True)
        returned = swap(nn(hidden_act, w_out[0]).astype(bf16))
        layer_out = (middle + tn(spread, returned)).astype(bf16)

        grad_normed2 = tn(spread, grad_back)
        grad_middle = grad_low.astype(f32) + norm_pull(grad_normed2 * gain_two, hat_two, rstd_two)
        grad_gain_two = jnp.sum(grad_normed2 * hat_two, axis=0, keepdims=True)
        grad_bias_two = jnp.sum(grad_normed2, axis=0, keepdims=True)
        grad_branch = grad_middle.astype(bf16)
        grad_att = nt(grad_branch, wo).astype(bf16)

        quads = grad_att.reshape(seq_dev, rows_seq, 2, half)
        quads = jnp.stack([quads[:, :, 0], quads[:, :, 1]]).reshape(4, rows_seq, half)
        came = [send(pick(quads, z ^ i), worker_of(i)) for i in range(4)]
        datt = jnp.concatenate(order_by_xor(came, chunk_at), axis=0)
        dqkv = attend_back(qkv, att, datt, lse, seg_col, seg_row)
        partial = nt(dqkv, wq)
        partial = partial.reshape(2, rows, width)
        grad_normed = pick(partial, k) + to_core(pick(partial, 1 - k).astype(bf16)).astype(f32)
        hat_half = pick(hat_seq.reshape(2, rows, width), k)
        grad_gain_one = jnp.sum(grad_normed * hat_half, axis=0, keepdims=True)
        grad_bias_one = jnp.sum(grad_normed, axis=0, keepdims=True)
        back = grad_normed.astype(bf16).reshape(2, rows_seq, width)
        back_a = send(pick(back, z0), home_of(0))
        back_b = send(pick(back, 1 - z0), home_of(1))
        normed_home = jnp.concatenate(
            [jnp.where(flip, back_b, back_a), jnp.where(flip, back_a, back_b)], axis=0
        ).astype(f32)
        hat_one, rstd_one = norm_parts(tok_rows)
        grad_tokens = grad_middle + norm_pull(normed_home * gain_one, hat_one, rstd_one)

        grad_wo = tn(att_home, grad_branch).reshape(width, 2, half)
        grad_wo = pick(grad_wo, k, 1) + to_core(pick(grad_wo, 1 - k, 1).astype(bf16)).astype(f32)
        grad_wq = tn(normed, dqkv)
        small = jnp.concatenate([grad_gain_one, grad_gain_two, grad_bias_one, grad_bias_two], axis=0)
        small = jnp.pad(small, ((0, LANES - 4), (0, 0))).T
        whole = jnp.concatenate([grad_wq, grad_wo, small], axis=1)
        whole = whole.reshape(cols, 2, seq_size * part_rows, wide)
        sums = []
        for kk in range(2):
            block = whole[:, kk].reshape((2,) * col_bits + (seq_size * part_rows, wide))
            bits = list(range(col_bits))
            if kk:
                bits = bits[::-1]
            left = list(range(col_bits))[::-1]
            for bit in bits:
                axis = left.index(bit)
                own_bit = (c >> bit) & 1
                away = to_col(pick(block, 1 - own_bit, axis).astype(bf16), bit)
                block = pick(block, own_bit, axis) + away.astype(f32)
                left.remove(bit)
            sums.append(block)
        own = jnp.where(is_one, sums[1], sums[0])
        away = to_core(jnp.where(is_one, sums[0], sums[1]).astype(bf16)).astype(f32)
        merged = [
            jnp.where(is_one, away, own)[:, : 4 * half],
            jnp.where(is_one, own, away)[:, : 4 * half],
            (own + away)[:, 4 * half :],
        ]
        merged = jnp.concatenate(merged, axis=1).reshape(seq_size, part_rows, 8 * half + LANES)
        final = pick(merged, z)
        for i in range(1, seq_size):
            final = final + to_seq(pick(merged, z ^ i).astype(bf16), i).astype(f32)
        pieces = [final[:, i * half : (i + 1) * half] for i in range(8)]
        grad_w_qkv = jnp.concatenate([pieces[i] for i in (0, 4, 1, 5, 2, 6)], axis=1)
        grad_w_attn_out = jnp.concatenate([pieces[3], pieces[7]], axis=1)
        grad_norms = final[:, 8 * half : 8 * half + 4]
        return (
            layer_out.reshape(seq_dev, rows_seq, width),
            grad_tokens.reshape(seq_dev, rows_seq, width),
            grad_w_qkv,
            grad_w_attn_out,
            grad_norms[:, 0:2],
            grad_norms[:, 2:4],
            grad_w_in.astype(f32)[None],
            grad_w_out.astype(f32)[None],
        )

    return local


def solution(mesh):
    return jax.shard_map(
        make_local(mesh.shape["exp"], mesh.shape["seq"]),
        mesh=mesh,
        in_specs=(
            P("exp", "seq", None),
            P("exp", "seq", None),
            P("exp", "seq"),
            P("exp", None),
            P(),
            P(("exp", "seq"), None),
            P(("exp", "seq"), None),
            P(("exp", "seq"), None),
            P(("exp", "seq"), None),
            P("exp", None, None),
            P("exp", None, None),
        ),
        out_specs=(
            P("exp", "seq", None),
            P("exp", "seq", None),
            P(("exp", "seq"), None),
            P(("exp", "seq"), None),
            P(("exp", "seq"), None),
            P(("exp", "seq"), None),
            P("exp", None, "seq"),
            P("exp", "seq", None),
        ),
        check_vma=False,
    )
```

```python
import functools

import jax
import jax.numpy as jnp
from jax import lax
from jax.experimental import pallas as pl
from jax.experimental.pallas import tpu as pltpu
from jax.sharding import PartitionSpec as P

HEAD_DIM = 64
LANES = 128
BOTH = ("exp", "seq")
epsilon = 1e-05
f32 = jnp.float32
bf16 = jnp.bfloat16


def norm_parts(feature):
    center = feature - jnp.mean(feature, axis=-1, keepdims=True)
    spread = jnp.mean(center * center, axis=-1, keepdims=True)
    rstd = lax.rsqrt(spread + epsilon)
    return center * rstd, rstd


def norm_pull(grad_hat, hat, rstd):
    first = jnp.mean(grad_hat, axis=-1, keepdims=True)
    second = jnp.mean(grad_hat * hat, axis=-1, keepdims=True)
    return rstd * (grad_hat - first - hat * second)


def nt(a, b):
    return lax.dot_general(a, b, (((1,), (1,)), ((), ())), preferred_element_type=f32)


def nn(a, b):
    return lax.dot_general(a, b, (((1,), (0,)), ((), ())), preferred_element_type=f32)


def tn(a, b):
    return lax.dot_general(a, b, (((0,), (0,)), ((), ())), preferred_element_type=f32)


def after(value, *earlier):
    return lax.optimization_barrier((value, earlier))[0]


def aligned(index, size, unit=None):
    return pl.ds(pl.multiple_of(index * size, unit or size), size)


def whole_block(*shape):
    return pl.BlockSpec(shape, lambda i, at: (0,) * len(shape))


def kernel_call(body, steps, at, arrays, in_specs, out_specs, out_shape, flops, name, scratch=()):
    in_specs = [spec or whole_block(*a.shape) for spec, a in zip(in_specs, arrays)]
    out_specs = [spec or whole_block(*o.shape) for spec, o in zip(out_specs, out_shape)]
    moved = sum(a.size * a.dtype.itemsize for a in (*arrays, *out_shape))
    return pl.pallas_call(
        body,
        grid_spec=pltpu.PrefetchScalarGridSpec(
            num_scalar_prefetch=1,
            grid=(steps,),
            in_specs=in_specs,
            out_specs=out_specs,
            scratch_shapes=list(scratch),
        ),
        out_shape=list(out_shape),
        compiler_params=pltpu.CompilerParams(vmem_limit_bytes=56 << 20),
        cost_estimate=pl.CostEstimate(flops=flops, bytes_accessed=moved, transcendentals=0),
        name=name,
    )(at, *arrays)


def single_call(body, at, arrays, out_shape, name, flops=0, scratch=()):
    return kernel_call(
        body,
        1,
        at,
        arrays,
        [None] * len(arrays),
        [None] * len(out_shape),
        out_shape,
        flops,
        name,
        scratch,
    )


def shape(kind, *dims):
    return jax.ShapeDtypeStruct(dims, kind)


CORE, FLAT, LOW, SEQ, EXP, CHUNK = range(6)


def allowed_keys(segc_ref, segr_ref, start, block):
    width = start + block
    keys = lax.broadcasted_iota(jnp.int32, (width, block), 0)
    queries = lax.broadcasted_iota(jnp.int32, (width, block), 1) + start
    same = segc_ref[0:width, :] == segr_ref[:, start : start + block]
    return same & (keys <= queries)


def split_kernel(at_ref, *refs, half, parts):
    got, (mine_ref, other_ref) = refs[:parts], refs[parts:]

    def fill(core):
        for i in range(parts):
            for ref, which in ((mine_ref, core), (other_ref, 1 - core)):
                for group in range(4):
                    start = (2 * group + which) * half
                    ref[i, :, group * half : (group + 1) * half] = got[i][:, start : start + half]
                ref[i, :, 4 * half :] = got[i][:, 8 * half :]

    pl.when(at_ref[CORE] == 0)(lambda: fill(0))
    pl.when(at_ref[CORE] == 1)(lambda: fill(1))


def norm_qkv_kernel(at_ref, *refs, half, parts, cols):
    pieces, (own_ref, other_ref) = refs[: 2 * cols], refs[2 * cols : 2 * cols + 2]
    wq_ref, wo_ref, rows_ref, normed_ref, qkv_ref, norm_ref = refs[2 * cols + 2 :]
    for kk in range(2):
        for m in range(cols):
            for i in range(parts):
                place = at_ref[FLAT] ^ ((2 * m + kk) * parts + i)
                block = pieces[kk * cols + m]
                wq_ref[place] = block[i, :, : 3 * half]
                wo_ref[place] = block[i, :, 3 * half : 4 * half]
                norm_ref[place] = block[i, :, 4 * half :].astype(f32)
    width = own_ref.shape[1]
    norm_rows = norm_ref[...].reshape(width, LANES).T[0:8]
    rows_ref[...] = norm_rows
    weights = wq_ref[...].reshape(width, 3 * half)
    rows = own_ref.shape[0]
    core = at_ref[CORE]
    for ref, place in ((own_ref, core), (other_ref, 1 - core)):
        hat, _ = norm_parts(ref[...].astype(f32))
        normed = (hat * norm_rows[0:1] + norm_rows[2:3]).astype(bf16)
        where = aligned(place, rows)
        normed_ref[where, :] = normed
        qkv_ref[where, :] = nn(normed, weights).astype(bf16)


GELU_ONE = 0.7978845608028654
GELU_TWO = GELU_ONE * 0.044715


def attend_kernel(at_ref, q_ref, k_ref, v_ref, segc_ref, segr_ref, att_ref, lse_ref, *outs_ref, block):
    total = q_ref.shape[0]
    values_t = v_ref[...].astype(f32).T.astype(bf16)
    lane = lax.broadcasted_iota(jnp.int32, (block, LANES), 1)
    for start in range(0, total, block):
        width = start + block
        allowed = allowed_keys(segc_ref, segr_ref, start, block)
        queries = q_ref[start:width, :] * 0.125
        outs = []
        for head in range(2):
            own = (lane >= HEAD_DIM) if head else (lane < HEAD_DIM)
            q_head = jnp.where(own, queries, 0.0).astype(bf16)
            scores = jnp.where(allowed, nt(k_ref[0:width, :], q_head), -1e30)
            top = jnp.max(scores, axis=0, keepdims=True)
            expo = jnp.exp(scores - top)
            total_row = jnp.sum(expo, axis=0, keepdims=True)
            out = nn(values_t[head * HEAD_DIM : (head + 1) * HEAD_DIM, 0:width], expo.astype(bf16))
            outs.append(out / total_row)
            lse_ref[0, head : head + 1, start:width] = top + jnp.log(total_row)
        att_ref[start:width, :] = jnp.concatenate(outs, axis=0).T.astype(bf16)
    rows = outs_ref[0].shape[0]
    for i, ref in enumerate(outs_ref):
        ref[...] = att_ref[aligned(at_ref[CHUNK] ^ i, rows), :]


def head_specs(total, pairs):
    return [
        pl.BlockSpec((total, LANES), lambda h, at, part=part: (0, part * pairs + h))
        for part in range(3)
    ]


def attend(at, qkv, seg_col, seg_row, chunks):
    total, width = qkv.shape
    pairs = width // 3 // LANES
    rows = total // chunks
    piece = pl.BlockSpec((rows, LANES), lambda h, at: (0, h))
    return kernel_call(
        functools.partial(attend_kernel, block=min(256, total)),
        pairs,
        at,
        [qkv, qkv, qkv, seg_col, seg_row],
        head_specs(total, pairs) + [None, None],
        [
            pl.BlockSpec((total, LANES), lambda h, at: (0, h)),
            pl.BlockSpec((1, 8, total), lambda h, at: (h, 0, 0)),
        ]
        + [piece] * chunks,
        [shape(bf16, total, pairs * LANES), shape(f32, pairs, 8, total)]
        + [shape(bf16, rows, pairs * LANES)] * chunks,
        4 * total * total * width // 6,
        "attend",
    )


def attend_back_kernel(
    at_ref, q_ref, k_ref, v_ref, att_ref, lse_ref, segc_ref, segr_ref, *refs, block, chunks
):
    came, (wq_ref, wk_ref, wv_ref) = refs[:chunks], refs[chunks : chunks + 3]
    out_ref, own_ref, other_ref, dk_ref, dv_ref, datt_ref, sum_ref = refs[chunks + 3 :]
    total = q_ref.shape[0]
    pairs = pl.num_programs(0)
    pair = pl.program_id(0)
    for i, ref in enumerate(came):
        datt_ref[aligned(at_ref[CHUNK] ^ i, total // chunks), :] = ref[...]
    lane = lax.broadcasted_iota(jnp.int32, (block, LANES), 1)
    lane_all = lax.broadcasted_iota(jnp.int32, (total, LANES), 1)
    dk_ref[...] = jnp.zeros_like(dk_ref)
    dv_ref[...] = jnp.zeros_like(dv_ref)
    row8 = lax.broadcasted_iota(jnp.int32, (8, LANES), 0)
    lane8 = lax.broadcasted_iota(jnp.int32, (8, LANES), 1)
    head_rows = jnp.where(row8 == lane8 // HEAD_DIM, 1.0, 0.0)

    for start in range(0, total, block):
        width = start + block
        allowed = allowed_keys(segc_ref, segr_ref, start, block)
        queries = q_ref[start:width, :] * 0.125
        grads = datt_ref[start:width, :]
        product = grads.astype(f32) * att_ref[start:width, :].astype(f32)
        delta = lax.dot_general(
            head_rows,
            product,
            (((1,), (1,)), ((), ())),
            precision=lax.Precision.HIGHEST,
            preferred_element_type=f32,
        )
        dq = jnp.zeros((block, LANES), f32)
        for head in range(2):
            own = (lane >= HEAD_DIM) if head else (lane < HEAD_DIM)
            own_all = (lane_all >= HEAD_DIM) if head else (lane_all < HEAD_DIM)
            q_head = jnp.where(own, queries, 0.0).astype(bf16)
            g_head = jnp.where(own, grads, 0.0).astype(bf16)
            k_head = jnp.where(own_all[0:width], k_ref[0:width, :], 0.0).astype(bf16)
            scores = nt(k_ref[0:width, :], q_head)
            probs = jnp.where(allowed, jnp.exp(scores - lse_ref[0, head : head + 1, start:width]), 0.0)
            dprobs = nt(v_ref[0:width, :], g_head)
            dscores = (probs * (dprobs - delta[head : head + 1, :])).astype(bf16)
            dv_ref[0:width, :] += nn(probs.astype(bf16), g_head)
            dk_ref[0:width, :] += nn(dscores, q_head)
            dq = dq + tn(dscores, k_head)
        out_ref[start:width, aligned(pair, LANES)] = (dq * 0.125).astype(bf16)
    dk = dk_ref[...].astype(bf16)
    dv = dv_ref[...].astype(bf16)
    out_ref[:, aligned(pairs + pair, LANES)] = dk
    out_ref[:, aligned(2 * pairs + pair, LANES)] = dv
    grads = jnp.concatenate([out_ref[:, aligned(pair, LANES)], dk, dv], axis=1)
    weights = jnp.concatenate([wq_ref[...], wk_ref[...], wv_ref[...]], axis=1)
    pulled = nt(grads, weights)

    @pl.when(pair == 0)
    def _():
        sum_ref[...] = pulled

    @pl.when(pair > 0)
    def _():
        sum_ref[...] += pulled

    @pl.when(pair == pairs - 1)
    def _():
        rows = own_ref.shape[0]
        core = at_ref[CORE]
        own_ref[...] = sum_ref[aligned(core, rows), :]
        other_ref[...] = sum_ref[aligned(1 - core, rows), :].astype(bf16)


def attend_back(at, qkv, att, lse, seg_col, seg_row, came, wq):
    total, width = qkv.shape
    model = wq.shape[0]
    pairs = width // 3 // LANES
    chunks = len(came)
    return kernel_call(
        functools.partial(attend_back_kernel, block=min(256, total), chunks=chunks),
        pairs,
        at,
        [qkv, qkv, qkv, att, lse, seg_col, seg_row, *came, wq, wq, wq],
        head_specs(total, pairs)
        + [
            pl.BlockSpec((total, LANES), lambda h, at: (0, h)),
            pl.BlockSpec((1, 8, total), lambda h, at: (h, 0, 0)),
            None,
            None,
        ]
        + [pl.BlockSpec((total // chunks, LANES), lambda h, at: (0, h))] * chunks
        + head_specs(model, pairs),
        [None, None, None],
        [
            shape(bf16, total, width),
            shape(f32, total // 2, model),
            shape(bf16, total // 2, model),
        ],
        10 * total * total * width // 6,
        "attend_back",
        [
            pltpu.VMEM((total, LANES), f32),
            pltpu.VMEM((total, LANES), f32),
            pltpu.VMEM((total, LANES), bf16),
            pltpu.VMEM((total, model), f32),
        ],
    )


def mix_kernel(at_ref, q0, q1, q2, q3, x_ref, wo_ref, gain_ref, bias_ref, slot_ref, att_ref, mid_ref, *packs):
    rows, half = q0.shape
    for i, quad in enumerate((q0, q1, q2, q3)):
        place = at_ref[SEQ] ^ i
        att_ref[aligned(place & 1, rows), aligned(place >> 1, half, LANES)] = quad[...]
    middle = x_ref[...].astype(f32) + nn(att_ref[...], wo_ref[...])
    mid_ref[...] = middle
    hat, _ = norm_parts(middle)
    sent = (hat * gain_ref[...] + bias_ref[...]).astype(bf16)
    slots = packs[0].shape[1]
    for m, pack in enumerate(packs):
        place = lax.broadcasted_iota(jnp.int32, (2 * slots, sent.shape[0]), 0) + 2 * m * slots
        spread = jnp.where(place == slot_ref[...], 1.0, 0.0).astype(bf16)
        rows_out = nn(spread, sent).astype(bf16)
        pack[0] = rows_out[:slots]
        pack[1] = rows_out[slots:]


def mid_back_kernel(at_ref, *refs, owners):
    backs = refs[:owners]
    mid_ref, dy_ref, wo_ref, gain_ref, slot_ref = refs[owners : owners + 5]
    gm_ref, branch_ref, sums_ref, q0, q1, q2, q3, all_ref, datt_ref = refs[owners + 5 :]
    slots = backs[0].shape[1]
    for b, back in enumerate(backs):
        all_ref[b * slots : (b + 1) * slots, :] = back[0]
    count = mid_ref.shape[0]
    place = lax.broadcasted_iota(jnp.int32, (count, owners * slots), 1)
    spread = jnp.where(place == slot_ref[...], 1.0, 0.0).astype(bf16)
    grad = nn(spread, all_ref[...])
    hat, rstd = norm_parts(mid_ref[...])
    sums_ref[0:1, :] = jnp.sum(grad * hat, axis=0, keepdims=True)
    sums_ref[1:2, :] = jnp.sum(grad, axis=0, keepdims=True)
    grad_middle = dy_ref[...].astype(f32) + norm_pull(grad * gain_ref[...], hat, rstd)
    gm_ref[...] = grad_middle
    branch = grad_middle.astype(bf16)
    branch_ref[...] = branch
    datt_ref[...] = nt(branch, wo_ref[...]).astype(bf16)
    rows, half = q0.shape
    for i, quad in enumerate((q0, q1, q2, q3)):
        at = at_ref[SEQ] ^ i
        quad[...] = datt_ref[aligned(at & 1, rows), aligned(at >> 1, half, LANES)]


def hidden_kernel(at_ref, *refs, blocks, chunk):
    rows, grads = refs[:blocks], refs[blocks : 2 * blocks]
    in_ref, out_ref, act_ref, dpre_ref, x_ref, d_ref = refs[2 * blocks :]
    slots = rows[0].shape[1]

    @pl.when(pl.program_id(0) == 0)
    def _():
        for b in range(blocks):
            x_ref[b * slots : (b + 1) * slots, :] = rows[b][0]
            d_ref[b * slots : (b + 1) * slots, :] = grads[b][0]

    for start in range(0, x_ref.shape[0], chunk):
        part = slice(start, start + chunk)
        pre = nn(x_ref[part, :], in_ref[...])
        dact = nt(d_ref[part, :], out_ref[...])
        square = pre * pre
        gate = 0.5 * jnp.tanh(pre * (GELU_ONE + GELU_TWO * square)) + 0.5
        act = pre * gate
        slope = gate + act * (1.0 - gate) * (2 * GELU_ONE + 6 * GELU_TWO * square)
        act_ref[part, :] = act.astype(bf16)
        dpre_ref[part, :] = (dact * slope).astype(bf16)


def pair_specs(blocks, slots, width):
    return [
        pl.BlockSpec((1, slots, width), lambda i, at, b=b: (b % 2, 0, 0)) for b in range(blocks)
    ]


def hidden_group(at, rows, grads, base, w_in, w_out):
    blocks = len(rows)
    _, slots, width = rows[0].shape
    count = blocks * slots
    hidden = w_in.shape[1]
    tile = 768 if hidden % 768 == 0 else hidden
    chunk = 256 if count % 256 == 0 else count
    column = pl.BlockSpec((count, tile), lambda i, at: (0, i))
    return kernel_call(
        functools.partial(hidden_kernel, blocks=blocks, chunk=chunk),
        hidden // tile,
        at,
        [*rows, *([grads] * blocks), w_in, w_out],
        pair_specs(blocks, slots, width)
        + [
            pl.BlockSpec((1, slots, width), lambda i, at, b=b: ((base + b) ^ at[EXP], 0, 0))
            for b in range(blocks)
        ]
        + [
            pl.BlockSpec((width, tile), lambda i, at: (0, i)),
            pl.BlockSpec((tile, width), lambda i, at: (i, 0)),
        ],
        [column, column, None, None],
        [shape(bf16, count, hidden)] * 2 + [shape(bf16, count, width)] * 2,
        4 * count * width * hidden * 2,
        "hidden_group",
    )


def back_kernel(at_ref, a_ref, w_ref, *outs):
    out = nt(a_ref[...], w_ref[...]).astype(bf16)
    slots = outs[0].shape[1]
    each = a_ref.shape[0] // slots
    for step in range(2 * len(outs) // each):

        @pl.when(pl.program_id(0) == step)
        def _(step=step):
            for j in range(each):
                block = step * each + j
                outs[block // 2][block % 2] = out[j * slots : (j + 1) * slots, :]


def back_group(at, dpre, w_in, blocks):
    count, hidden = dpre.shape
    width = w_in.shape[0]
    return kernel_call(
        back_kernel,
        2,
        at,
        [dpre, w_in],
        [pl.BlockSpec((count // 2, hidden), lambda i, at: (i, 0)), None],
        [None] * (blocks // 2),
        [shape(bf16, 2, count // blocks, width)] * (blocks // 2),
        2 * count * width * hidden,
        "back_group",
    )


def out_kernel(at_ref, a0_ref, a1_ref, w_ref, o_ref):
    slots = o_ref.shape[1]
    low = at_ref[EXP] & 1

    def fill(ref):
        out = nn(ref[...], w_ref[...]).astype(bf16)
        for u in range(2):
            o_ref[low ^ u] = out[u * slots : (u + 1) * slots, :]

    first = pl.program_id(0) < pl.num_programs(0) // 2
    pl.when(first)(lambda: fill(a0_ref))
    pl.when(jnp.logical_not(first))(lambda: fill(a1_ref))


def out_rows(at, acts, w_out, owners):
    count, hidden = acts[0].shape
    width = w_out.shape[1]
    slots = 2 * count // owners
    steps = owners // 2
    return kernel_call(
        out_kernel,
        steps,
        at,
        [*acts, w_out],
        [
            pl.BlockSpec((2 * slots, hidden), lambda i, at: (jnp.minimum(i, steps // 2 - 1), 0)),
            pl.BlockSpec((2 * slots, hidden), lambda i, at: (jnp.maximum(i - steps // 2, 0), 0)),
            None,
        ],
        [pl.BlockSpec((2, slots, width), lambda i, at: (i ^ (at[EXP] >> 1), 0, 0))],
        [shape(bf16, owners, slots, width)],
        4 * count * width * hidden,
        "out_rows",
    )[0]


def grad_weight_kernel(at_ref, a0_ref, a1_ref, b0_ref, b1_ref, o_ref):
    o_ref[...] = (tn(a0_ref[...], b0_ref[...]) + tn(a1_ref[...], b1_ref[...])).astype(bf16)


def grad_out_weight(at, acts, grads):
    count, hidden = acts[0].shape
    width = grads[0].shape[1]
    tile = 768 if hidden % 768 == 0 else hidden
    column = pl.BlockSpec((count, tile), lambda i, at: (0, i))
    return kernel_call(
        grad_weight_kernel,
        hidden // tile,
        at,
        [*acts, *grads],
        [column, column, None, None],
        [pl.BlockSpec((tile, width), lambda i, at: (i, 0))],
        [shape(bf16, hidden, width)],
        4 * count * width * hidden,
        "grad_out_weight",
    )[0]


def grad_in_weight(at, rows, dpres):
    count, hidden = dpres[0].shape
    width = rows[0].shape[1]
    tile = 768 if hidden % 768 == 0 else hidden
    column = pl.BlockSpec((count, tile), lambda i, at: (0, i))
    return kernel_call(
        grad_weight_kernel,
        hidden // tile,
        at,
        [*rows, *dpres],
        [None, None, column, column],
        [pl.BlockSpec((width, tile), lambda i, at: (0, i))],
        [shape(bf16, width, hidden)],
        4 * count * width * hidden,
        "grad_in_weight",
    )[0]


def norm_sum_kernel(at_ref, own_ref, came_ref, x_ref, back_a_ref, back_b_ref, sums_ref):
    rows = back_a_ref.shape[0]
    low = at_ref[LOW]
    gain, bias = 0.0, 0.0
    for out_ref, place in ((back_a_ref, low), (back_b_ref, 1 - low)):
        part = aligned(place, rows)
        grad = own_ref[part, :] + came_ref[part, :].astype(f32)
        hat, _ = norm_parts(x_ref[part, :].astype(f32))
        gain = gain + jnp.sum(grad * hat, axis=0, keepdims=True)
        bias = bias + jnp.sum(grad, axis=0, keepdims=True)
        out_ref[...] = grad.astype(bf16)
    sums_ref[0:1, :] = gain
    sums_ref[1:2, :] = bias


def tokens_kernel(at_ref, a_ref, b_ref, x_ref, gm_ref, gain_ref, out_ref):
    rows = a_ref.shape[0]
    low = at_ref[LOW]
    for ref, place in ((a_ref, low), (b_ref, 1 - low)):
        part = aligned(place, rows)
        hat, rstd = norm_parts(x_ref[part, :].astype(f32))
        grad = ref[...].astype(f32) * gain_ref[...]
        out_ref[part, :] = gm_ref[part, :] + norm_pull(grad, hat, rstd)


def grad_shared_kernel(at_ref, normed_ref, dqkv_ref, gwo_ref, small_ref, *refs, orders):
    outs, all_ref = refs[:4], refs[4]
    blocks, part_rows, wide = all_ref.shape
    columns = dqkv_ref.shape[1]
    half = gwo_ref.shape[1]
    each = 128
    for start in range(0, columns, each * 3):
        stop = start + each * 3
        part = tn(normed_ref[...], dqkv_ref[:, start:stop])
        all_ref[:, :, start:stop] = part.reshape(blocks, part_rows, stop - start)
    all_ref[:, :, columns : columns + half] = gwo_ref[...].reshape(blocks, part_rows, half)
    all_ref[:, :, columns + half :] = small_ref[...].reshape(blocks, part_rows, wide - columns - half)
    for kk in range(2):
        for side in range(2):
            ref = outs[2 * kk + side]
            for j in range(ref.shape[0]):
                m = orders[kk][side * ref.shape[0] + j]
                for i in range(ref.shape[1]):
                    place = at_ref[FLAT] ^ ((2 * m + kk) * ref.shape[1] + i)
                    ref[j, i] = all_ref[place].astype(ref.dtype)


def final_shared_kernel(at_ref, *refs, half):
    parts, (qkv_ref, out_ref, norm_ref) = refs[:-3], refs[-3:]
    total = parts[0][...].astype(f32)
    for part in parts[1:]:
        total = total + part[...].astype(f32)
    norm_ref[...] = total[0][:, 4 * half :] + total[1][:, 4 * half :]

    def fill(core):
        for mine in range(2):
            which = core ^ mine
            for group in range(3):
                start = (2 * group + which) * half
                qkv_ref[:, start : start + half] = total[mine][:, group * half : (group + 1) * half]
            out_ref[:, which * half : (which + 1) * half] = total[mine][:, 3 * half : 4 * half]

    pl.when(at_ref[CORE] == 0)(lambda: fill(0))
    pl.when(at_ref[CORE] == 1)(lambda: fill(1))


def make_local(exp_size, seq_size):
    cols = exp_size // 2
    col_bits = cols.bit_length() - 1

    def flat_perm(target):
        pairs = []
        for exp in range(exp_size):
            for seq in range(seq_size):
                col, core = exp >> 1, exp & 1
                new_col, new_core, new_seq = target(col, core, seq)
                pairs.append((exp * seq_size + seq, (new_col * 2 + new_core) * seq_size + new_seq))
        return pairs

    def send(array, target):
        return lax.ppermute(array, BOTH, flat_perm(target))

    def to_core(array):
        return send(array, lambda c, k, z: (c, 1 - k, z))

    def to_seq(array, shift):
        return send(array, lambda c, k, z: (c, k, z ^ shift))

    def to_col(array, bit):
        return send(array, lambda c, k, z: (c ^ (1 << bit), k, z))

    def exchange(pairs):
        sent = lambda m, pair: send(pair, lambda c, k, z: (c ^ m, k, z))
        near = [m for m in range(1, cols) if m & (m - 1) == 0]
        came = {0: pairs[0], **{m: sent(m, pairs[m]) for m in near}}
        far = [m for m in range(1, cols) if m not in near]
        waits = [came[m] for m in near]
        came.update({m: sent(m, after(pairs[m], waits)) for m in far})
        return [came[m] for m in range(cols)]

    def with_other(pairs):
        return [part for pair in pairs for part in (pair, to_core(pair))]

    def home_of(i):
        return lambda c, k, z: (c, z >> 1, (2 * k + (z & 1)) ^ i)

    def worker_of(i):
        return lambda c, k, z: (c, (z ^ i) >> 1, 2 * k + ((z ^ i) & 1))

    def step_bits(kk):
        return list(range(col_bits))[:: 1 - 2 * kk]

    def local(
        tokens,
        cotangent,
        token_ids,
        segments,
        hash_table,
        w_qkv,
        w_attn_out,
        norm_scale,
        norm_shift,
        w_in,
        w_out,
    ):
        seq_dev, rows_seq, width = tokens.shape
        rows = seq_dev * rows_seq
        slot_rows = 3 * rows // exp_size
        full_len = rows_seq * seq_size
        half = width // 2
        wide = 4 * half + LANES
        part_rows = w_qkv.shape[0]
        blocks = seq_size * 2 * cols
        w_in, w_out = w_in[0], w_out[0]
        exp_at = lax.axis_index("exp")
        z = lax.axis_index("seq")
        k = exp_at & 1
        is_one = k == 1
        z0 = z & 1
        at = jnp.stack([k, exp_at * seq_size + z, z0, z, exp_at, 2 * k + z0]).astype(jnp.int32)

        norms = jnp.concatenate([norm_scale, norm_shift], axis=1)
        norms = jnp.pad(norms, ((0, 0), (0, LANES - norms.shape[1])))
        pack = jnp.concatenate([w_qkv, w_attn_out, norms], axis=1)
        got = [pack] + [to_seq(pack, i) for i in range(1, seq_size)]
        seg_pair = jnp.where((z >> 1) == k, segments, to_core(segments))
        seg_row = jnp.where(z0 == 1, seg_pair[1:2], seg_pair[0:1])
        seg_col = seg_row.reshape(full_len, 1)

        expert = hash_table[token_ids.reshape(-1)]
        order = jnp.arange(rows, dtype=jnp.int32)
        earlier = (expert[None, :] == expert[:, None]) & (order[None, :] < order[:, None])
        slot_rank = jnp.sum(earlier.astype(jnp.int32), axis=1)
        slots = exp_size * slot_rows
        slot_index = expert * slot_rows + slot_rank
        slot_near = (expert ^ exp_at) * slot_rows + slot_rank
        spread = (jnp.arange(slots, dtype=jnp.int32)[:, None] == slot_index[None, :]).astype(bf16)

        def swap(array):
            return lax.all_to_all(
                array.reshape(exp_size, slot_rows, width),
                "exp",
                split_axis=0,
                concat_axis=0,
                tiled=True,
            )

        grad_low = cotangent.reshape(rows, width)
        grad_packed = nn(spread, grad_low).astype(bf16)
        got, _ = lax.optimization_barrier((got, (grad_packed, slot_near, seg_row, seg_col)))
        mine, other = single_call(
            functools.partial(split_kernel, half=half, parts=seq_size),
            at,
            got,
            [shape(bf16, seq_size, part_rows, wide)] * 2,
            "split_cores",
        )
        pair = [jnp.where(z0 == 1, tokens[1 - i], tokens[i]) for i in range(2)]
        here = [send(pair[0], home_of(0)), send(pair[1], home_of(1))]
        x_half = jnp.concatenate(
            [jnp.where(z0 == 1, here[1 - i], here[i]) for i in range(2)], axis=0
        )
        x_other = to_core(x_half)
        pieces = [[mine], [to_core(other)]]
        for step in range(col_bits):
            if step == 1:
                pieces, x_half = lax.optimization_barrier((pieces, x_half))
            pieces = [
                own + [to_col(piece, step_bits(kk)[step]) for piece in own]
                for kk, own in enumerate(pieces)
            ]
        ordered = []
        for kk in range(2):
            bits = step_bits(kk)
            by_place = {}
            for index, piece in enumerate(pieces[kk]):
                place = sum(1 << bits[step] for step in range(col_bits) if (index >> step) & 1)
                by_place[place] = piece
            ordered += [by_place[place] for place in range(cols)]
        wq, wo_own, norm_rows, normed, qkv = single_call(
            functools.partial(norm_qkv_kernel, half=half, parts=seq_size, cols=cols),
            at,
            [*ordered, x_half, x_other],
            [
                shape(bf16, blocks, part_rows, 3 * half),
                shape(bf16, blocks, part_rows, half),
                shape(f32, 8, width),
                shape(bf16, full_len, width),
                shape(bf16, full_len, 3 * half),
            ],
            "norm_qkv",
            flops=2 * full_len * width * 3 * half,
            scratch=[pltpu.VMEM((blocks, part_rows, LANES), f32)],
        )
        wq = wq.reshape(width, 3 * half)
        wo_own = wo_own.reshape(width, half)
        gain_one, gain_two, bias_two = norm_rows[0:1], norm_rows[1:2], norm_rows[3:4]
        grad_arrived = swap(after(grad_packed, qkv))
        att, lse, *chunks = attend(at, qkv, seg_col, seg_row, seq_size)
        wo_other = to_core(wo_own)
        wo = jnp.concatenate(
            [jnp.where(is_one, wo_other, wo_own), jnp.where(is_one, wo_own, wo_other)], axis=1
        )
        quads = [send(chunks[i], home_of(i)) for i in range(seq_size)]
        quads, grad_arrived = lax.optimization_barrier((quads, grad_arrived))
        x_home = tokens.reshape(rows, width)
        att_home, middle, *packs = single_call(
            mix_kernel,
            at,
            [*quads, x_home, wo, gain_two, bias_two, slot_near[None, :]],
            [shape(bf16, rows, width), shape(f32, rows, width)]
            + [shape(bf16, 2, slot_rows, width)] * cols,
            "mix",
            flops=2 * rows * width * (width + slots),
        )

        arrived = exchange(packs)
        group = exp_size // 2
        hidden = []
        for base in (0, group):
            pairs = arrived[base // 2 : (base + group) // 2]
            if base:
                pairs = after(pairs, hidden[0])
            hidden.append(
                hidden_group(at, with_other(pairs), grad_arrived, base, w_in, w_out)
            )
        acts, dpres, sents, grads = zip(*hidden)
        grad_outer = grad_out_weight(at, acts, grads)
        grad_w_out = lax.psum_scatter(grad_outer, "seq", scatter_dimension=0, tiled=True)
        dpres = after(dpres, grad_outer)
        grad_sents = [back_group(at, dpre, w_in, group) for dpre in dpres]
        grad_back = with_other(exchange(list(grad_sents[0]) + list(grad_sents[1])))
        grad_inner = grad_in_weight(at, sents, after(dpres, grad_sents))
        expert_out = out_rows(at, after(acts, grad_inner), w_out, exp_size)
        grad_back, expert_out = lax.optimization_barrier((grad_back, expert_out))
        returned = swap(expert_out)
        layer_out = (middle + tn(spread, returned.reshape(slots, width))).astype(bf16)

        outs = [
            *(shape(f32, rows, width), shape(bf16, rows, width), shape(f32, 8, width)),
            *[shape(bf16, rows_seq, half)] * seq_size,
        ]
        grad_middle, grad_branch, sums_two, *quads = kernel_call(
            functools.partial(mid_back_kernel, owners=exp_size),
            1,
            at,
            [*grad_back, middle, grad_low, wo, gain_two, slot_near[:, None]],
            pair_specs(exp_size, slot_rows, width) + [None] * 5,
            [None] * len(outs),
            outs,
            2 * rows * width * (width + slots),
            "mid_back",
            [pltpu.VMEM((slots, width), bf16), pltpu.VMEM((rows, width), bf16)],
        )

        came = [send(quads[i], worker_of(i)) for i in range(seq_size)]
        grad_w_in = lax.psum_scatter(
            after(grad_inner, came), "seq", scatter_dimension=1, tiled=True
        )
        dqkv, own, other = attend_back(at, qkv, att, lse, seg_col, seg_row, came, wq)
        back_a, back_b, sums_one = single_call(
            norm_sum_kernel,
            at,
            [own, to_core(after(other, returned)), x_half],
            [shape(bf16, rows_seq, width)] * 2 + [shape(f32, 8, width)],
            "norm_sum",
        )
        wide_w_out = grad_w_out.astype(f32)
        (grad_tokens,) = single_call(
            tokens_kernel,
            at,
            [
                *[send(part, home_of(i)) for i, part in enumerate((back_a, back_b))],
                after(x_home, wide_w_out),
                grad_middle,
                gain_one,
            ],
            [shape(f32, rows, width)],
            "tokens",
        )

        grad_wo = tn(att_home, grad_branch)
        wo_halves = [grad_wo[:, :half], grad_wo[:, half:]]
        grad_wo = jnp.where(is_one, wo_halves[1], wo_halves[0]) + to_core(
            jnp.where(is_one, wo_halves[0], wo_halves[1]).astype(bf16)
        ).astype(f32)
        small = jnp.stack([sums_one[0], sums_two[0], sums_one[1], sums_two[1]])
        small = jnp.pad(small, ((0, LANES - 4), (0, 0))).T
        orders = [
            sorted(range(cols), key=lambda m, kk=kk: [(m >> bit) & 1 for bit in step_bits(kk)])
            for kk in range(2)
        ]
        stay_go = single_call(
            functools.partial(grad_shared_kernel, orders=orders),
            at,
            [normed, dqkv, grad_wo, small],
            [shape(bf16, cols // 2, seq_size, part_rows, wide)] * 4,
            "grad_shared",
            flops=2 * full_len * width * 3 * half,
            scratch=[pltpu.VMEM((blocks, part_rows, wide), f32)],
        )
        sums = []
        for kk in range(2):
            stay, go = stay_go[2 * kk], stay_go[2 * kk + 1]
            for step in range(col_bits):
                came = to_col(go, step_bits(kk)[step])
                both = stay.astype(f32) + came.astype(f32)
                if step + 1 < col_bits:
                    count = both.shape[0] // 2
                    stay, go = both[:count], both[count:].astype(bf16)
            sums.append(both[0])
        lined = jnp.stack([sums[0].astype(bf16), to_core(sums[1].astype(bf16))], axis=1)
        parts = [lined[0]] + [to_seq(lined[i], i) for i in range(1, seq_size)]
        grad_w_qkv, grad_w_attn_out, grad_norms = single_call(
            functools.partial(final_shared_kernel, half=half),
            at,
            parts,
            [shape(f32, part_rows, columns) for columns in (6 * half, 2 * half, LANES)],
            "final_shared",
        )
        return (
            layer_out.reshape(seq_dev, rows_seq, width),
            grad_tokens.reshape(seq_dev, rows_seq, width),
            grad_w_qkv,
            grad_w_attn_out,
            grad_norms[:, 0:2],
            grad_norms[:, 2:4],
            grad_w_in.astype(f32)[None],
            wide_w_out[None],
        )

    return local


def solution(mesh):
    return jax.shard_map(
        make_local(mesh.shape["exp"], mesh.shape["seq"]),
        mesh=mesh,
        in_specs=(
            P("exp", "seq", None),
            P("exp", "seq", None),
            P("exp", "seq"),
            P("exp", None),
            P(),
            P(("exp", "seq"), None),
            P(("exp", "seq"), None),
            P(("exp", "seq"), None),
            P(("exp", "seq"), None),
            P("exp", None, None),
            P("exp", None, None),
        ),
        out_specs=(
            P("exp", "seq", None),
            P("exp", "seq", None),
            P(("exp", "seq"), None),
            P(("exp", "seq"), None),
            P(("exp", "seq"), None),
            P(("exp", "seq"), None),
            P("exp", None, "seq"),
            P("exp", "seq", None),
        ),
        check_vma=False,
    )
```

```python
import functools

import jax
import jax.numpy as jnp
from jax import lax
from jax.experimental import pallas as pl
from jax.experimental.pallas import tpu as pltpu
from jax.sharding import PartitionSpec as P

HEAD_DIM = 64
LANES = 128
BOTH = ("exp", "seq")
epsilon = 1e-05
f32 = jnp.float32
bf16 = jnp.bfloat16


def norm_parts(feature):
    center = feature - jnp.mean(feature, axis=-1, keepdims=True)
    spread = jnp.mean(center * center, axis=-1, keepdims=True)
    rstd = lax.rsqrt(spread + epsilon)
    return center * rstd, rstd


def norm_pull(grad_hat, hat, rstd):
    first = jnp.mean(grad_hat, axis=-1, keepdims=True)
    second = jnp.mean(grad_hat * hat, axis=-1, keepdims=True)
    return rstd * (grad_hat - first - hat * second)


def nt(a, b):
    return lax.dot_general(a, b, (((1,), (1,)), ((), ())), preferred_element_type=f32)


def nn(a, b):
    return lax.dot_general(a, b, (((1,), (0,)), ((), ())), preferred_element_type=f32)


def tn(a, b):
    return lax.dot_general(a, b, (((0,), (0,)), ((), ())), preferred_element_type=f32)


def after(value, *earlier):
    return lax.optimization_barrier((value, earlier))[0]


def aligned(index, size, unit=None):
    return pl.ds(pl.multiple_of(index * size, unit or size), size)


def whole_block(*shape):
    return pl.BlockSpec(shape, lambda i, at: (0,) * len(shape))


def kernel_call(body, steps, at, arrays, in_specs, out_specs, out_shape, flops, name, scratch=()):
    in_specs = [spec or whole_block(*a.shape) for spec, a in zip(in_specs, arrays)]
    out_specs = [spec or whole_block(*o.shape) for spec, o in zip(out_specs, out_shape)]
    moved = sum(a.size * a.dtype.itemsize for a in (*arrays, *out_shape))
    return pl.pallas_call(
        body,
        grid_spec=pltpu.PrefetchScalarGridSpec(
            num_scalar_prefetch=1,
            grid=(steps,),
            in_specs=in_specs,
            out_specs=out_specs,
            scratch_shapes=list(scratch),
        ),
        out_shape=list(out_shape),
        compiler_params=pltpu.CompilerParams(vmem_limit_bytes=56 << 20),
        cost_estimate=pl.CostEstimate(flops=flops, bytes_accessed=moved, transcendentals=0),
        name=name,
    )(at, *arrays)


def single_call(body, at, arrays, out_shape, name, flops=0, scratch=()):
    return kernel_call(
        body,
        1,
        at,
        arrays,
        [None] * len(arrays),
        [None] * len(out_shape),
        out_shape,
        flops,
        name,
        scratch,
    )


def shape(kind, *dims):
    return jax.ShapeDtypeStruct(dims, kind)


CORE, FLAT, LOW, SEQ, EXP, CHUNK = range(6)


def key_segments(segr_ref):
    rows = jnp.broadcast_to(segr_ref[...].astype(f32), (8, segr_ref.shape[1]))
    return rows.T[:, 0:1]


def allowed_keys(seg_keys, segr_ref, start, block):
    width = start + block
    keys = lax.broadcasted_iota(jnp.int32, (width, block), 0)
    queries = lax.broadcasted_iota(jnp.int32, (width, block), 1) + start
    same = seg_keys[0:width] == segr_ref[:, start : start + block].astype(f32)
    return same & (keys <= queries)


def split_kernel(at_ref, *refs, half, parts):
    got, (mine_ref, other_ref) = refs[:parts], refs[parts:]

    def fill(core):
        for i in range(parts):
            for ref, which in ((mine_ref, core), (other_ref, 1 - core)):
                for group in range(4):
                    start = (2 * group + which) * half
                    ref[i, :, group * half : (group + 1) * half] = got[i][:, start : start + half]
                ref[i, :, 4 * half :] = got[i][:, 8 * half :]

    pl.when(at_ref[CORE] == 0)(lambda: fill(0))
    pl.when(at_ref[CORE] == 1)(lambda: fill(1))


def norm_qkv_kernel(at_ref, *refs, half, parts, cols):
    pieces, (own_ref, other_ref) = refs[: 2 * cols], refs[2 * cols : 2 * cols + 2]
    wq_ref, wo_ref, rows_ref, hat_ref, normed_ref, qkv_ref, norm_ref = refs[2 * cols + 2 :]
    for kk in range(2):
        for m in range(cols):
            for i in range(parts):
                place = at_ref[FLAT] ^ ((2 * m + kk) * parts + i)
                block = pieces[kk * cols + m]
                wq_ref[place] = block[i, :, : 3 * half]
                wo_ref[place] = block[i, :, 3 * half : 4 * half]
                norm_ref[place] = block[i, :, 4 * half :].astype(f32)
    width = own_ref.shape[1]
    norm_rows = norm_ref[...].reshape(width, LANES).T[0:8]
    rows_ref[...] = norm_rows
    weights = wq_ref[...].reshape(width, 3 * half)
    rows = own_ref.shape[0]
    core = at_ref[CORE]
    for ref, place in ((own_ref, core), (other_ref, 1 - core)):
        hat, _ = norm_parts(ref[...].astype(f32))
        normed = (hat * norm_rows[0:1] + norm_rows[2:3]).astype(bf16)
        where = aligned(place, rows)
        hat_ref[where, :] = hat.astype(bf16)
        normed_ref[where, :] = normed
        qkv_ref[where, :] = nn(normed, weights).astype(bf16)


GELU_ONE = 0.7978845608028654
GELU_TWO = GELU_ONE * 0.044715


def attend_kernel(at_ref, q_ref, k_ref, v_ref, segr_ref, att_ref, lse_ref, *outs_ref, block):
    total = q_ref.shape[0]
    seg_keys = key_segments(segr_ref)
    values_t = v_ref[...].astype(f32).T.astype(bf16)
    lane = lax.broadcasted_iota(jnp.int32, (block, LANES), 1)
    for start in range(0, total, block):
        width = start + block
        allowed = allowed_keys(seg_keys, segr_ref, start, block)
        queries = q_ref[start:width, :] * 0.125
        outs = []
        for head in range(2):
            own = (lane >= HEAD_DIM) if head else (lane < HEAD_DIM)
            q_head = jnp.where(own, queries, 0.0).astype(bf16)
            scores = jnp.where(allowed, nt(k_ref[0:width, :], q_head), -1e30)
            top = jnp.max(scores, axis=0, keepdims=True)
            expo = jnp.exp(scores - top)
            total_row = jnp.sum(expo, axis=0, keepdims=True)
            out = nn(values_t[head * HEAD_DIM : (head + 1) * HEAD_DIM, 0:width], expo.astype(bf16))
            outs.append(out / total_row)
            lse_ref[0, head : head + 1, start:width] = top + jnp.log(total_row)
        att_ref[start:width, :] = jnp.concatenate(outs, axis=0).T.astype(bf16)
    rows = outs_ref[0].shape[0]
    for i, ref in enumerate(outs_ref):
        ref[...] = att_ref[aligned(at_ref[CHUNK] ^ i, rows), :]


def head_specs(total, pairs):
    return [
        pl.BlockSpec((total, LANES), lambda h, at, part=part: (0, part * pairs + h))
        for part in range(3)
    ]


def attend(at, qkv, seg_row, chunks):
    total, width = qkv.shape
    pairs = width // 3 // LANES
    rows = total // chunks
    piece = pl.BlockSpec((rows, LANES), lambda h, at: (0, h))
    return kernel_call(
        functools.partial(attend_kernel, block=min(256, total)),
        pairs,
        at,
        [qkv, qkv, qkv, seg_row],
        head_specs(total, pairs) + [None],
        [
            pl.BlockSpec((total, LANES), lambda h, at: (0, h)),
            pl.BlockSpec((1, 8, total), lambda h, at: (h, 0, 0)),
        ]
        + [piece] * chunks,
        [shape(bf16, total, pairs * LANES), shape(f32, pairs, 8, total)]
        + [shape(bf16, rows, pairs * LANES)] * chunks,
        4 * total * total * width // 6,
        "attend",
    )


def attend_back_kernel(
    at_ref, q_ref, k_ref, v_ref, att_ref, lse_ref, segr_ref, hat_ref, *refs, block, chunks
):
    came, (wq_ref, wk_ref, wv_ref) = refs[:chunks], refs[chunks : chunks + 3]
    out_ref, own_ref, other_ref, sums_ref, dk_ref, dv_ref, datt_ref, sum_ref = refs[chunks + 3 :]
    total = q_ref.shape[0]
    pairs = pl.num_programs(0)
    pair = pl.program_id(0)
    for i, ref in enumerate(came):
        datt_ref[aligned(at_ref[CHUNK] ^ i, total // chunks), :] = ref[...]
    lane = lax.broadcasted_iota(jnp.int32, (block, LANES), 1)
    lane_all = lax.broadcasted_iota(jnp.int32, (total, LANES), 1)
    dk_ref[...] = jnp.zeros_like(dk_ref)
    dv_ref[...] = jnp.zeros_like(dv_ref)
    seg_keys = key_segments(segr_ref)
    row8 = lax.broadcasted_iota(jnp.int32, (8, LANES), 0)
    lane8 = lax.broadcasted_iota(jnp.int32, (8, LANES), 1)
    head_rows = jnp.where(row8 == lane8 // HEAD_DIM, 1.0, 0.0)

    for start in range(0, total, block):
        width = start + block
        allowed = allowed_keys(seg_keys, segr_ref, start, block)
        queries = q_ref[start:width, :] * 0.125
        grads = datt_ref[start:width, :]
        product = grads.astype(f32) * att_ref[start:width, :].astype(f32)
        delta = lax.dot_general(
            head_rows,
            product,
            (((1,), (1,)), ((), ())),
            precision=lax.Precision.HIGHEST,
            preferred_element_type=f32,
        )
        dq = jnp.zeros((block, LANES), f32)
        for head in range(2):
            own = (lane >= HEAD_DIM) if head else (lane < HEAD_DIM)
            own_all = (lane_all >= HEAD_DIM) if head else (lane_all < HEAD_DIM)
            q_head = jnp.where(own, queries, 0.0).astype(bf16)
            g_head = jnp.where(own, grads, 0.0).astype(bf16)
            k_head = jnp.where(own_all[0:width], k_ref[0:width, :], 0.0).astype(bf16)
            scores = nt(k_ref[0:width, :], q_head)
            probs = jnp.where(allowed, jnp.exp(scores - lse_ref[0, head : head + 1, start:width]), 0.0)
            dprobs = nt(v_ref[0:width, :], g_head)
            dscores = (probs * (dprobs - delta[head : head + 1, :])).astype(bf16)
            dv_ref[0:width, :] += nn(probs.astype(bf16), g_head)
            dk_ref[0:width, :] += nn(dscores, q_head)
            dq = dq + tn(dscores, k_head)
        out_ref[start:width, aligned(pair, LANES)] = (dq * 0.125).astype(bf16)
    dk = dk_ref[...].astype(bf16)
    dv = dv_ref[...].astype(bf16)
    out_ref[:, aligned(pairs + pair, LANES)] = dk
    out_ref[:, aligned(2 * pairs + pair, LANES)] = dv
    grads = jnp.concatenate([out_ref[:, aligned(pair, LANES)], dk, dv], axis=1)
    weights = jnp.concatenate([wq_ref[...], wk_ref[...], wv_ref[...]], axis=1)
    pulled = nt(grads, weights)

    @pl.when(pair == 0)
    def _():
        sum_ref[...] = pulled

    @pl.when(pair > 0)
    def _():
        sum_ref[...] += pulled

    @pl.when(pair == pairs - 1)
    def _():
        rows = own_ref.shape[0]
        core = at_ref[CORE]
        own_ref[...] = sum_ref[aligned(core, rows), :]
        other_ref[...] = sum_ref[aligned(1 - core, rows), :].astype(bf16)
        sums_ref[0:1, :] = jnp.sum(sum_ref[...] * hat_ref[...].astype(f32), axis=0, keepdims=True)
        sums_ref[1:2, :] = jnp.sum(sum_ref[...], axis=0, keepdims=True)


def attend_back(at, qkv, att, lse, seg_row, hat, came, wq):
    total, width = qkv.shape
    model = wq.shape[0]
    pairs = width // 3 // LANES
    chunks = len(came)
    return kernel_call(
        functools.partial(attend_back_kernel, block=min(256, total), chunks=chunks),
        pairs,
        at,
        [qkv, qkv, qkv, att, lse, seg_row, hat, *came, wq, wq, wq],
        head_specs(total, pairs)
        + [
            pl.BlockSpec((total, LANES), lambda h, at: (0, h)),
            pl.BlockSpec((1, 8, total), lambda h, at: (h, 0, 0)),
            None,
            None,
        ]
        + [pl.BlockSpec((total // chunks, LANES), lambda h, at: (0, h))] * chunks
        + head_specs(model, pairs),
        [None] * 4,
        [
            shape(bf16, total, width),
            shape(f32, total // 2, model),
            shape(bf16, total // 2, model),
            shape(f32, 8, model),
        ],
        10 * total * total * width // 6,
        "attend_back",
        [
            pltpu.VMEM((total, LANES), f32),
            pltpu.VMEM((total, LANES), f32),
            pltpu.VMEM((total, LANES), bf16),
            pltpu.VMEM((total, model), f32),
        ],
    )


def mix_kernel(at_ref, q0, q1, q2, q3, x_ref, wo_ref, gain_ref, bias_ref, slot_ref, att_ref, mid_ref, *packs):
    rows, half = q0.shape
    for i, quad in enumerate((q0, q1, q2, q3)):
        place = at_ref[SEQ] ^ i
        att_ref[aligned(place & 1, rows), aligned(place >> 1, half, LANES)] = quad[...]
    middle = x_ref[...].astype(f32) + nn(att_ref[...], wo_ref[...])
    mid_ref[...] = middle
    hat, _ = norm_parts(middle)
    sent = (hat * gain_ref[...] + bias_ref[...]).astype(bf16)
    slots = packs[0].shape[1]
    for m, pack in enumerate(packs):
        place = lax.broadcasted_iota(jnp.int32, (2 * slots, sent.shape[0]), 0) + 2 * m * slots
        spread = jnp.where(place == slot_ref[...], 1.0, 0.0).astype(bf16)
        rows_out = nn(spread, sent).astype(bf16)
        pack[0] = rows_out[:slots]
        pack[1] = rows_out[slots:]


def mid_back_kernel(at_ref, *refs, owners):
    backs = refs[:owners]
    mid_ref, dy_ref, wo_ref, gain_ref, slot_ref = refs[owners : owners + 5]
    gm_ref, branch_ref, sums_ref, q0, q1, q2, q3, all_ref, datt_ref = refs[owners + 5 :]
    slots = backs[0].shape[1]
    for b, back in enumerate(backs):
        all_ref[b * slots : (b + 1) * slots, :] = back[0]
    count = mid_ref.shape[0]
    place = lax.broadcasted_iota(jnp.int32, (count, owners * slots), 1)
    spread = jnp.where(place == slot_ref[...], 1.0, 0.0).astype(bf16)
    grad = nn(spread, all_ref[...])
    hat, rstd = norm_parts(mid_ref[...])
    sums_ref[0:1, :] = jnp.sum(grad * hat, axis=0, keepdims=True)
    sums_ref[1:2, :] = jnp.sum(grad, axis=0, keepdims=True)
    grad_middle = dy_ref[...].astype(f32) + norm_pull(grad * gain_ref[...], hat, rstd)
    gm_ref[...] = grad_middle
    branch = grad_middle.astype(bf16)
    branch_ref[...] = branch
    datt_ref[...] = nt(branch, wo_ref[...]).astype(bf16)
    rows, half = q0.shape
    for i, quad in enumerate((q0, q1, q2, q3)):
        at = at_ref[SEQ] ^ i
        quad[...] = datt_ref[aligned(at & 1, rows), aligned(at >> 1, half, LANES)]


def layer_out_kernel(at_ref, *refs, owners):
    backs, (mid_ref, slot_ref, out_ref, all_ref) = refs[:owners], refs[owners:]
    slots = backs[0].shape[1]
    for b, back in enumerate(backs):
        all_ref[b * slots : (b + 1) * slots, :] = back[0]
    place = lax.broadcasted_iota(jnp.int32, (mid_ref.shape[0], owners * slots), 1)
    spread = jnp.where(place == slot_ref[...], 1.0, 0.0).astype(bf16)
    out_ref[...] = (mid_ref[...] + nn(spread, all_ref[...])).astype(bf16)


def hidden_kernel(at_ref, *refs, blocks, chunk):
    rows, grads = refs[:blocks], refs[blocks : 2 * blocks]
    in_ref, out_ref, act_ref, dpre_ref, x_ref, d_ref = refs[2 * blocks :]
    slots = rows[0].shape[1]

    @pl.when(pl.program_id(0) == 0)
    def _():
        for b in range(blocks):
            x_ref[b * slots : (b + 1) * slots, :] = rows[b][0]
            d_ref[b * slots : (b + 1) * slots, :] = grads[b][0]

    for start in range(0, x_ref.shape[0], chunk):
        part = slice(start, start + chunk)
        pre = nn(x_ref[part, :], in_ref[...])
        dact = nt(d_ref[part, :], out_ref[...])
        square = pre * pre
        gate = 0.5 * jnp.tanh(pre * (GELU_ONE + GELU_TWO * square)) + 0.5
        act = pre * gate
        slope = gate + act * (1.0 - gate) * (2 * GELU_ONE + 6 * GELU_TWO * square)
        act_ref[part, :] = act.astype(bf16)
        dpre_ref[part, :] = (dact * slope).astype(bf16)


def pair_specs(blocks, slots, width):
    return [
        pl.BlockSpec((1, slots, width), lambda i, at, b=b: (b % 2, 0, 0)) for b in range(blocks)
    ]


def hidden_group(at, rows, grads, members, w_in, w_out):
    blocks = len(rows)
    _, slots, width = rows[0].shape
    count = blocks * slots
    hidden = w_in.shape[1]
    tile = 768 if hidden % 768 == 0 else hidden
    chunk = next((size for size in (256, 384) if count % size == 0), count)
    column = pl.BlockSpec((count, tile), lambda i, at: (0, i))
    places = [2 * m + kk for m in members for kk in range(2)]
    return kernel_call(
        functools.partial(hidden_kernel, blocks=blocks, chunk=chunk),
        hidden // tile,
        at,
        [*rows, *([grads] * blocks), w_in, w_out],
        pair_specs(blocks, slots, width)
        + [pl.BlockSpec((1, slots, width), lambda i, at, b=b: (b ^ at[EXP], 0, 0)) for b in places]
        + [
            pl.BlockSpec((width, tile), lambda i, at: (0, i)),
            pl.BlockSpec((tile, width), lambda i, at: (i, 0)),
        ],
        [column, column, None, None],
        [shape(bf16, count, hidden)] * 2 + [shape(bf16, count, width)] * 2,
        4 * count * width * hidden,
        "hidden_group",
    )


def back_kernel(at_ref, a_ref, w_ref, *outs):
    out = nt(a_ref[...], w_ref[...]).astype(bf16)
    slots = outs[0].shape[1]
    for step, ref in enumerate(outs):

        @pl.when(pl.program_id(0) == step)
        def _(ref=ref):
            ref[0] = out[:slots]
            ref[1] = out[slots:]


def back_group(at, dpre, w_in, members):
    count, hidden = dpre.shape
    width = w_in.shape[0]
    pair = count // len(members)
    return kernel_call(
        back_kernel,
        len(members),
        at,
        [dpre, w_in],
        [pl.BlockSpec((pair, hidden), lambda i, at: (i, 0)), None],
        [None] * len(members),
        [shape(bf16, 2, pair // 2, width)] * len(members),
        2 * count * width * hidden,
        "back_group",
    )


def out_kernel(at_ref, *refs, starts, order):
    acts, w_ref, outs = refs[: len(starts) - 1], refs[len(starts) - 1], refs[len(starts) :]
    slots = outs[0].shape[1]
    step = pl.program_id(0)
    for group, act_ref in enumerate(acts):
        for i in range(starts[group], starts[group + 1]):

            @pl.when(step == i)
            def _(act_ref=act_ref, ref=outs[order[i]]):
                out = nn(act_ref[...], w_ref[...]).astype(bf16)
                ref[0] = out[:slots]
                ref[1] = out[slots:]


def out_rows(at, acts, w_out, groups):
    hidden, width = w_out.shape
    pair = acts[0].shape[0] // len(groups[0])
    starts = [sum(len(g) for g in groups[:i]) for i in range(len(groups) + 1)]
    return kernel_call(
        functools.partial(out_kernel, starts=starts, order=sum(groups, [])),
        starts[-1],
        at,
        [*acts, w_out],
        [
            pl.BlockSpec(
                (pair, hidden),
                lambda i, at, a=starts[g], b=starts[g + 1]: (jnp.clip(i, a, b - 1) - a, 0),
            )
            for g in range(len(groups))
        ]
        + [None],
        [None] * starts[-1],
        [shape(bf16, 2, pair // 2, width)] * starts[-1],
        2 * starts[-1] * pair * width * hidden,
        "out_rows",
    )


def grad_weight_kernel(at_ref, *refs):
    parts = (len(refs) - 1) // 2
    total = tn(refs[0][...], refs[parts][...])
    for i in range(1, parts):
        total = total + tn(refs[i][...], refs[parts + i][...])
    refs[-1][...] = total.astype(bf16)


def grad_out_weight(at, acts, grads):
    hidden, width = acts[0].shape[1], grads[0].shape[1]
    tile = 768 if hidden % 768 == 0 else hidden
    return kernel_call(
        grad_weight_kernel,
        hidden // tile,
        at,
        [*acts, *grads],
        [pl.BlockSpec((a.shape[0], tile), lambda i, at: (0, i)) for a in acts] + [None] * len(grads),
        [pl.BlockSpec((tile, width), lambda i, at: (i, 0))],
        [shape(bf16, hidden, width)],
        2 * sum(a.shape[0] for a in acts) * width * hidden,
        "grad_out_weight",
    )[0]


def grad_in_weight(at, rows, dpres):
    hidden, width = dpres[0].shape[1], rows[0].shape[1]
    tile = 768 if hidden % 768 == 0 else hidden
    return kernel_call(
        grad_weight_kernel,
        hidden // tile,
        at,
        [*rows, *dpres],
        [None] * len(rows) + [pl.BlockSpec((a.shape[0], tile), lambda i, at: (0, i)) for a in dpres],
        [pl.BlockSpec((width, tile), lambda i, at: (0, i))],
        [shape(bf16, width, hidden)],
        2 * sum(a.shape[0] for a in dpres) * width * hidden,
        "grad_in_weight",
    )[0]


def home_rows_kernel(at_ref, own_ref, came_ref, x_ref, gain_ref, back_a_ref, back_b_ref):
    rows = back_a_ref.shape[0]
    low = at_ref[LOW]
    for out_ref, place in ((back_a_ref, low), (back_b_ref, 1 - low)):
        part = aligned(place, rows)
        grad = own_ref[part, :] + came_ref[part, :].astype(f32)
        hat, rstd = norm_parts(x_ref[part, :].astype(f32))
        out_ref[...] = norm_pull(grad * gain_ref[...], hat, rstd).astype(bf16)


def tokens_kernel(at_ref, a_ref, b_ref, gm_ref, out_ref):
    rows = a_ref.shape[0]
    low = at_ref[LOW]
    for ref, place in ((a_ref, low), (b_ref, 1 - low)):
        part = aligned(place, rows)
        out_ref[part, :] = gm_ref[part, :] + ref[...].astype(f32)


def grad_shared_kernel(at_ref, normed_ref, dqkv_ref, gwo_ref, small_ref, *refs, orders):
    outs, all_ref = refs[:4], refs[4]
    blocks, part_rows, wide = all_ref.shape
    columns = dqkv_ref.shape[1]
    half = gwo_ref.shape[1]
    each = 128
    for start in range(0, columns, each * 3):
        stop = start + each * 3
        part = tn(normed_ref[...], dqkv_ref[:, start:stop])
        all_ref[:, :, start:stop] = part.reshape(blocks, part_rows, stop - start)
    all_ref[:, :, columns : columns + half] = gwo_ref[...].reshape(blocks, part_rows, half)
    all_ref[:, :, columns + half :] = small_ref[...].reshape(blocks, part_rows, wide - columns - half)
    for kk in range(2):
        for side in range(2):
            ref = outs[2 * kk + side]
            for j in range(ref.shape[0]):
                m = orders[kk][side * ref.shape[0] + j]
                for i in range(ref.shape[1]):
                    place = at_ref[FLAT] ^ ((2 * m + kk) * ref.shape[1] + i)
                    ref[j, i] = all_ref[place].astype(ref.dtype)


def final_shared_kernel(at_ref, *refs, half):
    parts, (qkv_ref, out_ref, scale_ref, shift_ref) = refs[:-4], refs[-4:]
    total = parts[0][...].astype(f32)
    for part in parts[1:]:
        total = total + part[...].astype(f32)
    norms = total[0][:, 4 * half :] + total[1][:, 4 * half :]
    row = lax.broadcasted_iota(jnp.int32, (8, norms.shape[1]), 0)
    lane = lax.broadcasted_iota(jnp.int32, (8, norms.shape[1]), 1)
    turned = lax.dot_general(
        jnp.where(row == lane, 1.0, 0.0),
        norms,
        (((1,), (1,)), ((), ())),
        precision=lax.Precision.HIGHEST,
        preferred_element_type=f32,
    )
    scale_ref[...] = turned[0:2]
    shift_ref[...] = turned[2:4]

    def fill(core):
        for mine in range(2):
            which = core ^ mine
            for group in range(3):
                start = (2 * group + which) * half
                qkv_ref[:, start : start + half] = total[mine][:, group * half : (group + 1) * half]
            out_ref[:, which * half : (which + 1) * half] = total[mine][:, 3 * half : 4 * half]

    pl.when(at_ref[CORE] == 0)(lambda: fill(0))
    pl.when(at_ref[CORE] == 1)(lambda: fill(1))


def make_local(exp_size, seq_size):
    cols = exp_size // 2
    col_bits = cols.bit_length() - 1
    near = [m for m in range(1, cols) if m & (m - 1) == 0]
    far = [m for m in range(1, cols) if m & (m - 1)]
    groups = [[0], near, far]

    def flat_perm(target):
        pairs = []
        for exp in range(exp_size):
            for seq in range(seq_size):
                col, core = exp >> 1, exp & 1
                new_col, new_core, new_seq = target(col, core, seq)
                pairs.append((exp * seq_size + seq, (new_col * 2 + new_core) * seq_size + new_seq))
        return pairs

    def send(array, target):
        return lax.ppermute(array, BOTH, flat_perm(target))

    def to_core(array):
        return send(array, lambda c, k, z: (c, 1 - k, z))

    def to_seq(array, shift):
        return send(array, lambda c, k, z: (c, k, z ^ shift))

    def to_col(array, bit):
        return send(array, lambda c, k, z: (c ^ (1 << bit), k, z))

    def exchange(pairs):
        came = exchange_near(pairs)
        return exchange_far(pairs, came)

    def chip_send(m, pair):
        return send(pair, lambda c, k, z: (c ^ m, k, z))

    def exchange_near(pairs):
        return {0: pairs[0], **{m: chip_send(m, pairs[m]) for m in near}}

    def exchange_far(pairs, came):
        waits = [came[m] for m in near]
        rest = {m: chip_send(m, after(pairs[m], waits)) for m in far}
        return [rest[m] if m in rest else came[m] for m in range(cols)]

    def with_other(pairs):
        return [part for pair in pairs for part in (pair, to_core(pair))]

    def home_of(i):
        return lambda c, k, z: (c, z >> 1, (2 * k + (z & 1)) ^ i)

    def worker_of(i):
        return lambda c, k, z: (c, (z ^ i) >> 1, 2 * k + ((z ^ i) & 1))

    def step_bits(kk):
        return list(range(col_bits))[:: 1 - 2 * kk]

    def local(
        tokens,
        cotangent,
        token_ids,
        segments,
        hash_table,
        w_qkv,
        w_attn_out,
        norm_scale,
        norm_shift,
        w_in,
        w_out,
    ):
        seq_dev, rows_seq, width = tokens.shape
        rows = seq_dev * rows_seq
        slot_rows = 3 * rows // exp_size
        full_len = rows_seq * seq_size
        half = width // 2
        wide = 4 * half + LANES
        part_rows = w_qkv.shape[0]
        blocks = seq_size * 2 * cols
        w_in, w_out = w_in[0], w_out[0]
        exp_at = lax.axis_index("exp")
        z = lax.axis_index("seq")
        k = exp_at & 1
        is_one = k == 1
        z0 = z & 1
        at = jnp.stack([k, exp_at * seq_size + z, z0, z, exp_at, 2 * k + z0]).astype(jnp.int32)

        norms = jnp.concatenate([norm_scale, norm_shift], axis=1)
        norms = jnp.pad(norms, ((0, 0), (0, LANES - norms.shape[1])))
        pack = jnp.concatenate([w_qkv, w_attn_out, norms], axis=1)
        got = [pack] + [to_seq(pack, i) for i in range(1, seq_size)]
        seg_pair = jnp.where((z >> 1) == k, segments, to_core(segments))
        seg_row = jnp.where(z0 == 1, seg_pair[1:2], seg_pair[0:1])

        expert = hash_table[token_ids.reshape(-1)]
        order = jnp.arange(rows, dtype=jnp.int32)
        earlier = (expert[None, :] == expert[:, None]) & (order[None, :] < order[:, None])
        slot_rank = jnp.sum(earlier.astype(jnp.int32), axis=1)
        slots = exp_size * slot_rows
        slot_index = expert * slot_rows + slot_rank
        slot_near = (expert ^ exp_at) * slot_rows + slot_rank
        spread = (jnp.arange(slots, dtype=jnp.int32)[:, None] == slot_index[None, :]).astype(bf16)

        def swap(array):
            return lax.all_to_all(
                array.reshape(exp_size, slot_rows, width),
                "exp",
                split_axis=0,
                concat_axis=0,
                tiled=True,
            )

        grad_low = cotangent.reshape(rows, width)
        grad_packed = nn(spread, grad_low).astype(bf16)
        got, _ = lax.optimization_barrier((got, (grad_packed, slot_near, seg_row)))
        mine, other = single_call(
            functools.partial(split_kernel, half=half, parts=seq_size),
            at,
            got,
            [shape(bf16, seq_size, part_rows, wide)] * 2,
            "split_cores",
        )
        pair = [jnp.where(z0 == 1, tokens[1 - i], tokens[i]) for i in range(2)]
        here = [send(pair[0], home_of(0)), send(pair[1], home_of(1))]
        x_half = jnp.concatenate(
            [jnp.where(z0 == 1, here[1 - i], here[i]) for i in range(2)], axis=0
        )
        pieces = [[mine], [to_core(other)]]
        x_other = None
        for step in range(col_bits):
            if step == 1:
                pieces, x_half = lax.optimization_barrier((pieces, x_half))
                x_other = to_core(x_half)
            pieces = [
                own + [to_col(piece, step_bits(kk)[step]) for piece in own]
                for kk, own in enumerate(pieces)
            ]
        ordered = []
        for kk in range(2):
            bits = step_bits(kk)
            by_place = {}
            for index, piece in enumerate(pieces[kk]):
                place = sum(1 << bits[step] for step in range(col_bits) if (index >> step) & 1)
                by_place[place] = piece
            ordered += [by_place[place] for place in range(cols)]
        wq, wo_own, norm_rows, hat, normed, qkv = single_call(
            functools.partial(norm_qkv_kernel, half=half, parts=seq_size, cols=cols),
            at,
            [*ordered, x_half, x_other],
            [
                shape(bf16, blocks, part_rows, 3 * half),
                shape(bf16, blocks, part_rows, half),
                shape(f32, 8, width),
                shape(bf16, full_len, width),
                shape(bf16, full_len, width),
                shape(bf16, full_len, 3 * half),
            ],
            "norm_qkv",
            flops=2 * full_len * width * 3 * half,
            scratch=[pltpu.VMEM((blocks, part_rows, LANES), f32)],
        )
        wq = wq.reshape(width, 3 * half)
        wo_own = wo_own.reshape(width, half)
        gain_one, gain_two, bias_two = norm_rows[0:1], norm_rows[1:2], norm_rows[3:4]
        grad_arrived = swap(after(grad_packed, qkv))
        att, lse, *chunks = attend(at, qkv, seg_row, seq_size)
        wo_other = to_core(wo_own)
        wo = jnp.concatenate(
            [jnp.where(is_one, wo_other, wo_own), jnp.where(is_one, wo_own, wo_other)], axis=1
        )
        quads = [send(chunks[i], home_of(i)) for i in range(seq_size)]
        quads, grad_arrived = lax.optimization_barrier((quads, grad_arrived))
        x_home = tokens.reshape(rows, width)
        att_home, middle, *packs = single_call(
            mix_kernel,
            at,
            [*quads, x_home, wo, gain_two, bias_two, slot_near[None, :]],
            [shape(bf16, rows, width), shape(f32, rows, width)]
            + [shape(bf16, 2, slot_rows, width)] * cols,
            "mix",
            flops=2 * rows * width * (width + slots),
        )

        arrived = exchange(packs)
        hidden = []
        for members in groups:
            pairs = [arrived[m] for m in members]
            if hidden:
                pairs = after(pairs, hidden[-1])
            hidden.append(
                hidden_group(at, with_other(pairs), grad_arrived, members, w_in, w_out)
            )
        acts, dpres, sents, grads = zip(*hidden)
        grad_outer = grad_out_weight(at, acts, grads)
        grad_w_out = lax.psum_scatter(grad_outer, "seq", scatter_dimension=0, tiled=True)
        dpres = after(dpres, grad_outer)
        grad_sents = {}
        for i in (1, 2, 0):
            parts = back_group(at, dpres[i], w_in, groups[i])
            grad_sents.update(zip(groups[i], parts))
            dpres = after(dpres, parts)
        grad_back = exchange([grad_sents[m] for m in range(cols)])
        expert_out = out_rows(at, after(acts, dpres), w_out, groups)
        grad_back = with_other(after(grad_back, expert_out))
        expert_out = after(expert_out, grad_back)
        returned_near = exchange_near(expert_out)

        outs = [
            *(shape(f32, rows, width), shape(bf16, rows, width), shape(f32, 8, width)),
            *[shape(bf16, rows_seq, half)] * seq_size,
        ]
        grad_middle, grad_branch, sums_two, *quads = kernel_call(
            functools.partial(mid_back_kernel, owners=exp_size),
            1,
            at,
            [*grad_back, middle, grad_low, wo, gain_two, slot_near[:, None]],
            pair_specs(exp_size, slot_rows, width) + [None] * 5,
            [None] * len(outs),
            outs,
            2 * rows * width * (width + slots),
            "mid_back",
            [pltpu.VMEM((slots, width), bf16), pltpu.VMEM((rows, width), bf16)],
        )

        quads, returned_near = lax.optimization_barrier((quads, returned_near))
        came = [send(quads[i], worker_of(i)) for i in range(seq_size)]
        returned = exchange_far(expert_out, returned_near)
        grad_inner = grad_in_weight(at, sents, after(dpres, quads))
        grad_w_in = lax.psum_scatter(
            after(grad_inner, came), "seq", scatter_dimension=1, tiled=True
        )
        grad_wo = tn(att_home, grad_branch)
        wo_halves = [grad_wo[:, :half], grad_wo[:, half:]]
        grad_wo = jnp.where(is_one, wo_halves[1], wo_halves[0]) + to_core(
            jnp.where(is_one, wo_halves[0], wo_halves[1]).astype(bf16)
        ).astype(f32)
        came = after(came, grad_wo)
        dqkv, own, other, sums_one = attend_back(at, qkv, att, lse, seg_row, hat, came, wq)
        other = to_core(other)
        small = jnp.stack([sums_one[0], sums_two[0], sums_one[1], sums_two[1]])
        small = jnp.pad(small, ((0, LANES - 4), (0, 0))).T
        orders = [
            sorted(range(cols), key=lambda m, kk=kk: [(m >> bit) & 1 for bit in step_bits(kk)])
            for kk in range(2)
        ]
        stay_go = single_call(
            functools.partial(grad_shared_kernel, orders=orders),
            at,
            [normed, dqkv, grad_wo, small],
            [shape(bf16, cols // 2, seq_size, part_rows, wide)] * 4,
            "grad_shared",
            flops=2 * full_len * width * 3 * half,
            scratch=[pltpu.VMEM((blocks, part_rows, wide), f32)],
        )
        returned = with_other(returned)
        stay_go, returned = lax.optimization_barrier((stay_go, returned))
        back_a, back_b = single_call(
            home_rows_kernel,
            at,
            [after(own, stay_go), other, x_half, gain_one],
            [shape(bf16, rows_seq, width)] * 2,
            "home_rows",
        )
        layer_out = kernel_call(
            functools.partial(layer_out_kernel, owners=exp_size),
            1,
            at,
            [*returned, middle, slot_near[:, None]],
            pair_specs(exp_size, slot_rows, width) + [None, None],
            [None],
            [shape(bf16, rows, width)],
            2 * rows * width * slots,
            "layer_out",
            [pltpu.VMEM((slots, width), bf16)],
        )[0]
        wide_w_out = grad_w_out.astype(f32)[None]
        wide_w_in = grad_w_in.astype(f32)[None]
        (grad_tokens,) = single_call(
            tokens_kernel,
            at,
            [
                *[send(part, home_of(i)) for i, part in enumerate((back_a, back_b))],
                after(grad_middle, wide_w_in),
            ],
            [shape(f32, rows, width)],
            "tokens",
        )

        sums = []
        for kk in range(2):
            stay, go = stay_go[2 * kk], stay_go[2 * kk + 1]
            for step in range(col_bits):
                came = to_col(go, step_bits(kk)[step])
                if step == 0:
                    came = after(came, (back_a, back_b, wide_w_out))
                both = stay.astype(f32) + came.astype(f32)
                if step + 1 < col_bits:
                    count = both.shape[0] // 2
                    stay, go = both[:count], both[count:].astype(bf16)
            sums.append(both[0])
        lined = jnp.stack([sums[0].astype(bf16), to_core(sums[1].astype(bf16))], axis=1)
        parts = [lined[0]] + [to_seq(lined[i], i) for i in range(1, seq_size)]
        grad_w_qkv, grad_w_attn_out, grad_norm_scale, grad_norm_shift = single_call(
            functools.partial(final_shared_kernel, half=half),
            at,
            parts,
            [
                shape(f32, part_rows, 6 * half),
                shape(f32, part_rows, 2 * half),
                shape(f32, 2, part_rows),
                shape(f32, 2, part_rows),
            ],
            "final_shared",
        )
        return (
            layer_out.reshape(seq_dev, rows_seq, width),
            grad_tokens.reshape(seq_dev, rows_seq, width),
            grad_w_qkv,
            grad_w_attn_out,
            grad_norm_scale.T,
            grad_norm_shift.T,
            wide_w_in,
            wide_w_out,
        )

    return local


def solution(mesh):
    return jax.shard_map(
        make_local(mesh.shape["exp"], mesh.shape["seq"]),
        mesh=mesh,
        in_specs=(
            P("exp", "seq", None),
            P("exp", "seq", None),
            P("exp", "seq"),
            P("exp", None),
            P(),
            P(("exp", "seq"), None),
            P(("exp", "seq"), None),
            P(("exp", "seq"), None),
            P(("exp", "seq"), None),
            P("exp", None, None),
            P("exp", None, None),
        ),
        out_specs=(
            P("exp", "seq", None),
            P("exp", "seq", None),
            P(("exp", "seq"), None),
            P(("exp", "seq"), None),
            P(("exp", "seq"), None),
            P(("exp", "seq"), None),
            P("exp", None, "seq"),
            P("exp", "seq", None),
        ),
        check_vma=False,
    )
```

```python
import functools

import jax
import jax.numpy as jnp
from jax import lax
from jax.experimental import pallas as pl
from jax.experimental.pallas import tpu as pltpu
from jax.sharding import PartitionSpec as P

HEAD_DIM = 64
LANES = 128
BOTH = ("exp", "seq")
epsilon = 1e-05
f32 = jnp.float32
bf16 = jnp.bfloat16


def norm_parts(feature):
    center = feature - jnp.mean(feature, axis=-1, keepdims=True)
    spread = jnp.mean(center * center, axis=-1, keepdims=True)
    rstd = lax.rsqrt(spread + epsilon)
    return center * rstd, rstd


def norm_pull(grad_hat, hat, rstd):
    first = jnp.mean(grad_hat, axis=-1, keepdims=True)
    second = jnp.mean(grad_hat * hat, axis=-1, keepdims=True)
    return rstd * (grad_hat - first - hat * second)


def nt(a, b):
    return lax.dot_general(a, b, (((1,), (1,)), ((), ())), preferred_element_type=f32)


def nn(a, b):
    return lax.dot_general(a, b, (((1,), (0,)), ((), ())), preferred_element_type=f32)


def tn(a, b):
    return lax.dot_general(a, b, (((0,), (0,)), ((), ())), preferred_element_type=f32)


def after(value, *earlier):
    return lax.optimization_barrier((value, earlier))[0]


def aligned(index, size, unit=None):
    return pl.ds(pl.multiple_of(index * size, unit or size), size)


def whole_block(*shape):
    return pl.BlockSpec(shape, lambda i, at: (0,) * len(shape))


def kernel_call(body, steps, at, arrays, in_specs, out_specs, out_shape, flops, name, scratch=()):
    in_specs = [spec or whole_block(*a.shape) for spec, a in zip(in_specs, arrays)]
    out_specs = [spec or whole_block(*o.shape) for spec, o in zip(out_specs, out_shape)]
    moved = sum(a.size * a.dtype.itemsize for a in (*arrays, *out_shape))
    return pl.pallas_call(
        body,
        grid_spec=pltpu.PrefetchScalarGridSpec(
            num_scalar_prefetch=1,
            grid=(steps,),
            in_specs=in_specs,
            out_specs=out_specs,
            scratch_shapes=list(scratch),
        ),
        out_shape=list(out_shape),
        compiler_params=pltpu.CompilerParams(vmem_limit_bytes=56 << 20),
        cost_estimate=pl.CostEstimate(flops=flops, bytes_accessed=moved, transcendentals=0),
        name=name,
    )(at, *arrays)


def single_call(body, at, arrays, out_shape, name, flops=0, scratch=()):
    return kernel_call(
        body,
        1,
        at,
        arrays,
        [None] * len(arrays),
        [None] * len(out_shape),
        out_shape,
        flops,
        name,
        scratch,
    )


def shape(kind, *dims):
    return jax.ShapeDtypeStruct(dims, kind)


CORE, FLAT, LOW, SEQ, EXP, CHUNK = range(6)


def key_segments(segr_ref):
    rows = jnp.broadcast_to(segr_ref[...].astype(f32), (8, segr_ref.shape[1]))
    return rows.T[:, 0:1]


def allowed_keys(seg_keys, segr_ref, start, block):
    width = start + block
    keys = lax.broadcasted_iota(jnp.int32, (width, block), 0)
    queries = lax.broadcasted_iota(jnp.int32, (width, block), 1) + start
    same = seg_keys[0:width] == segr_ref[:, start : start + block].astype(f32)
    return same & (keys <= queries)


def split_kernel(at_ref, *refs, half, parts):
    got, (mine_ref, other_ref) = refs[:parts], refs[parts:]

    def fill(core):
        for i in range(parts):
            for ref, which in ((mine_ref, core), (other_ref, 1 - core)):
                for group in range(4):
                    start = (2 * group + which) * half
                    ref[i, :, group * half : (group + 1) * half] = got[i][:, start : start + half]
                ref[i, :, 4 * half :] = got[i][:, 8 * half :]

    pl.when(at_ref[CORE] == 0)(lambda: fill(0))
    pl.when(at_ref[CORE] == 1)(lambda: fill(1))


def norm_qkv_kernel(at_ref, *refs, half, parts, cols):
    pieces, (own_ref, other_ref) = refs[: 2 * cols], refs[2 * cols : 2 * cols + 2]
    wq_ref, wo_ref, rows_ref, hat_ref, normed_ref, qkv_ref, norm_ref = refs[2 * cols + 2 :]
    for kk in range(2):
        for m in range(cols):
            for i in range(parts):
                place = at_ref[FLAT] ^ ((2 * m + kk) * parts + i)
                block = pieces[kk * cols + m]
                wq_ref[place] = block[i, :, : 3 * half]
                wo_ref[place] = block[i, :, 3 * half : 4 * half]
                norm_ref[place] = block[i, :, 4 * half :].astype(f32)
    width = own_ref.shape[1]
    norm_rows = norm_ref[...].reshape(width, LANES).T[0:8]
    rows_ref[...] = norm_rows
    weights = wq_ref[...].reshape(width, 3 * half)
    rows = own_ref.shape[0]
    core = at_ref[CORE]
    for ref, place in ((own_ref, core), (other_ref, 1 - core)):
        hat, _ = norm_parts(ref[...].astype(f32))
        normed = (hat * norm_rows[0:1] + norm_rows[2:3]).astype(bf16)
        where = aligned(place, rows)
        hat_ref[where, :] = hat.astype(bf16)
        normed_ref[where, :] = normed
        qkv_ref[where, :] = nn(normed, weights).astype(bf16)


GELU_ONE = 0.7978845608028654
GELU_TWO = GELU_ONE * 0.044715


def attend_kernel(at_ref, q_ref, k_ref, v_ref, segr_ref, att_ref, lse_ref, *outs_ref, block):
    total = q_ref.shape[0]
    seg_keys = key_segments(segr_ref)
    values_t = v_ref[...].astype(f32).T.astype(bf16)
    lane = lax.broadcasted_iota(jnp.int32, (block, LANES), 1)
    for start in range(0, total, block):
        width = start + block
        allowed = allowed_keys(seg_keys, segr_ref, start, block)
        queries = q_ref[start:width, :] * 0.125
        outs = []
        for head in range(2):
            own = (lane >= HEAD_DIM) if head else (lane < HEAD_DIM)
            q_head = jnp.where(own, queries, 0.0).astype(bf16)
            scores = jnp.where(allowed, nt(k_ref[0:width, :], q_head), -1e30)
            top = jnp.max(scores, axis=0, keepdims=True)
            expo = jnp.exp(scores - top)
            total_row = jnp.sum(expo, axis=0, keepdims=True)
            out = nn(values_t[head * HEAD_DIM : (head + 1) * HEAD_DIM, 0:width], expo.astype(bf16))
            outs.append(out / total_row)
            lse_ref[0, head : head + 1, start:width] = top + jnp.log(total_row)
        att_ref[start:width, :] = jnp.concatenate(outs, axis=0).T.astype(bf16)
    rows = outs_ref[0].shape[0]
    for i, ref in enumerate(outs_ref):
        ref[...] = att_ref[aligned(at_ref[CHUNK] ^ i, rows), :]


def head_specs(total, pairs):
    return [
        pl.BlockSpec((total, LANES), lambda h, at, part=part: (0, part * pairs + h))
        for part in range(3)
    ]


def attend(at, qkv, seg_row, chunks):
    total, width = qkv.shape
    pairs = width // 3 // LANES
    rows = total // chunks
    piece = pl.BlockSpec((rows, LANES), lambda h, at: (0, h))
    return kernel_call(
        functools.partial(attend_kernel, block=min(512, total)),
        pairs,
        at,
        [qkv, qkv, qkv, seg_row],
        head_specs(total, pairs) + [None],
        [
            pl.BlockSpec((total, LANES), lambda h, at: (0, h)),
            pl.BlockSpec((1, 8, total), lambda h, at: (h, 0, 0)),
        ]
        + [piece] * chunks,
        [shape(bf16, total, pairs * LANES), shape(f32, pairs, 8, total)]
        + [shape(bf16, rows, pairs * LANES)] * chunks,
        4 * total * total * width // 6,
        "attend",
    )


def attend_back_kernel(
    at_ref, q_ref, k_ref, v_ref, att_ref, lse_ref, segr_ref, hat_ref, *refs, block, chunks
):
    came, (wq_ref, wk_ref, wv_ref) = refs[:chunks], refs[chunks : chunks + 3]
    out_ref, own_ref, other_ref, sums_ref, dk_ref, dv_ref, datt_ref, sum_ref = refs[chunks + 3 :]
    total = q_ref.shape[0]
    pairs = pl.num_programs(0)
    pair = pl.program_id(0)
    for i, ref in enumerate(came):
        datt_ref[aligned(at_ref[CHUNK] ^ i, total // chunks), :] = ref[...]
    lane = lax.broadcasted_iota(jnp.int32, (block, LANES), 1)
    lane_all = lax.broadcasted_iota(jnp.int32, (total, LANES), 1)
    dk_ref[...] = jnp.zeros_like(dk_ref)
    dv_ref[...] = jnp.zeros_like(dv_ref)
    seg_keys = key_segments(segr_ref)
    row8 = lax.broadcasted_iota(jnp.int32, (8, LANES), 0)
    lane8 = lax.broadcasted_iota(jnp.int32, (8, LANES), 1)
    head_rows = jnp.where(row8 == lane8 // HEAD_DIM, 1.0, 0.0)

    for start in range(0, total, block):
        width = start + block
        allowed = allowed_keys(seg_keys, segr_ref, start, block)
        queries = q_ref[start:width, :] * 0.125
        grads = datt_ref[start:width, :]
        product = grads.astype(f32) * att_ref[start:width, :].astype(f32)
        delta = lax.dot_general(
            head_rows,
            product,
            (((1,), (1,)), ((), ())),
            precision=lax.Precision.HIGHEST,
            preferred_element_type=f32,
        )
        dq = jnp.zeros((block, LANES), f32)
        for head in range(2):
            own = (lane >= HEAD_DIM) if head else (lane < HEAD_DIM)
            own_all = (lane_all >= HEAD_DIM) if head else (lane_all < HEAD_DIM)
            q_head = jnp.where(own, queries, 0.0).astype(bf16)
            g_head = jnp.where(own, grads, 0.0).astype(bf16)
            k_head = jnp.where(own_all[0:width], k_ref[0:width, :], 0.0).astype(bf16)
            scores = nt(k_ref[0:width, :], q_head)
            probs = jnp.where(allowed, jnp.exp(scores - lse_ref[0, head : head + 1, start:width]), 0.0)
            dprobs = nt(v_ref[0:width, :], g_head)
            dscores = (probs * (dprobs - delta[head : head + 1, :])).astype(bf16)
            dv_ref[0:width, :] += nn(probs.astype(bf16), g_head)
            dk_ref[0:width, :] += nn(dscores, q_head)
            dq = dq + tn(dscores, k_head)
        out_ref[start:width, aligned(pair, LANES)] = (dq * 0.125).astype(bf16)
    dk = dk_ref[...].astype(bf16)
    dv = dv_ref[...].astype(bf16)
    out_ref[:, aligned(pairs + pair, LANES)] = dk
    out_ref[:, aligned(2 * pairs + pair, LANES)] = dv
    grads = jnp.concatenate([out_ref[:, aligned(pair, LANES)], dk, dv], axis=1)
    weights = jnp.concatenate([wq_ref[...], wk_ref[...], wv_ref[...]], axis=1)
    pulled = nt(grads, weights)

    @pl.when(pair == 0)
    def _():
        sum_ref[...] = pulled

    @pl.when(pair > 0)
    def _():
        sum_ref[...] += pulled

    @pl.when(pair == pairs - 1)
    def _():
        rows = own_ref.shape[0]
        core = at_ref[CORE]
        own_ref[...] = sum_ref[aligned(core, rows), :]
        other_ref[...] = sum_ref[aligned(1 - core, rows), :].astype(bf16)
        sums_ref[0:1, :] = jnp.sum(sum_ref[...] * hat_ref[...].astype(f32), axis=0, keepdims=True)
        sums_ref[1:2, :] = jnp.sum(sum_ref[...], axis=0, keepdims=True)


def attend_back(at, qkv, att, lse, seg_row, hat, came, wq):
    total, width = qkv.shape
    model = wq.shape[0]
    pairs = width // 3 // LANES
    chunks = len(came)
    return kernel_call(
        functools.partial(attend_back_kernel, block=min(256, total), chunks=chunks),
        pairs,
        at,
        [qkv, qkv, qkv, att, lse, seg_row, hat, *came, wq, wq, wq],
        head_specs(total, pairs)
        + [
            pl.BlockSpec((total, LANES), lambda h, at: (0, h)),
            pl.BlockSpec((1, 8, total), lambda h, at: (h, 0, 0)),
            None,
            None,
        ]
        + [pl.BlockSpec((total // chunks, LANES), lambda h, at: (0, h))] * chunks
        + head_specs(model, pairs),
        [None] * 4,
        [
            shape(bf16, total, width),
            shape(f32, total // 2, model),
            shape(bf16, total // 2, model),
            shape(f32, 8, model),
        ],
        10 * total * total * width // 6,
        "attend_back",
        [
            pltpu.VMEM((total, LANES), f32),
            pltpu.VMEM((total, LANES), f32),
            pltpu.VMEM((total, LANES), bf16),
            pltpu.VMEM((total, model), f32),
        ],
    )


def mix_kernel(at_ref, q0, q1, q2, q3, x_ref, wo_ref, gain_ref, bias_ref, slot_ref, att_ref, mid_ref, *packs):
    rows, half = q0.shape
    for i, quad in enumerate((q0, q1, q2, q3)):
        place = at_ref[SEQ] ^ i
        att_ref[aligned(place & 1, rows), aligned(place >> 1, half, LANES)] = quad[...]
    middle = x_ref[...].astype(f32) + nn(att_ref[...], wo_ref[...])
    mid_ref[...] = middle
    hat, _ = norm_parts(middle)
    sent = (hat * gain_ref[...] + bias_ref[...]).astype(bf16)
    slots = packs[0].shape[1]
    for m, pack in enumerate(packs):
        place = lax.broadcasted_iota(jnp.int32, (2 * slots, sent.shape[0]), 0) + 2 * m * slots
        spread = jnp.where(place == slot_ref[...], 1.0, 0.0).astype(bf16)
        rows_out = nn(spread, sent).astype(bf16)
        pack[0] = rows_out[:slots]
        pack[1] = rows_out[slots:]


def mid_back_kernel(at_ref, *refs, owners):
    backs = refs[:owners]
    mid_ref, dy_ref, wo_ref, gain_ref, slot_ref = refs[owners : owners + 5]
    gm_ref, branch_ref, sums_ref, q0, q1, q2, q3, all_ref, datt_ref = refs[owners + 5 :]
    slots = backs[0].shape[1]
    for b, back in enumerate(backs):
        all_ref[b * slots : (b + 1) * slots, :] = back[0]
    count = mid_ref.shape[0]
    place = lax.broadcasted_iota(jnp.int32, (count, owners * slots), 1)
    spread = jnp.where(place == slot_ref[...], 1.0, 0.0).astype(bf16)
    grad = nn(spread, all_ref[...])
    hat, rstd = norm_parts(mid_ref[...])
    sums_ref[0:1, :] = jnp.sum(grad * hat, axis=0, keepdims=True)
    sums_ref[1:2, :] = jnp.sum(grad, axis=0, keepdims=True)
    grad_middle = dy_ref[...].astype(f32) + norm_pull(grad * gain_ref[...], hat, rstd)
    gm_ref[...] = grad_middle
    branch = grad_middle.astype(bf16)
    branch_ref[...] = branch
    datt_ref[...] = nt(branch, wo_ref[...]).astype(bf16)
    rows, half = q0.shape
    for i, quad in enumerate((q0, q1, q2, q3)):
        at = at_ref[SEQ] ^ i
        quad[...] = datt_ref[aligned(at & 1, rows), aligned(at >> 1, half, LANES)]


def layer_out_kernel(at_ref, *refs, owners):
    backs, (mid_ref, slot_ref, out_ref, all_ref) = refs[:owners], refs[owners:]
    slots = backs[0].shape[1]
    for b, back in enumerate(backs):
        all_ref[b * slots : (b + 1) * slots, :] = back[0]
    place = lax.broadcasted_iota(jnp.int32, (mid_ref.shape[0], owners * slots), 1)
    spread = jnp.where(place == slot_ref[...], 1.0, 0.0).astype(bf16)
    out_ref[...] = (mid_ref[...] + nn(spread, all_ref[...])).astype(bf16)


def hidden_kernel(at_ref, *refs, blocks, chunk, earlier):
    rows, grads = refs[:blocks], refs[blocks : 2 * blocks]
    in_ref, out_ref, *refs = refs[2 * blocks :]
    acts, dys, refs = refs[:earlier], refs[earlier : 2 * earlier], refs[2 * earlier :]
    act_ref, dpre_ref, x_ref, d_ref = refs[:4]
    slots = rows[0].shape[1]

    @pl.when(pl.program_id(0) == 0)
    def _():
        for b in range(blocks):
            x_ref[b * slots : (b + 1) * slots, :] = rows[b][0]
            d_ref[b * slots : (b + 1) * slots, :] = grads[b][0]

    for start in range(0, x_ref.shape[0], chunk):
        part = slice(start, start + chunk)
        pre = nn(x_ref[part, :], in_ref[...])
        dact = nt(d_ref[part, :], out_ref[...])
        square = pre * pre
        gate = 0.5 * jnp.tanh(pre * (GELU_ONE + GELU_TWO * square)) + 0.5
        act = pre * gate
        slope = gate + act * (1.0 - gate) * (2 * GELU_ONE + 6 * GELU_TWO * square)
        act_ref[part, :] = act.astype(bf16)
        dpre_ref[part, :] = (dact * slope).astype(bf16)
    if earlier:
        total = tn(act_ref[...], d_ref[...])
        for other_act, other_dy in zip(acts, dys):
            total = total + tn(other_act[...], other_dy[...])
        refs[4][...] = total.astype(bf16)


def pair_specs(blocks, slots, width):
    return [
        pl.BlockSpec((1, slots, width), lambda i, at, b=b: (b % 2, 0, 0)) for b in range(blocks)
    ]


def hidden_group(at, rows, grads, members, w_in, w_out, earlier=()):
    acts, dys = [g[0] for g in earlier], [g[3] for g in earlier]
    blocks = len(rows)
    _, slots, width = rows[0].shape
    count = blocks * slots
    hidden = w_in.shape[1]
    tile = 768 if hidden % 768 == 0 else hidden
    chunk = next((size for size in (768, 384) if count % size == 0), count)
    column = pl.BlockSpec((count, tile), lambda i, at: (0, i))
    places = [2 * m + kk for m in members for kk in range(2)]
    return kernel_call(
        functools.partial(hidden_kernel, blocks=blocks, chunk=chunk, earlier=len(acts)),
        hidden // tile,
        at,
        [*rows, *([grads] * blocks), w_in, w_out, *acts, *dys],
        pair_specs(blocks, slots, width)
        + [pl.BlockSpec((1, slots, width), lambda i, at, b=b: (b ^ at[EXP], 0, 0)) for b in places]
        + [
            pl.BlockSpec((width, tile), lambda i, at: (0, i)),
            pl.BlockSpec((tile, width), lambda i, at: (i, 0)),
        ]
        + [pl.BlockSpec((a.shape[0], tile), lambda i, at: (0, i)) for a in acts]
        + [None] * len(dys),
        [column, column, None, None]
        + [pl.BlockSpec((tile, width), lambda i, at: (i, 0))] * bool(acts),
        [shape(bf16, count, hidden)] * 2
        + [shape(bf16, count, width)] * 2
        + [shape(bf16, hidden, width)] * bool(acts),
        (4 * count + 2 * sum(a.shape[0] for a in acts)) * width * hidden,
        "hidden_group",
    )


def back_kernel(at_ref, a_ref, w_ref, *outs):
    out = nt(a_ref[...], w_ref[...]).astype(bf16)
    slots = outs[0].shape[1]
    for step, ref in enumerate(outs):

        @pl.when(pl.program_id(0) == step)
        def _(ref=ref):
            ref[0] = out[:slots]
            ref[1] = out[slots:]


def back_group(at, dpre, w_in, members):
    count, hidden = dpre.shape
    width = w_in.shape[0]
    pair = count // len(members)
    return kernel_call(
        back_kernel,
        len(members),
        at,
        [dpre, w_in],
        [pl.BlockSpec((pair, hidden), lambda i, at: (i, 0)), None],
        [None] * len(members),
        [shape(bf16, 2, pair // 2, width)] * len(members),
        2 * count * width * hidden,
        "back_group",
    )


def out_kernel(at_ref, *refs, starts, order):
    acts, w_ref, outs = refs[: len(starts) - 1], refs[len(starts) - 1], refs[len(starts) :]
    slots = outs[0].shape[1]
    step = pl.program_id(0)
    for group, act_ref in enumerate(acts):
        for i in range(starts[group], starts[group + 1]):

            @pl.when(step == i)
            def _(act_ref=act_ref, ref=outs[order[i]]):
                out = nn(act_ref[...], w_ref[...]).astype(bf16)
                ref[0] = out[:slots]
                ref[1] = out[slots:]


def out_rows(at, acts, w_out, groups):
    hidden, width = w_out.shape
    pair = acts[0].shape[0] // len(groups[0])
    starts = [sum(len(g) for g in groups[:i]) for i in range(len(groups) + 1)]
    return kernel_call(
        functools.partial(out_kernel, starts=starts, order=sum(groups, [])),
        starts[-1],
        at,
        [*acts, w_out],
        [
            pl.BlockSpec(
                (pair, hidden),
                lambda i, at, a=starts[g], b=starts[g + 1]: (jnp.clip(i, a, b - 1) - a, 0),
            )
            for g in range(len(groups))
        ]
        + [None],
        [None] * starts[-1],
        [shape(bf16, 2, pair // 2, width)] * starts[-1],
        2 * starts[-1] * pair * width * hidden,
        "out_rows",
    )


def grad_weight_kernel(at_ref, *refs):
    parts = (len(refs) - 1) // 2
    total = tn(refs[0][...], refs[parts][...])
    for i in range(1, parts):
        total = total + tn(refs[i][...], refs[parts + i][...])
    refs[-1][...] = total.astype(bf16)


def grad_in_weight(at, rows, dpres):
    hidden, width = dpres[0].shape[1], rows[0].shape[1]
    tile = 768 if hidden % 768 == 0 else hidden
    return kernel_call(
        grad_weight_kernel,
        hidden // tile,
        at,
        [*rows, *dpres],
        [None] * len(rows) + [pl.BlockSpec((a.shape[0], tile), lambda i, at: (0, i)) for a in dpres],
        [pl.BlockSpec((width, tile), lambda i, at: (0, i))],
        [shape(bf16, width, hidden)],
        2 * sum(a.shape[0] for a in dpres) * width * hidden,
        "grad_in_weight",
    )[0]


def home_rows_kernel(at_ref, own_ref, came_ref, x_ref, gain_ref, back_a_ref, back_b_ref):
    rows = back_a_ref.shape[0]
    low = at_ref[LOW]
    for out_ref, place in ((back_a_ref, low), (back_b_ref, 1 - low)):
        part = aligned(place, rows)
        grad = own_ref[part, :] + came_ref[part, :].astype(f32)
        hat, rstd = norm_parts(x_ref[part, :].astype(f32))
        out_ref[...] = norm_pull(grad * gain_ref[...], hat, rstd).astype(bf16)


def tokens_kernel(at_ref, a_ref, b_ref, gm_ref, out_ref):
    rows = a_ref.shape[0]
    low = at_ref[LOW]
    for ref, place in ((a_ref, low), (b_ref, 1 - low)):
        part = aligned(place, rows)
        out_ref[part, :] = gm_ref[part, :] + ref[...].astype(f32)


def grad_shared_kernel(at_ref, normed_ref, dqkv_ref, gwo_ref, small_ref, *refs, orders):
    outs, all_ref = refs[:4], refs[4]
    blocks, part_rows, wide = all_ref.shape
    columns = dqkv_ref.shape[1]
    half = gwo_ref.shape[1]
    each = 128
    for start in range(0, columns, each * 3):
        stop = start + each * 3
        part = tn(normed_ref[...], dqkv_ref[:, start:stop])
        all_ref[:, :, start:stop] = part.reshape(blocks, part_rows, stop - start)
    all_ref[:, :, columns : columns + half] = gwo_ref[...].reshape(blocks, part_rows, half)
    all_ref[:, :, columns + half :] = small_ref[...].reshape(blocks, part_rows, wide - columns - half)
    for kk in range(2):
        for side in range(2):
            ref = outs[2 * kk + side]
            for j in range(ref.shape[0]):
                m = orders[kk][side * ref.shape[0] + j]
                for i in range(ref.shape[1]):
                    place = at_ref[FLAT] ^ ((2 * m + kk) * ref.shape[1] + i)
                    ref[j, i] = all_ref[place].astype(ref.dtype)


def final_shared_kernel(at_ref, *refs, half):
    parts, (qkv_ref, out_ref, scale_ref, shift_ref) = refs[:-4], refs[-4:]
    total = parts[0][...].astype(f32)
    for part in parts[1:]:
        total = total + part[...].astype(f32)
    norms = total[0][:, 4 * half :] + total[1][:, 4 * half :]
    row = lax.broadcasted_iota(jnp.int32, (8, norms.shape[1]), 0)
    lane = lax.broadcasted_iota(jnp.int32, (8, norms.shape[1]), 1)
    turned = lax.dot_general(
        jnp.where(row == lane, 1.0, 0.0),
        norms,
        (((1,), (1,)), ((), ())),
        precision=lax.Precision.HIGHEST,
        preferred_element_type=f32,
    )
    scale_ref[...] = turned[0:2]
    shift_ref[...] = turned[2:4]

    def fill(core):
        for mine in range(2):
            which = core ^ mine
            for group in range(3):
                start = (2 * group + which) * half
                qkv_ref[:, start : start + half] = total[mine][:, group * half : (group + 1) * half]
            out_ref[:, which * half : (which + 1) * half] = total[mine][:, 3 * half : 4 * half]

    pl.when(at_ref[CORE] == 0)(lambda: fill(0))
    pl.when(at_ref[CORE] == 1)(lambda: fill(1))


def make_local(exp_size, seq_size):
    cols = exp_size // 2
    col_bits = cols.bit_length() - 1
    near = [m for m in range(1, cols) if m & (m - 1) == 0]
    far = [m for m in range(1, cols) if m & (m - 1)]
    groups = [[0], near, far]

    def flat_perm(target):
        pairs = []
        for exp in range(exp_size):
            for seq in range(seq_size):
                col, core = exp >> 1, exp & 1
                new_col, new_core, new_seq = target(col, core, seq)
                pairs.append((exp * seq_size + seq, (new_col * 2 + new_core) * seq_size + new_seq))
        return pairs

    def send(array, target):
        return lax.ppermute(array, BOTH, flat_perm(target))

    def to_core(array):
        return send(array, lambda c, k, z: (c, 1 - k, z))

    def to_seq(array, shift):
        return send(array, lambda c, k, z: (c, k, z ^ shift))

    def to_col(array, bit):
        return send(array, lambda c, k, z: (c ^ (1 << bit), k, z))

    def exchange(pairs):
        came = exchange_near(pairs)
        return exchange_far(pairs, came)

    def chip_send(m, pair):
        return send(pair, lambda c, k, z: (c ^ m, k, z))

    def exchange_near(pairs):
        return {0: pairs[0], **{m: chip_send(m, pairs[m]) for m in near}}

    def exchange_far(pairs, came):
        waits = [came[m] for m in near]
        rest = {m: chip_send(m, after(pairs[m], waits)) for m in far}
        return [rest[m] if m in rest else came[m] for m in range(cols)]

    def with_other(pairs):
        return [part for pair in pairs for part in (pair, to_core(pair))]

    def home_of(i):
        return lambda c, k, z: (c, z >> 1, (2 * k + (z & 1)) ^ i)

    def worker_of(i):
        return lambda c, k, z: (c, (z ^ i) >> 1, 2 * k + ((z ^ i) & 1))

    def step_bits(kk):
        return list(range(col_bits))[:: 1 - 2 * kk]

    def local(
        tokens,
        cotangent,
        token_ids,
        segments,
        hash_table,
        w_qkv,
        w_attn_out,
        norm_scale,
        norm_shift,
        w_in,
        w_out,
    ):
        seq_dev, rows_seq, width = tokens.shape
        rows = seq_dev * rows_seq
        slot_rows = 3 * rows // exp_size
        full_len = rows_seq * seq_size
        half = width // 2
        wide = 4 * half + LANES
        part_rows = w_qkv.shape[0]
        blocks = seq_size * 2 * cols
        w_in, w_out = w_in[0], w_out[0]
        exp_at = lax.axis_index("exp")
        z = lax.axis_index("seq")
        k = exp_at & 1
        is_one = k == 1
        z0 = z & 1
        at = jnp.stack([k, exp_at * seq_size + z, z0, z, exp_at, 2 * k + z0]).astype(jnp.int32)

        norms = jnp.concatenate([norm_scale, norm_shift], axis=1)
        norms = jnp.pad(norms, ((0, 0), (0, LANES - norms.shape[1])))
        pack = jnp.concatenate([w_qkv, w_attn_out, norms], axis=1)
        got = [pack] + [to_seq(pack, i) for i in range(1, seq_size)]
        seg_pair = jnp.where((z >> 1) == k, segments, to_core(segments))
        seg_row = jnp.where(z0 == 1, seg_pair[1:2], seg_pair[0:1])

        expert = hash_table[token_ids.reshape(-1)]
        order = jnp.arange(rows, dtype=jnp.int32)
        earlier = (expert[None, :] == expert[:, None]) & (order[None, :] < order[:, None])
        slot_rank = jnp.sum(earlier.astype(jnp.int32), axis=1)
        slots = exp_size * slot_rows
        slot_index = expert * slot_rows + slot_rank
        slot_near = (expert ^ exp_at) * slot_rows + slot_rank
        spread = (jnp.arange(slots, dtype=jnp.int32)[:, None] == slot_index[None, :]).astype(bf16)

        def swap(array):
            return lax.all_to_all(
                array.reshape(exp_size, slot_rows, width),
                "exp",
                split_axis=0,
                concat_axis=0,
                tiled=True,
            )

        grad_low = cotangent.reshape(rows, width)
        grad_packed = nn(spread, grad_low).astype(bf16)
        got, _ = lax.optimization_barrier((got, (grad_packed, slot_near, seg_row)))
        mine, other = single_call(
            functools.partial(split_kernel, half=half, parts=seq_size),
            at,
            got,
            [shape(bf16, seq_size, part_rows, wide)] * 2,
            "split_cores",
        )
        pair = [jnp.where(z0 == 1, tokens[1 - i], tokens[i]) for i in range(2)]
        here = [send(pair[0], home_of(0)), send(pair[1], home_of(1))]
        x_half = jnp.concatenate(
            [jnp.where(z0 == 1, here[1 - i], here[i]) for i in range(2)], axis=0
        )
        pieces = [[mine], [to_core(other)]]
        x_other = None
        for step in range(col_bits):
            if step == 1:
                pieces, x_half = lax.optimization_barrier((pieces, x_half))
                x_other = to_core(x_half)
            pieces = [
                own + [to_col(piece, step_bits(kk)[step]) for piece in own]
                for kk, own in enumerate(pieces)
            ]
        ordered = []
        for kk in range(2):
            bits = step_bits(kk)
            by_place = {}
            for index, piece in enumerate(pieces[kk]):
                place = sum(1 << bits[step] for step in range(col_bits) if (index >> step) & 1)
                by_place[place] = piece
            ordered += [by_place[place] for place in range(cols)]
        wq, wo_own, norm_rows, hat, normed, qkv = single_call(
            functools.partial(norm_qkv_kernel, half=half, parts=seq_size, cols=cols),
            at,
            [*ordered, x_half, x_other],
            [
                shape(bf16, blocks, part_rows, 3 * half),
                shape(bf16, blocks, part_rows, half),
                shape(f32, 8, width),
                shape(bf16, full_len, width),
                shape(bf16, full_len, width),
                shape(bf16, full_len, 3 * half),
            ],
            "norm_qkv",
            flops=2 * full_len * width * 3 * half,
            scratch=[pltpu.VMEM((blocks, part_rows, LANES), f32)],
        )
        wq = wq.reshape(width, 3 * half)
        wo_own = wo_own.reshape(width, half)
        gain_one, gain_two, bias_two = norm_rows[0:1], norm_rows[1:2], norm_rows[3:4]
        grad_arrived = swap(after(grad_packed, qkv))
        att, lse, *chunks = attend(at, qkv, seg_row, seq_size)
        wo_other = to_core(wo_own)
        wo = jnp.concatenate(
            [jnp.where(is_one, wo_other, wo_own), jnp.where(is_one, wo_own, wo_other)], axis=1
        )
        quads = [send(chunks[i], home_of(i)) for i in range(seq_size)]
        quads, grad_arrived = lax.optimization_barrier((quads, grad_arrived))
        x_home = tokens.reshape(rows, width)
        att_home, middle, *packs = single_call(
            mix_kernel,
            at,
            [*quads, x_home, wo, gain_two, bias_two, slot_near[None, :]],
            [shape(bf16, rows, width), shape(f32, rows, width)]
            + [shape(bf16, 2, slot_rows, width)] * cols,
            "mix",
            flops=2 * rows * width * (width + slots),
        )

        arrived = exchange(packs)
        hidden = []
        for members in groups:
            pairs = [arrived[m] for m in members]
            if hidden:
                pairs = after(pairs, hidden[-1])
            earlier = hidden if len(hidden) == 2 else ()
            hidden.append(
                hidden_group(
                    at, with_other(pairs), grad_arrived, members, w_in, w_out, earlier
                )
            )
        grad_outer = hidden[2][4]
        hidden[2] = hidden[2][:4]
        acts, dpres, sents, grads = zip(*hidden)
        grad_w_out = lax.psum_scatter(grad_outer, "seq", scatter_dimension=0, tiled=True)
        dpres = after(dpres, grad_outer)
        grad_sents = {}
        for i in (1, 2, 0):
            parts = back_group(at, dpres[i], w_in, groups[i])
            grad_sents.update(zip(groups[i], parts))
            dpres = after(dpres, parts)
        grad_back = exchange([grad_sents[m] for m in range(cols)])
        expert_out = out_rows(at, after(acts, dpres), w_out, groups)
        grad_back = with_other(after(grad_back, expert_out))
        expert_out = after(expert_out, grad_back)
        returned_near = exchange_near(expert_out)

        outs = [
            *(shape(f32, rows, width), shape(bf16, rows, width), shape(f32, 8, width)),
            *[shape(bf16, rows_seq, half)] * seq_size,
        ]
        grad_middle, grad_branch, sums_two, *quads = kernel_call(
            functools.partial(mid_back_kernel, owners=exp_size),
            1,
            at,
            [*grad_back, middle, grad_low, wo, gain_two, slot_near[:, None]],
            pair_specs(exp_size, slot_rows, width) + [None] * 5,
            [None] * len(outs),
            outs,
            2 * rows * width * (width + slots),
            "mid_back",
            [pltpu.VMEM((slots, width), bf16), pltpu.VMEM((rows, width), bf16)],
        )

        quads, returned_near = lax.optimization_barrier((quads, returned_near))
        came = [send(quads[i], worker_of(i)) for i in range(seq_size)]
        returned = exchange_far(expert_out, returned_near)
        grad_inner = grad_in_weight(at, sents, after(dpres, quads))
        grad_w_in = lax.psum_scatter(
            after(grad_inner, came), "seq", scatter_dimension=1, tiled=True
        )
        grad_wo = tn(att_home, grad_branch)
        wo_halves = [grad_wo[:, :half], grad_wo[:, half:]]
        grad_wo = jnp.where(is_one, wo_halves[1], wo_halves[0]) + to_core(
            jnp.where(is_one, wo_halves[0], wo_halves[1]).astype(bf16)
        ).astype(f32)
        came = after(came, grad_wo)
        dqkv, own, other, sums_one = attend_back(at, qkv, att, lse, seg_row, hat, came, wq)
        other = to_core(other)
        small = jnp.stack([sums_one[0], sums_two[0], sums_one[1], sums_two[1]])
        small = jnp.pad(small, ((0, LANES - 4), (0, 0))).T
        orders = [
            sorted(range(cols), key=lambda m, kk=kk: [(m >> bit) & 1 for bit in step_bits(kk)])
            for kk in range(2)
        ]
        stay_go = single_call(
            functools.partial(grad_shared_kernel, orders=orders),
            at,
            [normed, dqkv, grad_wo, small],
            [shape(bf16, cols // 2, seq_size, part_rows, wide)] * 4,
            "grad_shared",
            flops=2 * full_len * width * 3 * half,
            scratch=[pltpu.VMEM((blocks, part_rows, wide), f32)],
        )
        returned = with_other(returned)
        stay_go, returned = lax.optimization_barrier((stay_go, returned))
        back_a, back_b = single_call(
            home_rows_kernel,
            at,
            [after(own, stay_go), other, x_half, gain_one],
            [shape(bf16, rows_seq, width)] * 2,
            "home_rows",
        )
        layer_out = kernel_call(
            functools.partial(layer_out_kernel, owners=exp_size),
            1,
            at,
            [*returned, middle, slot_near[:, None]],
            pair_specs(exp_size, slot_rows, width) + [None, None],
            [None],
            [shape(bf16, rows, width)],
            2 * rows * width * slots,
            "layer_out",
            [pltpu.VMEM((slots, width), bf16)],
        )[0]
        wide_w_out = grad_w_out.astype(f32)[None]
        wide_w_in = grad_w_in.astype(f32)[None]
        (grad_tokens,) = single_call(
            tokens_kernel,
            at,
            [
                *[send(part, home_of(i)) for i, part in enumerate((back_a, back_b))],
                after(grad_middle, wide_w_in),
            ],
            [shape(f32, rows, width)],
            "tokens",
        )

        sums = []
        for kk in range(2):
            stay, go = stay_go[2 * kk], stay_go[2 * kk + 1]
            for step in range(col_bits):
                came = to_col(go, step_bits(kk)[step])
                if step == 0:
                    came = after(came, (back_a, back_b, wide_w_out))
                both = stay.astype(f32) + came.astype(f32)
                if step + 1 < col_bits:
                    count = both.shape[0] // 2
                    stay, go = both[:count], both[count:].astype(bf16)
            sums.append(both[0])
        lined = jnp.stack([sums[0].astype(bf16), to_core(sums[1].astype(bf16))], axis=1)
        parts = [lined[0]] + [to_seq(lined[i], i) for i in range(1, seq_size)]
        grad_w_qkv, grad_w_attn_out, grad_norm_scale, grad_norm_shift = single_call(
            functools.partial(final_shared_kernel, half=half),
            at,
            parts,
            [
                shape(f32, part_rows, 6 * half),
                shape(f32, part_rows, 2 * half),
                shape(f32, 2, part_rows),
                shape(f32, 2, part_rows),
            ],
            "final_shared",
        )
        return (
            layer_out.reshape(seq_dev, rows_seq, width),
            grad_tokens.reshape(seq_dev, rows_seq, width),
            grad_w_qkv,
            grad_w_attn_out,
            grad_norm_scale.T,
            grad_norm_shift.T,
            wide_w_in,
            wide_w_out,
        )

    return local


def solution(mesh):
    return jax.shard_map(
        make_local(mesh.shape["exp"], mesh.shape["seq"]),
        mesh=mesh,
        in_specs=(
            P("exp", "seq", None),
            P("exp", "seq", None),
            P("exp", "seq"),
            P("exp", None),
            P(),
            P(("exp", "seq"), None),
            P(("exp", "seq"), None),
            P(("exp", "seq"), None),
            P(("exp", "seq"), None),
            P("exp", None, None),
            P("exp", None, None),
        ),
        out_specs=(
            P("exp", "seq", None),
            P("exp", "seq", None),
            P(("exp", "seq"), None),
            P(("exp", "seq"), None),
            P(("exp", "seq"), None),
            P(("exp", "seq"), None),
            P("exp", None, "seq"),
            P("exp", "seq", None),
        ),
        check_vma=False,
    )
```

```python
import functools

import jax
import jax.numpy as jnp
from jax import lax
from jax.experimental import pallas as pl
from jax.experimental.pallas import tpu as pltpu
from jax.sharding import PartitionSpec as P

HEAD_DIM = 64
LANES = 128
BOTH = ("exp", "seq")
epsilon = 1e-05
f32 = jnp.float32
bf16 = jnp.bfloat16


def norm_parts(feature):
    center = feature - jnp.mean(feature, axis=-1, keepdims=True)
    spread = jnp.mean(center * center, axis=-1, keepdims=True)
    rstd = lax.rsqrt(spread + epsilon)
    return center * rstd, rstd


def norm_pull(grad_hat, hat, rstd):
    first = jnp.mean(grad_hat, axis=-1, keepdims=True)
    second = jnp.mean(grad_hat * hat, axis=-1, keepdims=True)
    return rstd * (grad_hat - first - hat * second)


def nt(a, b):
    return lax.dot_general(a, b, (((1,), (1,)), ((), ())), preferred_element_type=f32)


def nn(a, b):
    return lax.dot_general(a, b, (((1,), (0,)), ((), ())), preferred_element_type=f32)


def tn(a, b):
    return lax.dot_general(a, b, (((0,), (0,)), ((), ())), preferred_element_type=f32)


def after(value, *earlier):
    return lax.optimization_barrier((value, earlier))[0]


def aligned(index, size, unit=None):
    return pl.ds(pl.multiple_of(index * size, unit or size), size)


def whole_block(*shape):
    return pl.BlockSpec(shape, lambda i, at: (0,) * len(shape))


def kernel_call(body, steps, at, arrays, in_specs, out_specs, out_shape, flops, name, scratch=()):
    in_specs = [spec or whole_block(*a.shape) for spec, a in zip(in_specs, arrays)]
    out_specs = [spec or whole_block(*o.shape) for spec, o in zip(out_specs, out_shape)]
    moved = sum(a.size * a.dtype.itemsize for a in (*arrays, *out_shape))
    return pl.pallas_call(
        body,
        grid_spec=pltpu.PrefetchScalarGridSpec(
            num_scalar_prefetch=1,
            grid=(steps,),
            in_specs=in_specs,
            out_specs=out_specs,
            scratch_shapes=list(scratch),
        ),
        out_shape=list(out_shape),
        compiler_params=pltpu.CompilerParams(vmem_limit_bytes=56 << 20),
        cost_estimate=pl.CostEstimate(flops=flops, bytes_accessed=moved, transcendentals=0),
        name=name,
    )(at, *arrays)


def single_call(body, at, arrays, out_shape, name, flops=0, scratch=()):
    return kernel_call(
        body,
        1,
        at,
        arrays,
        [None] * len(arrays),
        [None] * len(out_shape),
        out_shape,
        flops,
        name,
        scratch,
    )


def shape(kind, *dims):
    return jax.ShapeDtypeStruct(dims, kind)


CORE, FLAT, LOW, SEQ, EXP, CHUNK = range(6)


def key_segments(segr_ref):
    rows = jnp.broadcast_to(segr_ref[...].astype(f32), (8, segr_ref.shape[1]))
    return rows.T[:, 0:1]


def allowed_keys(seg_keys, segr_ref, start, block):
    width = start + block
    keys = lax.broadcasted_iota(jnp.int32, (width, block), 0)
    queries = lax.broadcasted_iota(jnp.int32, (width, block), 1) + start
    same = seg_keys[0:width] == segr_ref[:, start : start + block].astype(f32)
    return same & (keys <= queries)


def split_kernel(at_ref, *refs, half, parts):
    got, (mine_ref, other_ref) = refs[:parts], refs[parts:]

    def fill(core):
        for i in range(parts):
            for ref, which in ((mine_ref, core), (other_ref, 1 - core)):
                for group in range(4):
                    start = (2 * group + which) * half
                    ref[i, :, group * half : (group + 1) * half] = got[i][:, start : start + half]
                ref[i, :, 4 * half :] = got[i][:, 8 * half :]

    pl.when(at_ref[CORE] == 0)(lambda: fill(0))
    pl.when(at_ref[CORE] == 1)(lambda: fill(1))


def norm_qkv_kernel(at_ref, *refs, half, parts, cols):
    pieces, (own_ref, other_ref) = refs[: 2 * cols], refs[2 * cols : 2 * cols + 2]
    wq_ref, wo_ref, rows_ref, hat_ref, normed_ref, qkv_ref, norm_ref = refs[2 * cols + 2 :]
    for kk in range(2):
        for m in range(cols):
            for i in range(parts):
                place = at_ref[FLAT] ^ ((2 * m + kk) * parts + i)
                block = pieces[kk * cols + m]
                wq_ref[place] = block[i, :, : 3 * half]
                wo_ref[place] = block[i, :, 3 * half : 4 * half]
                norm_ref[place] = block[i, :, 4 * half :].astype(f32)
    width = own_ref.shape[1]
    norm_rows = norm_ref[...].reshape(width, LANES).T[0:8]
    rows_ref[...] = norm_rows
    weights = wq_ref[...].reshape(width, 3 * half)
    rows = own_ref.shape[0]
    core = at_ref[CORE]
    for ref, place in ((own_ref, core), (other_ref, 1 - core)):
        hat, _ = norm_parts(ref[...].astype(f32))
        normed = (hat * norm_rows[0:1] + norm_rows[2:3]).astype(bf16)
        where = aligned(place, rows)
        hat_ref[where, :] = hat.astype(bf16)
        normed_ref[where, :] = normed
        qkv_ref[where, :] = nn(normed, weights).astype(bf16)


GELU_ONE = 0.7978845608028654
GELU_TWO = GELU_ONE * 0.044715


def attend_kernel(at_ref, q_ref, k_ref, v_ref, segr_ref, att_ref, lse_ref, *outs_ref, block):
    total = q_ref.shape[0]
    seg_keys = key_segments(segr_ref)
    values_t = v_ref[...].astype(f32).T.astype(bf16)
    lane = lax.broadcasted_iota(jnp.int32, (block, LANES), 1)
    for start in range(0, total, block):
        width = start + block
        allowed = allowed_keys(seg_keys, segr_ref, start, block)
        queries = q_ref[start:width, :] * 0.125
        outs = []
        for head in range(2):
            own = (lane >= HEAD_DIM) if head else (lane < HEAD_DIM)
            q_head = jnp.where(own, queries, 0.0).astype(bf16)
            scores = jnp.where(allowed, nt(k_ref[0:width, :], q_head), -1e30)
            top = jnp.max(scores, axis=0, keepdims=True)
            expo = jnp.exp(scores - top)
            total_row = jnp.sum(expo, axis=0, keepdims=True)
            out = nn(values_t[head * HEAD_DIM : (head + 1) * HEAD_DIM, 0:width], expo.astype(bf16))
            outs.append(out / total_row)
            lse_ref[0, head : head + 1, start:width] = top + jnp.log(total_row)
        att_ref[start:width, :] = jnp.concatenate(outs, axis=0).T.astype(bf16)
    rows = outs_ref[0].shape[0]
    for i, ref in enumerate(outs_ref):
        ref[...] = att_ref[aligned(at_ref[CHUNK] ^ i, rows), :]


def head_specs(total, pairs):
    return [
        pl.BlockSpec((total, LANES), lambda h, at, part=part: (0, part * pairs + h))
        for part in range(3)
    ]


def attend(at, qkv, seg_row, chunks):
    total, width = qkv.shape
    pairs = width // 3 // LANES
    rows = total // chunks
    piece = pl.BlockSpec((rows, LANES), lambda h, at: (0, h))
    return kernel_call(
        functools.partial(attend_kernel, block=min(512, total)),
        pairs,
        at,
        [qkv, qkv, qkv, seg_row],
        head_specs(total, pairs) + [None],
        [
            pl.BlockSpec((total, LANES), lambda h, at: (0, h)),
            pl.BlockSpec((1, 8, total), lambda h, at: (h, 0, 0)),
        ]
        + [piece] * chunks,
        [shape(bf16, total, pairs * LANES), shape(f32, pairs, 8, total)]
        + [shape(bf16, rows, pairs * LANES)] * chunks,
        4 * total * total * width // 6,
        "attend",
    )


def attend_back_kernel(
    at_ref, q_ref, k_ref, v_ref, att_ref, lse_ref, segr_ref, hat_ref, *refs, block, chunks
):
    came, (wq_ref, wk_ref, wv_ref) = refs[:chunks], refs[chunks : chunks + 3]
    out_ref, own_ref, other_ref, sums_ref, dk_ref, dv_ref, datt_ref, sum_ref = refs[chunks + 3 :]
    total = q_ref.shape[0]
    pairs = pl.num_programs(0)
    pair = pl.program_id(0)
    for i, ref in enumerate(came):
        datt_ref[aligned(at_ref[CHUNK] ^ i, total // chunks), :] = ref[...]
    lane = lax.broadcasted_iota(jnp.int32, (block, LANES), 1)
    lane_all = lax.broadcasted_iota(jnp.int32, (total, LANES), 1)
    dk_ref[...] = jnp.zeros_like(dk_ref)
    dv_ref[...] = jnp.zeros_like(dv_ref)
    seg_keys = key_segments(segr_ref)
    row8 = lax.broadcasted_iota(jnp.int32, (8, LANES), 0)
    lane8 = lax.broadcasted_iota(jnp.int32, (8, LANES), 1)
    head_rows = jnp.where(row8 == lane8 // HEAD_DIM, 1.0, 0.0)

    for start in range(0, total, block):
        width = start + block
        allowed = allowed_keys(seg_keys, segr_ref, start, block)
        queries = q_ref[start:width, :] * 0.125
        grads = datt_ref[start:width, :]
        product = grads.astype(f32) * att_ref[start:width, :].astype(f32)
        delta = lax.dot_general(
            head_rows,
            product,
            (((1,), (1,)), ((), ())),
            precision=lax.Precision.HIGHEST,
            preferred_element_type=f32,
        )
        dq = jnp.zeros((block, LANES), f32)
        for head in range(2):
            own = (lane >= HEAD_DIM) if head else (lane < HEAD_DIM)
            own_all = (lane_all >= HEAD_DIM) if head else (lane_all < HEAD_DIM)
            q_head = jnp.where(own, queries, 0.0).astype(bf16)
            g_head = jnp.where(own, grads, 0.0).astype(bf16)
            k_head = jnp.where(own_all[0:width], k_ref[0:width, :], 0.0).astype(bf16)
            scores = nt(k_ref[0:width, :], q_head)
            probs = jnp.where(allowed, jnp.exp(scores - lse_ref[0, head : head + 1, start:width]), 0.0)
            dprobs = nt(v_ref[0:width, :], g_head)
            dscores = (probs * (dprobs - delta[head : head + 1, :])).astype(bf16)
            dv_ref[0:width, :] += nn(probs.astype(bf16), g_head)
            dk_ref[0:width, :] += nn(dscores, q_head)
            dq = dq + tn(dscores, k_head)
        out_ref[start:width, aligned(pair, LANES)] = (dq * 0.125).astype(bf16)
    dk = dk_ref[...].astype(bf16)
    dv = dv_ref[...].astype(bf16)
    out_ref[:, aligned(pairs + pair, LANES)] = dk
    out_ref[:, aligned(2 * pairs + pair, LANES)] = dv
    grads = jnp.concatenate([out_ref[:, aligned(pair, LANES)], dk, dv], axis=1)
    weights = jnp.concatenate([wq_ref[...], wk_ref[...], wv_ref[...]], axis=1)
    pulled = nt(grads, weights)

    @pl.when(pair == 0)
    def _():
        sum_ref[...] = pulled

    @pl.when(pair > 0)
    def _():
        sum_ref[...] += pulled

    @pl.when(pair == pairs - 1)
    def _():
        rows = own_ref.shape[0]
        core = at_ref[CORE]
        own_ref[...] = sum_ref[aligned(core, rows), :]
        other_ref[...] = sum_ref[aligned(1 - core, rows), :].astype(bf16)
        sums_ref[0:1, :] = jnp.sum(sum_ref[...] * hat_ref[...].astype(f32), axis=0, keepdims=True)
        sums_ref[1:2, :] = jnp.sum(sum_ref[...], axis=0, keepdims=True)


def attend_back(at, qkv, att, lse, seg_row, hat, came, wq):
    total, width = qkv.shape
    model = wq.shape[0]
    pairs = width // 3 // LANES
    chunks = len(came)
    return kernel_call(
        functools.partial(attend_back_kernel, block=min(256, total), chunks=chunks),
        pairs,
        at,
        [qkv, qkv, qkv, att, lse, seg_row, hat, *came, wq, wq, wq],
        head_specs(total, pairs)
        + [
            pl.BlockSpec((total, LANES), lambda h, at: (0, h)),
            pl.BlockSpec((1, 8, total), lambda h, at: (h, 0, 0)),
            None,
            None,
        ]
        + [pl.BlockSpec((total // chunks, LANES), lambda h, at: (0, h))] * chunks
        + head_specs(model, pairs),
        [None] * 4,
        [
            shape(bf16, total, width),
            shape(f32, total // 2, model),
            shape(bf16, total // 2, model),
            shape(f32, 8, model),
        ],
        10 * total * total * width // 6,
        "attend_back",
        [
            pltpu.VMEM((total, LANES), f32),
            pltpu.VMEM((total, LANES), f32),
            pltpu.VMEM((total, LANES), bf16),
            pltpu.VMEM((total, model), f32),
        ],
    )


def mix_kernel(at_ref, q0, q1, q2, q3, x_ref, wo_ref, gain_ref, bias_ref, slot_ref, att_ref, mid_ref, *packs):
    rows, half = q0.shape
    for i, quad in enumerate((q0, q1, q2, q3)):
        place = at_ref[SEQ] ^ i
        att_ref[aligned(place & 1, rows), aligned(place >> 1, half, LANES)] = quad[...]
    middle = x_ref[...].astype(f32) + nn(att_ref[...], wo_ref[...])
    mid_ref[...] = middle
    hat, _ = norm_parts(middle)
    sent = (hat * gain_ref[...] + bias_ref[...]).astype(bf16)
    slots = packs[0].shape[1]
    for m, pack in enumerate(packs):
        place = lax.broadcasted_iota(jnp.int32, (2 * slots, sent.shape[0]), 0) + 2 * m * slots
        spread = jnp.where(place == slot_ref[...], 1.0, 0.0).astype(bf16)
        rows_out = nn(spread, sent).astype(bf16)
        pack[0] = rows_out[:slots]
        pack[1] = rows_out[slots:]


def mid_back_kernel(at_ref, *refs, owners):
    backs = refs[:owners]
    mid_ref, dy_ref, wo_ref, gain_ref, slot_ref = refs[owners : owners + 5]
    gm_ref, branch_ref, sums_ref, q0, q1, q2, q3, all_ref, datt_ref = refs[owners + 5 :]
    slots = backs[0].shape[1]
    for b, back in enumerate(backs):
        all_ref[b * slots : (b + 1) * slots, :] = back[0]
    count = mid_ref.shape[0]
    place = lax.broadcasted_iota(jnp.int32, (count, owners * slots), 1)
    spread = jnp.where(place == slot_ref[...], 1.0, 0.0).astype(bf16)
    grad = nn(spread, all_ref[...])
    hat, rstd = norm_parts(mid_ref[...])
    sums_ref[0:1, :] = jnp.sum(grad * hat, axis=0, keepdims=True)
    sums_ref[1:2, :] = jnp.sum(grad, axis=0, keepdims=True)
    grad_middle = dy_ref[...].astype(f32) + norm_pull(grad * gain_ref[...], hat, rstd)
    gm_ref[...] = grad_middle
    branch = grad_middle.astype(bf16)
    branch_ref[...] = branch
    datt_ref[...] = nt(branch, wo_ref[...]).astype(bf16)
    rows, half = q0.shape
    for i, quad in enumerate((q0, q1, q2, q3)):
        at = at_ref[SEQ] ^ i
        quad[...] = datt_ref[aligned(at & 1, rows), aligned(at >> 1, half, LANES)]


def layer_out_kernel(at_ref, *refs, owners):
    backs, (mid_ref, slot_ref, out_ref, all_ref) = refs[:owners], refs[owners:]
    slots = backs[0].shape[1]
    for b, back in enumerate(backs):
        all_ref[b * slots : (b + 1) * slots, :] = back[0]
    place = lax.broadcasted_iota(jnp.int32, (mid_ref.shape[0], owners * slots), 1)
    spread = jnp.where(place == slot_ref[...], 1.0, 0.0).astype(bf16)
    out_ref[...] = (mid_ref[...] + nn(spread, all_ref[...])).astype(bf16)


def hidden_kernel(at_ref, *refs, blocks, chunk, earlier):
    rows, grads = refs[:blocks], refs[blocks : 2 * blocks]
    in_ref, out_ref, *refs = refs[2 * blocks :]
    acts, dys, refs = refs[:earlier], refs[earlier : 2 * earlier], refs[2 * earlier :]
    act_ref, dpre_ref, x_ref, d_ref = refs[:4]
    slots = rows[0].shape[1]

    @pl.when(pl.program_id(0) == 0)
    def _():
        for b in range(blocks):
            x_ref[b * slots : (b + 1) * slots, :] = rows[b][0]
            d_ref[b * slots : (b + 1) * slots, :] = grads[b][0]

    for start in range(0, x_ref.shape[0], chunk):
        part = slice(start, start + chunk)
        pre = nn(x_ref[part, :], in_ref[...])
        dact = nt(d_ref[part, :], out_ref[...])
        square = pre * pre
        gate = 0.5 * jnp.tanh(pre * (GELU_ONE + GELU_TWO * square)) + 0.5
        act = pre * gate
        slope = gate + act * (1.0 - gate) * (2 * GELU_ONE + 6 * GELU_TWO * square)
        act_ref[part, :] = act.astype(bf16)
        dpre_ref[part, :] = (dact * slope).astype(bf16)
    if earlier:
        total = tn(act_ref[...], d_ref[...])
        for other_act, other_dy in zip(acts, dys):
            total = total + tn(other_act[...], other_dy[...])
        refs[4][...] = total.astype(bf16)


def pair_specs(blocks, slots, width):
    return [
        pl.BlockSpec((1, slots, width), lambda i, at, b=b: (b % 2, 0, 0)) for b in range(blocks)
    ]


def hidden_group(at, rows, grads, members, w_in, w_out, earlier=()):
    acts, dys = [g[0] for g in earlier], [g[3] for g in earlier]
    blocks = len(rows)
    _, slots, width = rows[0].shape
    count = blocks * slots
    hidden = w_in.shape[1]
    tile = next((size for size in (512 if earlier else 768, 768) if hidden % size == 0), hidden)
    chunk = next((size for size in (768, 384) if count % size == 0), count)
    column = pl.BlockSpec((count, tile), lambda i, at: (0, i))
    places = [2 * m + kk for m in members for kk in range(2)]
    return kernel_call(
        functools.partial(hidden_kernel, blocks=blocks, chunk=chunk, earlier=len(acts)),
        hidden // tile,
        at,
        [*rows, *([grads] * blocks), w_in, w_out, *acts, *dys],
        pair_specs(blocks, slots, width)
        + [pl.BlockSpec((1, slots, width), lambda i, at, b=b: (b ^ at[EXP], 0, 0)) for b in places]
        + [
            pl.BlockSpec((width, tile), lambda i, at: (0, i)),
            pl.BlockSpec((tile, width), lambda i, at: (i, 0)),
        ]
        + [pl.BlockSpec((a.shape[0], tile), lambda i, at: (0, i)) for a in acts]
        + [None] * len(dys),
        [column, column, None, None]
        + [pl.BlockSpec((tile, width), lambda i, at: (i, 0))] * bool(acts),
        [shape(bf16, count, hidden)] * 2
        + [shape(bf16, count, width)] * 2
        + [shape(bf16, hidden, width)] * bool(acts),
        (4 * count + 2 * sum(a.shape[0] for a in acts)) * width * hidden,
        "hidden_group",
    )


def back_kernel(at_ref, a_ref, w_ref, *outs):
    out = nt(a_ref[...], w_ref[...]).astype(bf16)
    slots = outs[0].shape[1]
    for step, ref in enumerate(outs):

        @pl.when(pl.program_id(0) == step)
        def _(ref=ref):
            ref[0] = out[:slots]
            ref[1] = out[slots:]


def back_group(at, dpre, w_in, members):
    count, hidden = dpre.shape
    width = w_in.shape[0]
    pair = count // len(members)
    return kernel_call(
        back_kernel,
        len(members),
        at,
        [dpre, w_in],
        [pl.BlockSpec((pair, hidden), lambda i, at: (i, 0)), None],
        [None] * len(members),
        [shape(bf16, 2, pair // 2, width)] * len(members),
        2 * count * width * hidden,
        "back_group",
    )


def out_kernel(at_ref, *refs, starts, order):
    acts, w_ref, outs = refs[: len(starts) - 1], refs[len(starts) - 1], refs[len(starts) :]
    slots = outs[0].shape[1]
    step = pl.program_id(0)
    for group, act_ref in enumerate(acts):
        for i in range(starts[group], starts[group + 1]):

            @pl.when(step == i)
            def _(act_ref=act_ref, ref=outs[order[i]]):
                out = nn(act_ref[...], w_ref[...]).astype(bf16)
                ref[0] = out[:slots]
                ref[1] = out[slots:]


def out_rows(at, acts, w_out, groups):
    hidden, width = w_out.shape
    pair = acts[0].shape[0] // len(groups[0])
    starts = [sum(len(g) for g in groups[:i]) for i in range(len(groups) + 1)]
    return kernel_call(
        functools.partial(out_kernel, starts=starts, order=sum(groups, [])),
        starts[-1],
        at,
        [*acts, w_out],
        [
            pl.BlockSpec(
                (pair, hidden),
                lambda i, at, a=starts[g], b=starts[g + 1]: (jnp.clip(i, a, b - 1) - a, 0),
            )
            for g in range(len(groups))
        ]
        + [None],
        [None] * starts[-1],
        [shape(bf16, 2, pair // 2, width)] * starts[-1],
        2 * starts[-1] * pair * width * hidden,
        "out_rows",
    )


def grad_weight_kernel(at_ref, *refs):
    parts = (len(refs) - 1) // 2
    total = tn(refs[0][...], refs[parts][...])
    for i in range(1, parts):
        total = total + tn(refs[i][...], refs[parts + i][...])
    refs[-1][...] = total.astype(bf16)


def grad_in_weight(at, rows, dpres):
    hidden, width = dpres[0].shape[1], rows[0].shape[1]
    tile = 768 if hidden % 768 == 0 else hidden
    return kernel_call(
        grad_weight_kernel,
        hidden // tile,
        at,
        [*rows, *dpres],
        [None] * len(rows) + [pl.BlockSpec((a.shape[0], tile), lambda i, at: (0, i)) for a in dpres],
        [pl.BlockSpec((width, tile), lambda i, at: (0, i))],
        [shape(bf16, width, hidden)],
        2 * sum(a.shape[0] for a in dpres) * width * hidden,
        "grad_in_weight",
    )[0]


def home_rows_kernel(at_ref, own_ref, came_ref, x_ref, gain_ref, back_a_ref, back_b_ref):
    rows = back_a_ref.shape[0]
    low = at_ref[LOW]
    for out_ref, place in ((back_a_ref, low), (back_b_ref, 1 - low)):
        part = aligned(place, rows)
        grad = own_ref[part, :] + came_ref[part, :].astype(f32)
        hat, rstd = norm_parts(x_ref[part, :].astype(f32))
        out_ref[...] = norm_pull(grad * gain_ref[...], hat, rstd).astype(bf16)


def tokens_kernel(at_ref, a_ref, b_ref, gm_ref, out_ref):
    rows = a_ref.shape[0]
    low = at_ref[LOW]
    for ref, place in ((a_ref, low), (b_ref, 1 - low)):
        part = aligned(place, rows)
        out_ref[part, :] = gm_ref[part, :] + ref[...].astype(f32)


def grad_shared_kernel(at_ref, normed_ref, dqkv_ref, gwo_ref, small_ref, *refs, orders):
    outs, all_ref = refs[:4], refs[4]
    blocks, part_rows, wide = all_ref.shape
    columns = dqkv_ref.shape[1]
    half = gwo_ref.shape[1]
    each = 128
    for start in range(0, columns, each * 3):
        stop = start + each * 3
        part = tn(normed_ref[...], dqkv_ref[:, start:stop])
        all_ref[:, :, start:stop] = part.reshape(blocks, part_rows, stop - start)
    all_ref[:, :, columns : columns + half] = gwo_ref[...].reshape(blocks, part_rows, half)
    all_ref[:, :, columns + half :] = small_ref[...].reshape(blocks, part_rows, wide - columns - half)
    for kk in range(2):
        for side in range(2):
            ref = outs[2 * kk + side]
            for j in range(ref.shape[0]):
                m = orders[kk][side * ref.shape[0] + j]
                for i in range(ref.shape[1]):
                    place = at_ref[FLAT] ^ ((2 * m + kk) * ref.shape[1] + i)
                    ref[j, i] = all_ref[place].astype(ref.dtype)


def final_shared_kernel(at_ref, *refs, half):
    parts, (qkv_ref, out_ref, scale_ref, shift_ref) = refs[:-4], refs[-4:]
    total = parts[0][...].astype(f32)
    for part in parts[1:]:
        total = total + part[...].astype(f32)
    norms = total[0][:, 4 * half :] + total[1][:, 4 * half :]
    row = lax.broadcasted_iota(jnp.int32, (8, norms.shape[1]), 0)
    lane = lax.broadcasted_iota(jnp.int32, (8, norms.shape[1]), 1)
    turned = lax.dot_general(
        jnp.where(row == lane, 1.0, 0.0),
        norms,
        (((1,), (1,)), ((), ())),
        precision=lax.Precision.HIGHEST,
        preferred_element_type=f32,
    )
    scale_ref[...] = turned[0:2]
    shift_ref[...] = turned[2:4]

    def fill(core):
        for mine in range(2):
            which = core ^ mine
            for group in range(3):
                start = (2 * group + which) * half
                qkv_ref[:, start : start + half] = total[mine][:, group * half : (group + 1) * half]
            out_ref[:, which * half : (which + 1) * half] = total[mine][:, 3 * half : 4 * half]

    pl.when(at_ref[CORE] == 0)(lambda: fill(0))
    pl.when(at_ref[CORE] == 1)(lambda: fill(1))


def make_local(exp_size, seq_size):
    cols = exp_size // 2
    col_bits = cols.bit_length() - 1
    near = [m for m in range(1, cols) if m & (m - 1) == 0]
    far = [m for m in range(1, cols) if m & (m - 1)]
    groups = [[0], near, far]

    def flat_perm(target):
        pairs = []
        for exp in range(exp_size):
            for seq in range(seq_size):
                col, core = exp >> 1, exp & 1
                new_col, new_core, new_seq = target(col, core, seq)
                pairs.append((exp * seq_size + seq, (new_col * 2 + new_core) * seq_size + new_seq))
        return pairs

    def send(array, target):
        return lax.ppermute(array, BOTH, flat_perm(target))

    def to_core(array):
        return send(array, lambda c, k, z: (c, 1 - k, z))

    def to_seq(array, shift):
        return send(array, lambda c, k, z: (c, k, z ^ shift))

    def to_col(array, bit):
        return send(array, lambda c, k, z: (c ^ (1 << bit), k, z))

    def exchange(pairs):
        came = exchange_near(pairs)
        return exchange_far(pairs, came)

    def chip_send(m, pair):
        return send(pair, lambda c, k, z: (c ^ m, k, z))

    def exchange_near(pairs):
        return {0: pairs[0], **{m: chip_send(m, pairs[m]) for m in near}}

    def exchange_far(pairs, came):
        waits = [came[m] for m in near]
        rest = {m: chip_send(m, after(pairs[m], waits)) for m in far}
        return [rest[m] if m in rest else came[m] for m in range(cols)]

    def with_other(pairs):
        return [part for pair in pairs for part in (pair, to_core(pair))]

    def home_of(i):
        return lambda c, k, z: (c, z >> 1, (2 * k + (z & 1)) ^ i)

    def worker_of(i):
        return lambda c, k, z: (c, (z ^ i) >> 1, 2 * k + ((z ^ i) & 1))

    def step_bits(kk):
        return list(range(col_bits))[:: 1 - 2 * kk]

    def local(
        tokens,
        cotangent,
        token_ids,
        segments,
        hash_table,
        w_qkv,
        w_attn_out,
        norm_scale,
        norm_shift,
        w_in,
        w_out,
    ):
        seq_dev, rows_seq, width = tokens.shape
        rows = seq_dev * rows_seq
        slot_rows = 3 * rows // exp_size
        full_len = rows_seq * seq_size
        half = width // 2
        wide = 4 * half + LANES
        part_rows = w_qkv.shape[0]
        blocks = seq_size * 2 * cols
        w_in, w_out = w_in[0], w_out[0]
        exp_at = lax.axis_index("exp")
        z = lax.axis_index("seq")
        k = exp_at & 1
        is_one = k == 1
        z0 = z & 1
        at = jnp.stack([k, exp_at * seq_size + z, z0, z, exp_at, 2 * k + z0]).astype(jnp.int32)

        norms = jnp.concatenate([norm_scale, norm_shift], axis=1)
        norms = jnp.pad(norms, ((0, 0), (0, LANES - norms.shape[1])))
        pack = jnp.concatenate([w_qkv, w_attn_out, norms], axis=1)
        got = [pack] + [to_seq(pack, i) for i in range(1, seq_size)]
        seg_pair = jnp.where((z >> 1) == k, segments, to_core(segments))
        seg_row = jnp.where(z0 == 1, seg_pair[1:2], seg_pair[0:1])

        expert = hash_table[token_ids.reshape(-1)]
        order = jnp.arange(rows, dtype=jnp.int32)
        earlier = (expert[None, :] == expert[:, None]) & (order[None, :] < order[:, None])
        slot_rank = jnp.sum(earlier.astype(jnp.int32), axis=1)
        slots = exp_size * slot_rows
        slot_index = expert * slot_rows + slot_rank
        slot_near = (expert ^ exp_at) * slot_rows + slot_rank
        spread = (jnp.arange(slots, dtype=jnp.int32)[:, None] == slot_index[None, :]).astype(bf16)

        def swap(array):
            return lax.all_to_all(
                array.reshape(exp_size, slot_rows, width),
                "exp",
                split_axis=0,
                concat_axis=0,
                tiled=True,
            )

        grad_low = cotangent.reshape(rows, width)
        grad_packed = nn(spread, grad_low).astype(bf16)
        got, _ = lax.optimization_barrier((got, (grad_packed, slot_near, seg_row)))
        mine, other = single_call(
            functools.partial(split_kernel, half=half, parts=seq_size),
            at,
            got,
            [shape(bf16, seq_size, part_rows, wide)] * 2,
            "split_cores",
        )
        pair = [jnp.where(z0 == 1, tokens[1 - i], tokens[i]) for i in range(2)]
        here = [send(pair[0], home_of(0)), send(pair[1], home_of(1))]
        x_half = jnp.concatenate(
            [jnp.where(z0 == 1, here[1 - i], here[i]) for i in range(2)], axis=0
        )
        pieces = [[mine], [to_core(other)]]
        x_other = None
        for step in range(col_bits):
            if step == 1:
                pieces, x_half = lax.optimization_barrier((pieces, x_half))
                x_other = to_core(x_half)
            pieces = [
                own + [to_col(piece, step_bits(kk)[step]) for piece in own]
                for kk, own in enumerate(pieces)
            ]
        ordered = []
        for kk in range(2):
            bits = step_bits(kk)
            by_place = {}
            for index, piece in enumerate(pieces[kk]):
                place = sum(1 << bits[step] for step in range(col_bits) if (index >> step) & 1)
                by_place[place] = piece
            ordered += [by_place[place] for place in range(cols)]
        wq, wo_own, norm_rows, hat, normed, qkv = single_call(
            functools.partial(norm_qkv_kernel, half=half, parts=seq_size, cols=cols),
            at,
            [*ordered, x_half, x_other],
            [
                shape(bf16, blocks, part_rows, 3 * half),
                shape(bf16, blocks, part_rows, half),
                shape(f32, 8, width),
                shape(bf16, full_len, width),
                shape(bf16, full_len, width),
                shape(bf16, full_len, 3 * half),
            ],
            "norm_qkv",
            flops=2 * full_len * width * 3 * half,
            scratch=[pltpu.VMEM((blocks, part_rows, LANES), f32)],
        )
        wq = wq.reshape(width, 3 * half)
        wo_own = wo_own.reshape(width, half)
        gain_one, gain_two, bias_two = norm_rows[0:1], norm_rows[1:2], norm_rows[3:4]
        grad_arrived = swap(after(grad_packed, qkv))
        att, lse, *chunks = attend(at, qkv, seg_row, seq_size)
        wo_other = to_core(wo_own)
        wo = jnp.concatenate(
            [jnp.where(is_one, wo_other, wo_own), jnp.where(is_one, wo_own, wo_other)], axis=1
        )
        quads = [send(chunks[i], home_of(i)) for i in range(seq_size)]
        quads, grad_arrived = lax.optimization_barrier((quads, grad_arrived))
        x_home = tokens.reshape(rows, width)
        att_home, middle, *packs = single_call(
            mix_kernel,
            at,
            [*quads, x_home, wo, gain_two, bias_two, slot_near[None, :]],
            [shape(bf16, rows, width), shape(f32, rows, width)]
            + [shape(bf16, 2, slot_rows, width)] * cols,
            "mix",
            flops=2 * rows * width * (width + slots),
        )

        arrived = exchange(packs)
        hidden = []
        for members in groups:
            pairs = [arrived[m] for m in members]
            if hidden:
                pairs = after(pairs, hidden[-1])
            earlier = hidden if len(hidden) == 2 else ()
            hidden.append(
                hidden_group(
                    at, with_other(pairs), grad_arrived, members, w_in, w_out, earlier
                )
            )
        grad_outer = hidden[2][4]
        hidden[2] = hidden[2][:4]
        acts, dpres, sents, grads = zip(*hidden)
        grad_w_out = lax.psum_scatter(grad_outer, "seq", scatter_dimension=0, tiled=True)
        dpres = after(dpres, grad_outer)
        grad_sents = {}
        for i in (1, 2, 0):
            parts = back_group(at, dpres[i], w_in, groups[i])
            grad_sents.update(zip(groups[i], parts))
            dpres = after(dpres, parts)
        grad_back = exchange([grad_sents[m] for m in range(cols)])
        expert_out = out_rows(at, after(acts, dpres), w_out, groups)
        grad_back = with_other(after(grad_back, expert_out))
        expert_out = after(expert_out, grad_back)
        returned_near = exchange_near(expert_out)

        outs = [
            *(shape(f32, rows, width), shape(bf16, rows, width), shape(f32, 8, width)),
            *[shape(bf16, rows_seq, half)] * seq_size,
        ]
        grad_middle, grad_branch, sums_two, *quads = kernel_call(
            functools.partial(mid_back_kernel, owners=exp_size),
            1,
            at,
            [*grad_back, middle, grad_low, wo, gain_two, slot_near[:, None]],
            pair_specs(exp_size, slot_rows, width) + [None] * 5,
            [None] * len(outs),
            outs,
            2 * rows * width * (width + slots),
            "mid_back",
            [pltpu.VMEM((slots, width), bf16), pltpu.VMEM((rows, width), bf16)],
        )

        quads, returned_near = lax.optimization_barrier((quads, returned_near))
        came = [send(quads[i], worker_of(i)) for i in range(seq_size)]
        returned = exchange_far(expert_out, returned_near)
        grad_inner = grad_in_weight(at, sents, after(dpres, quads))
        grad_w_in = lax.psum_scatter(
            after(grad_inner, came), "seq", scatter_dimension=1, tiled=True
        )
        grad_wo = tn(att_home, grad_branch)
        wo_halves = [grad_wo[:, :half], grad_wo[:, half:]]
        grad_wo = jnp.where(is_one, wo_halves[1], wo_halves[0]) + to_core(
            jnp.where(is_one, wo_halves[0], wo_halves[1]).astype(bf16)
        ).astype(f32)
        came = after(came, grad_wo)
        dqkv, own, other, sums_one = attend_back(at, qkv, att, lse, seg_row, hat, came, wq)
        other = to_core(other)
        small = jnp.stack([sums_one[0], sums_two[0], sums_one[1], sums_two[1]])
        small = jnp.pad(small, ((0, LANES - 4), (0, 0))).T
        orders = [
            sorted(range(cols), key=lambda m, kk=kk: [(m >> bit) & 1 for bit in step_bits(kk)])
            for kk in range(2)
        ]
        stay_go = single_call(
            functools.partial(grad_shared_kernel, orders=orders),
            at,
            [normed, dqkv, grad_wo, small],
            [shape(bf16, cols // 2, seq_size, part_rows, wide)] * 4,
            "grad_shared",
            flops=2 * full_len * width * 3 * half,
            scratch=[pltpu.VMEM((blocks, part_rows, wide), f32)],
        )
        returned = with_other(returned)
        stay_go, returned = lax.optimization_barrier((stay_go, returned))
        wide_w_out = grad_w_out.astype(f32)[None]
        sums = []
        for kk in range(2):
            stay, go = stay_go[2 * kk], stay_go[2 * kk + 1]
            for step in range(col_bits):
                came = to_col(go, step_bits(kk)[step])
                if step == 0:
                    came = after(came, wide_w_out)
                both = stay.astype(f32) + came.astype(f32)
                if step + 1 < col_bits:
                    count = both.shape[0] // 2
                    stay, go = both[:count], both[count:].astype(bf16)
            sums.append(both[0])
        lined = jnp.stack([sums[0].astype(bf16), to_core(sums[1].astype(bf16))], axis=1)
        own_late, lined = lax.optimization_barrier((own, lined))
        parts = [lined[0]] + [to_seq(lined[i], i) for i in range(1, seq_size)]
        back_a, back_b = single_call(
            home_rows_kernel,
            at,
            [own_late, other, x_half, gain_one],
            [shape(bf16, rows_seq, width)] * 2,
            "home_rows",
        )
        layer_out = kernel_call(
            functools.partial(layer_out_kernel, owners=exp_size),
            1,
            at,
            [*returned, middle, slot_near[:, None]],
            pair_specs(exp_size, slot_rows, width) + [None, None],
            [None],
            [shape(bf16, rows, width)],
            2 * rows * width * slots,
            "layer_out",
            [pltpu.VMEM((slots, width), bf16)],
        )[0]
        wide_w_in = grad_w_in.astype(f32)[None]
        (grad_tokens,) = single_call(
            tokens_kernel,
            at,
            [
                *[send(part, home_of(i)) for i, part in enumerate((back_a, back_b))],
                after(grad_middle, wide_w_in),
            ],
            [shape(f32, rows, width)],
            "tokens",
        )

        grad_w_qkv, grad_w_attn_out, grad_norm_scale, grad_norm_shift = single_call(
            functools.partial(final_shared_kernel, half=half),
            at,
            parts,
            [
                shape(f32, part_rows, 6 * half),
                shape(f32, part_rows, 2 * half),
                shape(f32, 2, part_rows),
                shape(f32, 2, part_rows),
            ],
            "final_shared",
        )
        return (
            layer_out.reshape(seq_dev, rows_seq, width),
            grad_tokens.reshape(seq_dev, rows_seq, width),
            grad_w_qkv,
            grad_w_attn_out,
            grad_norm_scale.T,
            grad_norm_shift.T,
            wide_w_in,
            wide_w_out,
        )

    return local


def solution(mesh):
    return jax.shard_map(
        make_local(mesh.shape["exp"], mesh.shape["seq"]),
        mesh=mesh,
        in_specs=(
            P("exp", "seq", None),
            P("exp", "seq", None),
            P("exp", "seq"),
            P("exp", None),
            P(),
            P(("exp", "seq"), None),
            P(("exp", "seq"), None),
            P(("exp", "seq"), None),
            P(("exp", "seq"), None),
            P("exp", None, None),
            P("exp", None, None),
        ),
        out_specs=(
            P("exp", "seq", None),
            P("exp", "seq", None),
            P(("exp", "seq"), None),
            P(("exp", "seq"), None),
            P(("exp", "seq"), None),
            P(("exp", "seq"), None),
            P("exp", None, "seq"),
            P("exp", "seq", None),
        ),
        check_vma=False,
    )
```

```python
import functools

import jax
import jax.numpy as jnp
from jax import lax
from jax.experimental import pallas as pl
from jax.experimental.pallas import tpu as pltpu
from jax.sharding import PartitionSpec as P

HEAD_DIM = 64
LANES = 128
BOTH = ("exp", "seq")
epsilon = 1e-05
f32 = jnp.float32
bf16 = jnp.bfloat16


def norm_parts(feature):
    center = feature - jnp.mean(feature, axis=-1, keepdims=True)
    spread = jnp.mean(center * center, axis=-1, keepdims=True)
    rstd = lax.rsqrt(spread + epsilon)
    return center * rstd, rstd


def norm_pull(grad_hat, hat, rstd):
    first = jnp.mean(grad_hat, axis=-1, keepdims=True)
    second = jnp.mean(grad_hat * hat, axis=-1, keepdims=True)
    return rstd * (grad_hat - first - hat * second)


def nt(a, b):
    return lax.dot_general(a, b, (((1,), (1,)), ((), ())), preferred_element_type=f32)


def nn(a, b):
    return lax.dot_general(a, b, (((1,), (0,)), ((), ())), preferred_element_type=f32)


def tn(a, b):
    return lax.dot_general(a, b, (((0,), (0,)), ((), ())), preferred_element_type=f32)


def after(value, *earlier):
    return lax.optimization_barrier((value, earlier))[0]


def aligned(index, size, unit=None):
    return pl.ds(pl.multiple_of(index * size, unit or size), size)


def whole_block(*shape):
    return pl.BlockSpec(shape, lambda i, at: (0,) * len(shape))


def kernel_call(body, steps, at, arrays, in_specs, out_specs, out_shape, flops, name, scratch=()):
    in_specs = [spec or whole_block(*a.shape) for spec, a in zip(in_specs, arrays)]
    out_specs = [spec or whole_block(*o.shape) for spec, o in zip(out_specs, out_shape)]
    moved = sum(a.size * a.dtype.itemsize for a in (*arrays, *out_shape))
    return pl.pallas_call(
        body,
        grid_spec=pltpu.PrefetchScalarGridSpec(
            num_scalar_prefetch=1,
            grid=(steps,),
            in_specs=in_specs,
            out_specs=out_specs,
            scratch_shapes=list(scratch),
        ),
        out_shape=list(out_shape),
        compiler_params=pltpu.CompilerParams(vmem_limit_bytes=56 << 20),
        cost_estimate=pl.CostEstimate(flops=flops, bytes_accessed=moved, transcendentals=0),
        name=name,
    )(at, *arrays)


def single_call(body, at, arrays, out_shape, name, flops=0, scratch=()):
    return kernel_call(
        body,
        1,
        at,
        arrays,
        [None] * len(arrays),
        [None] * len(out_shape),
        out_shape,
        flops,
        name,
        scratch,
    )


def shape(kind, *dims):
    return jax.ShapeDtypeStruct(dims, kind)


CORE, FLAT, LOW, SEQ, EXP, CHUNK = range(6)


def key_segments(segr_ref):
    rows = jnp.broadcast_to(segr_ref[...].astype(f32), (8, segr_ref.shape[1]))
    return rows.T[:, 0:1]


def allowed_keys(seg_keys, segr_ref, start, block):
    row = segr_ref[:, start : start + block].astype(f32)
    keys = lax.broadcasted_iota(jnp.int32, (block, block), 0)
    queries = lax.broadcasted_iota(jnp.int32, (block, block), 1)
    own = (seg_keys[start : start + block] == row) & (keys <= queries)
    return (seg_keys[0:start] == row, own) if start else (own,)


def masked(values, allowed, fill):
    if len(allowed) == 1:
        return jnp.where(allowed[0], values, fill)
    start = allowed[0].shape[0]
    parts = (values[:start], values[start:])
    return jnp.concatenate([jnp.where(a, v, fill) for a, v in zip(allowed, parts)], axis=0)


def split_kernel(at_ref, *refs, half, parts):
    got, (mine_ref, other_ref) = refs[:parts], refs[parts:]

    def fill(core):
        for i in range(parts):
            for ref, which in ((mine_ref, core), (other_ref, 1 - core)):
                for group in range(4):
                    start = (2 * group + which) * half
                    ref[i, :, group * half : (group + 1) * half] = got[i][:, start : start + half]
                ref[i, :, 4 * half :] = got[i][:, 8 * half :]

    pl.when(at_ref[CORE] == 0)(lambda: fill(0))
    pl.when(at_ref[CORE] == 1)(lambda: fill(1))


def norm_qkv_kernel(at_ref, *refs, half, parts, cols):
    pieces, (own_ref, other_ref) = refs[: 2 * cols], refs[2 * cols : 2 * cols + 2]
    wq_ref, wo_ref, rows_ref, hat_ref, normed_ref, qkv_ref, norm_ref = refs[2 * cols + 2 :]
    for kk in range(2):
        for m in range(cols):
            for i in range(parts):
                place = at_ref[FLAT] ^ ((2 * m + kk) * parts + i)
                block = pieces[kk * cols + m]
                wq_ref[place] = block[i, :, : 3 * half]
                wo_ref[place] = block[i, :, 3 * half : 4 * half]
                norm_ref[place] = block[i, :, 4 * half :].astype(f32)
    width = own_ref.shape[1]
    norm_rows = norm_ref[...].reshape(width, LANES).T[0:8]
    rows_ref[...] = norm_rows
    weights = wq_ref[...].reshape(width, 3 * half)
    rows = own_ref.shape[0]
    core = at_ref[CORE]
    for ref, place in ((own_ref, core), (other_ref, 1 - core)):
        hat, _ = norm_parts(ref[...].astype(f32))
        normed = (hat * norm_rows[0:1] + norm_rows[2:3]).astype(bf16)
        where = aligned(place, rows)
        hat_ref[where, :] = hat.astype(bf16)
        normed_ref[where, :] = normed
        qkv_ref[where, :] = nn(normed, weights).astype(bf16)


GELU_ONE = 0.7978845608028654
GELU_TWO = GELU_ONE * 0.044715


def attend_kernel(at_ref, q_ref, k_ref, v_ref, segr_ref, att_ref, lse_ref, *outs_ref, block):
    total = q_ref.shape[0]
    seg_keys = key_segments(segr_ref)
    values_t = v_ref[...].astype(f32).T.astype(bf16)
    lane = lax.broadcasted_iota(jnp.int32, (block, LANES), 1)
    for start in range(0, total, block):
        width = start + block
        allowed = allowed_keys(seg_keys, segr_ref, start, block)
        queries = q_ref[start:width, :] * 0.125
        outs = []
        for head in range(2):
            own = (lane >= HEAD_DIM) if head else (lane < HEAD_DIM)
            q_head = jnp.where(own, queries, 0.0).astype(bf16)
            scores = masked(nt(k_ref[0:width, :], q_head), allowed, -1e30)
            top = jnp.max(scores, axis=0, keepdims=True)
            expo = jnp.exp(scores - top)
            total_row = jnp.sum(expo, axis=0, keepdims=True)
            out = nn(values_t[head * HEAD_DIM : (head + 1) * HEAD_DIM, 0:width], expo.astype(bf16))
            outs.append(out / total_row)
            lse_ref[0, head : head + 1, start:width] = top + jnp.log(total_row)
        att_ref[start:width, :] = jnp.concatenate(outs, axis=0).T.astype(bf16)
    rows = outs_ref[0].shape[0]
    for i, ref in enumerate(outs_ref):
        ref[...] = att_ref[aligned(at_ref[CHUNK] ^ i, rows), :]


def head_specs(total, pairs):
    return [
        pl.BlockSpec((total, LANES), lambda h, at, part=part: (0, part * pairs + h))
        for part in range(3)
    ]


def attend(at, qkv, seg_row, chunks):
    total, width = qkv.shape
    pairs = width // 3 // LANES
    rows = total // chunks
    piece = pl.BlockSpec((rows, LANES), lambda h, at: (0, h))
    return kernel_call(
        functools.partial(attend_kernel, block=min(512, total)),
        pairs,
        at,
        [qkv, qkv, qkv, seg_row],
        head_specs(total, pairs) + [None],
        [
            pl.BlockSpec((total, LANES), lambda h, at: (0, h)),
            pl.BlockSpec((1, 8, total), lambda h, at: (h, 0, 0)),
        ]
        + [piece] * chunks,
        [shape(bf16, total, pairs * LANES), shape(f32, pairs, 8, total)]
        + [shape(bf16, rows, pairs * LANES)] * chunks,
        4 * total * total * width // 6,
        "attend",
    )


def attend_back_kernel(
    at_ref, q_ref, k_ref, v_ref, att_ref, lse_ref, segr_ref, hat_ref, *refs, block, chunks
):
    came, (wq_ref, wk_ref, wv_ref) = refs[:chunks], refs[chunks : chunks + 3]
    out_ref, own_ref, other_ref, sums_ref, dk_ref, dv_ref, datt_ref, sum_ref = refs[chunks + 3 :]
    total = q_ref.shape[0]
    pairs = pl.num_programs(0)
    pair = pl.program_id(0)
    for i, ref in enumerate(came):
        datt_ref[aligned(at_ref[CHUNK] ^ i, total // chunks), :] = ref[...]
    lane = lax.broadcasted_iota(jnp.int32, (block, LANES), 1)
    lane_all = lax.broadcasted_iota(jnp.int32, (total, LANES), 1)
    dk_ref[...] = jnp.zeros_like(dk_ref)
    dv_ref[...] = jnp.zeros_like(dv_ref)
    seg_keys = key_segments(segr_ref)
    row8 = lax.broadcasted_iota(jnp.int32, (8, LANES), 0)
    lane8 = lax.broadcasted_iota(jnp.int32, (8, LANES), 1)
    head_rows = jnp.where(row8 == lane8 // HEAD_DIM, 1.0, 0.0)

    for start in range(0, total, block):
        width = start + block
        allowed = allowed_keys(seg_keys, segr_ref, start, block)
        queries = q_ref[start:width, :] * 0.125
        grads = datt_ref[start:width, :]
        product = grads.astype(f32) * att_ref[start:width, :].astype(f32)
        delta = lax.dot_general(
            head_rows,
            product,
            (((1,), (1,)), ((), ())),
            precision=lax.Precision.HIGHEST,
            preferred_element_type=f32,
        )
        dq = jnp.zeros((block, LANES), f32)
        for head in range(2):
            own = (lane >= HEAD_DIM) if head else (lane < HEAD_DIM)
            own_all = (lane_all >= HEAD_DIM) if head else (lane_all < HEAD_DIM)
            q_head = jnp.where(own, queries, 0.0).astype(bf16)
            g_head = jnp.where(own, grads, 0.0).astype(bf16)
            k_head = jnp.where(own_all[0:width], k_ref[0:width, :], 0.0).astype(bf16)
            scores = nt(k_ref[0:width, :], q_head)
            probs = masked(jnp.exp(scores - lse_ref[0, head : head + 1, start:width]), allowed, 0.0)
            dprobs = nt(v_ref[0:width, :], g_head)
            dscores = (probs * (dprobs - delta[head : head + 1, :])).astype(bf16)
            dv_ref[0:width, :] += nn(probs.astype(bf16), g_head)
            dk_ref[0:width, :] += nn(dscores, q_head)
            dq = dq + tn(dscores, k_head)
        out_ref[start:width, aligned(pair, LANES)] = (dq * 0.125).astype(bf16)
    dk = dk_ref[...].astype(bf16)
    dv = dv_ref[...].astype(bf16)
    out_ref[:, aligned(pairs + pair, LANES)] = dk
    out_ref[:, aligned(2 * pairs + pair, LANES)] = dv
    grads = jnp.concatenate([out_ref[:, aligned(pair, LANES)], dk, dv], axis=1)
    weights = jnp.concatenate([wq_ref[...], wk_ref[...], wv_ref[...]], axis=1)
    pulled = nt(grads, weights)

    @pl.when(pair == 0)
    def _():
        sum_ref[...] = pulled

    @pl.when(pair > 0)
    def _():
        sum_ref[...] += pulled

    @pl.when(pair == pairs - 1)
    def _():
        rows = own_ref.shape[0]
        core = at_ref[CORE]
        own_ref[...] = sum_ref[aligned(core, rows), :]
        other_ref[...] = sum_ref[aligned(1 - core, rows), :].astype(bf16)
        sums_ref[0:1, :] = jnp.sum(sum_ref[...] * hat_ref[...].astype(f32), axis=0, keepdims=True)
        sums_ref[1:2, :] = jnp.sum(sum_ref[...], axis=0, keepdims=True)


def attend_back(at, qkv, att, lse, seg_row, hat, came, wq):
    total, width = qkv.shape
    model = wq.shape[0]
    pairs = width // 3 // LANES
    chunks = len(came)
    return kernel_call(
        functools.partial(attend_back_kernel, block=min(256, total), chunks=chunks),
        pairs,
        at,
        [qkv, qkv, qkv, att, lse, seg_row, hat, *came, wq, wq, wq],
        head_specs(total, pairs)
        + [
            pl.BlockSpec((total, LANES), lambda h, at: (0, h)),
            pl.BlockSpec((1, 8, total), lambda h, at: (h, 0, 0)),
            None,
            None,
        ]
        + [pl.BlockSpec((total // chunks, LANES), lambda h, at: (0, h))] * chunks
        + head_specs(model, pairs),
        [None] * 4,
        [
            shape(bf16, total, width),
            shape(f32, total // 2, model),
            shape(bf16, total // 2, model),
            shape(f32, 8, model),
        ],
        10 * total * total * width // 6,
        "attend_back",
        [
            pltpu.VMEM((total, LANES), f32),
            pltpu.VMEM((total, LANES), f32),
            pltpu.VMEM((total, LANES), bf16),
            pltpu.VMEM((total, model), f32),
        ],
    )


def mix_kernel(at_ref, q0, q1, q2, q3, x_ref, wo_ref, gain_ref, bias_ref, slot_ref, att_ref, mid_ref, *packs):
    rows, half = q0.shape
    for i, quad in enumerate((q0, q1, q2, q3)):
        place = at_ref[SEQ] ^ i
        att_ref[aligned(place & 1, rows), aligned(place >> 1, half, LANES)] = quad[...]
    middle = x_ref[...].astype(f32) + nn(att_ref[...], wo_ref[...])
    mid_ref[...] = middle
    hat, _ = norm_parts(middle)
    sent = (hat * gain_ref[...] + bias_ref[...]).astype(bf16)
    slots = packs[0].shape[1]
    for m, pack in enumerate(packs):
        place = lax.broadcasted_iota(jnp.int32, (2 * slots, sent.shape[0]), 0) + 2 * m * slots
        spread = jnp.where(place == slot_ref[...], 1.0, 0.0).astype(bf16)
        rows_out = nn(spread, sent).astype(bf16)
        pack[0] = rows_out[:slots]
        pack[1] = rows_out[slots:]


def mid_back_kernel(at_ref, *refs, owners):
    backs = refs[:owners]
    mid_ref, dy_ref, wo_ref, gain_ref, slot_ref = refs[owners : owners + 5]
    gm_ref, branch_ref, sums_ref, q0, q1, q2, q3, all_ref, datt_ref = refs[owners + 5 :]
    slots = backs[0].shape[1]
    for b, back in enumerate(backs):
        all_ref[b * slots : (b + 1) * slots, :] = back[0]
    count = mid_ref.shape[0]
    place = lax.broadcasted_iota(jnp.int32, (count, owners * slots), 1)
    spread = jnp.where(place == slot_ref[...], 1.0, 0.0).astype(bf16)
    grad = nn(spread, all_ref[...])
    hat, rstd = norm_parts(mid_ref[...])
    sums_ref[0:1, :] = jnp.sum(grad * hat, axis=0, keepdims=True)
    sums_ref[1:2, :] = jnp.sum(grad, axis=0, keepdims=True)
    grad_middle = dy_ref[...].astype(f32) + norm_pull(grad * gain_ref[...], hat, rstd)
    gm_ref[...] = grad_middle
    branch = grad_middle.astype(bf16)
    branch_ref[...] = branch
    datt_ref[...] = nt(branch, wo_ref[...]).astype(bf16)
    rows, half = q0.shape
    for i, quad in enumerate((q0, q1, q2, q3)):
        at = at_ref[SEQ] ^ i
        quad[...] = datt_ref[aligned(at & 1, rows), aligned(at >> 1, half, LANES)]


def layer_out_kernel(at_ref, *refs, owners):
    backs, (mid_ref, slot_ref, out_ref, all_ref) = refs[:owners], refs[owners:]
    slots = backs[0].shape[1]
    for b, back in enumerate(backs):
        all_ref[b * slots : (b + 1) * slots, :] = back[0]
    place = lax.broadcasted_iota(jnp.int32, (mid_ref.shape[0], owners * slots), 1)
    spread = jnp.where(place == slot_ref[...], 1.0, 0.0).astype(bf16)
    out_ref[...] = (mid_ref[...] + nn(spread, all_ref[...])).astype(bf16)


def hidden_kernel(at_ref, *refs, blocks, chunk, earlier):
    rows, grads = refs[:blocks], refs[blocks : 2 * blocks]
    in_ref, out_ref, *refs = refs[2 * blocks :]
    acts, dys, refs = refs[:earlier], refs[earlier : 2 * earlier], refs[2 * earlier :]
    act_ref, dpre_ref, x_ref, d_ref = refs[:4]
    slots = rows[0].shape[1]

    @pl.when(pl.program_id(0) == 0)
    def _():
        for b in range(blocks):
            x_ref[b * slots : (b + 1) * slots, :] = rows[b][0]
            d_ref[b * slots : (b + 1) * slots, :] = grads[b][0]

    for start in range(0, x_ref.shape[0], chunk):
        part = slice(start, start + chunk)
        pre = nn(x_ref[part, :], in_ref[...])
        dact = nt(d_ref[part, :], out_ref[...])
        square = pre * pre
        gate = 0.5 * jnp.tanh(pre * (GELU_ONE + GELU_TWO * square)) + 0.5
        act = pre * gate
        slope = gate + act * (1.0 - gate) * (2 * GELU_ONE + 6 * GELU_TWO * square)
        act_ref[part, :] = act.astype(bf16)
        dpre_ref[part, :] = (dact * slope).astype(bf16)
    if earlier:
        total = tn(act_ref[...], d_ref[...])
        for other_act, other_dy in zip(acts, dys):
            total = total + tn(other_act[...], other_dy[...])
        refs[4][...] = total.astype(bf16)


def pair_specs(blocks, slots, width):
    return [
        pl.BlockSpec((1, slots, width), lambda i, at, b=b: (b % 2, 0, 0)) for b in range(blocks)
    ]


def hidden_group(at, rows, grads, members, w_in, w_out, earlier=()):
    acts, dys = [g[0] for g in earlier], [g[3] for g in earlier]
    blocks = len(rows)
    _, slots, width = rows[0].shape
    count = blocks * slots
    hidden = w_in.shape[1]
    tile = next((size for size in (512 if earlier else 768, 768) if hidden % size == 0), hidden)
    chunk = next((size for size in (768, 384) if count % size == 0), count)
    column = pl.BlockSpec((count, tile), lambda i, at: (0, i))
    places = [2 * m + kk for m in members for kk in range(2)]
    return kernel_call(
        functools.partial(hidden_kernel, blocks=blocks, chunk=chunk, earlier=len(acts)),
        hidden // tile,
        at,
        [*rows, *([grads] * blocks), w_in, w_out, *acts, *dys],
        pair_specs(blocks, slots, width)
        + [pl.BlockSpec((1, slots, width), lambda i, at, b=b: (b ^ at[EXP], 0, 0)) for b in places]
        + [
            pl.BlockSpec((width, tile), lambda i, at: (0, i)),
            pl.BlockSpec((tile, width), lambda i, at: (i, 0)),
        ]
        + [pl.BlockSpec((a.shape[0], tile), lambda i, at: (0, i)) for a in acts]
        + [None] * len(dys),
        [column, column, None, None]
        + [pl.BlockSpec((tile, width), lambda i, at: (i, 0))] * bool(acts),
        [shape(bf16, count, hidden)] * 2
        + [shape(bf16, count, width)] * 2
        + [shape(bf16, hidden, width)] * bool(acts),
        (4 * count + 2 * sum(a.shape[0] for a in acts)) * width * hidden,
        "hidden_group",
    )


def back_kernel(at_ref, a_ref, w_ref, *outs):
    out = nt(a_ref[...], w_ref[...]).astype(bf16)
    slots = outs[0].shape[1]
    for step, ref in enumerate(outs):

        @pl.when(pl.program_id(0) == step)
        def _(ref=ref):
            ref[0] = out[:slots]
            ref[1] = out[slots:]


def back_group(at, dpre, w_in, members):
    count, hidden = dpre.shape
    width = w_in.shape[0]
    pair = count // len(members)
    return kernel_call(
        back_kernel,
        len(members),
        at,
        [dpre, w_in],
        [pl.BlockSpec((pair, hidden), lambda i, at: (i, 0)), None],
        [None] * len(members),
        [shape(bf16, 2, pair // 2, width)] * len(members),
        2 * count * width * hidden,
        "back_group",
    )


def out_kernel(at_ref, *refs, starts, order):
    acts, w_ref, outs = refs[: len(starts) - 1], refs[len(starts) - 1], refs[len(starts) :]
    slots = outs[0].shape[1]
    step = pl.program_id(0)
    for group, act_ref in enumerate(acts):
        for i in range(starts[group], starts[group + 1]):

            @pl.when(step == i)
            def _(act_ref=act_ref, ref=outs[order[i]]):
                out = nn(act_ref[...], w_ref[...]).astype(bf16)
                ref[0] = out[:slots]
                ref[1] = out[slots:]


def out_rows(at, acts, w_out, groups):
    hidden, width = w_out.shape
    pair = acts[0].shape[0] // len(groups[0])
    starts = [sum(len(g) for g in groups[:i]) for i in range(len(groups) + 1)]
    return kernel_call(
        functools.partial(out_kernel, starts=starts, order=sum(groups, [])),
        starts[-1],
        at,
        [*acts, w_out],
        [
            pl.BlockSpec(
                (pair, hidden),
                lambda i, at, a=starts[g], b=starts[g + 1]: (jnp.clip(i, a, b - 1) - a, 0),
            )
            for g in range(len(groups))
        ]
        + [None],
        [None] * starts[-1],
        [shape(bf16, 2, pair // 2, width)] * starts[-1],
        2 * starts[-1] * pair * width * hidden,
        "out_rows",
    )


def grad_weight_kernel(at_ref, *refs):
    parts = (len(refs) - 1) // 2
    total = tn(refs[0][...], refs[parts][...])
    for i in range(1, parts):
        total = total + tn(refs[i][...], refs[parts + i][...])
    refs[-1][...] = total.astype(bf16)


def grad_in_weight(at, rows, dpres):
    hidden, width = dpres[0].shape[1], rows[0].shape[1]
    tile = 768 if hidden % 768 == 0 else hidden
    return kernel_call(
        grad_weight_kernel,
        hidden // tile,
        at,
        [*rows, *dpres],
        [None] * len(rows) + [pl.BlockSpec((a.shape[0], tile), lambda i, at: (0, i)) for a in dpres],
        [pl.BlockSpec((width, tile), lambda i, at: (0, i))],
        [shape(bf16, width, hidden)],
        2 * sum(a.shape[0] for a in dpres) * width * hidden,
        "grad_in_weight",
    )[0]


def home_rows_kernel(at_ref, own_ref, came_ref, x_ref, gain_ref, back_a_ref, back_b_ref):
    rows = back_a_ref.shape[0]
    low = at_ref[LOW]
    for out_ref, place in ((back_a_ref, low), (back_b_ref, 1 - low)):
        part = aligned(place, rows)
        grad = own_ref[part, :] + came_ref[part, :].astype(f32)
        hat, rstd = norm_parts(x_ref[part, :].astype(f32))
        out_ref[...] = norm_pull(grad * gain_ref[...], hat, rstd).astype(bf16)


def tokens_kernel(at_ref, a_ref, b_ref, gm_ref, out_ref):
    rows = a_ref.shape[0]
    low = at_ref[LOW]
    for ref, place in ((a_ref, low), (b_ref, 1 - low)):
        part = aligned(place, rows)
        out_ref[part, :] = gm_ref[part, :] + ref[...].astype(f32)


def grad_shared_kernel(at_ref, normed_ref, dqkv_ref, gwo_ref, small_ref, *refs, orders):
    outs, all_ref = refs[:4], refs[4]
    blocks, part_rows, wide = all_ref.shape
    columns = dqkv_ref.shape[1]
    half = gwo_ref.shape[1]
    each = 128
    for start in range(0, columns, each * 3):
        stop = start + each * 3
        part = tn(normed_ref[...], dqkv_ref[:, start:stop])
        all_ref[:, :, start:stop] = part.reshape(blocks, part_rows, stop - start)
    all_ref[:, :, columns : columns + half] = gwo_ref[...].reshape(blocks, part_rows, half)
    all_ref[:, :, columns + half :] = small_ref[...].reshape(blocks, part_rows, wide - columns - half)
    for kk in range(2):
        for side in range(2):
            ref = outs[2 * kk + side]
            for j in range(ref.shape[0]):
                m = orders[kk][side * ref.shape[0] + j]
                for i in range(ref.shape[1]):
                    place = at_ref[FLAT] ^ ((2 * m + kk) * ref.shape[1] + i)
                    ref[j, i] = all_ref[place].astype(ref.dtype)


def final_shared_kernel(at_ref, *refs, half):
    parts, (qkv_ref, out_ref, scale_ref, shift_ref) = refs[:-4], refs[-4:]
    total = parts[0][...].astype(f32)
    for part in parts[1:]:
        total = total + part[...].astype(f32)
    norms = total[0][:, 4 * half :] + total[1][:, 4 * half :]
    row = lax.broadcasted_iota(jnp.int32, (8, norms.shape[1]), 0)
    lane = lax.broadcasted_iota(jnp.int32, (8, norms.shape[1]), 1)
    turned = lax.dot_general(
        jnp.where(row == lane, 1.0, 0.0),
        norms,
        (((1,), (1,)), ((), ())),
        precision=lax.Precision.HIGHEST,
        preferred_element_type=f32,
    )
    scale_ref[...] = turned[0:2]
    shift_ref[...] = turned[2:4]

    def fill(core):
        for mine in range(2):
            which = core ^ mine
            for group in range(3):
                start = (2 * group + which) * half
                qkv_ref[:, start : start + half] = total[mine][:, group * half : (group + 1) * half]
            out_ref[:, which * half : (which + 1) * half] = total[mine][:, 3 * half : 4 * half]

    pl.when(at_ref[CORE] == 0)(lambda: fill(0))
    pl.when(at_ref[CORE] == 1)(lambda: fill(1))


def make_local(exp_size, seq_size):
    cols = exp_size // 2
    col_bits = cols.bit_length() - 1
    near = [m for m in range(1, cols) if m & (m - 1) == 0]
    far = [m for m in range(1, cols) if m & (m - 1)]
    groups = [[0], near, far]

    def flat_perm(target):
        pairs = []
        for exp in range(exp_size):
            for seq in range(seq_size):
                col, core = exp >> 1, exp & 1
                new_col, new_core, new_seq = target(col, core, seq)
                pairs.append((exp * seq_size + seq, (new_col * 2 + new_core) * seq_size + new_seq))
        return pairs

    def send(array, target):
        return lax.ppermute(array, BOTH, flat_perm(target))

    def to_core(array):
        return send(array, lambda c, k, z: (c, 1 - k, z))

    def to_seq(array, shift):
        return send(array, lambda c, k, z: (c, k, z ^ shift))

    def to_col(array, bit):
        return send(array, lambda c, k, z: (c ^ (1 << bit), k, z))

    def exchange(pairs):
        came = exchange_near(pairs)
        return exchange_far(pairs, came)

    def chip_send(m, pair):
        return send(pair, lambda c, k, z: (c ^ m, k, z))

    def exchange_near(pairs):
        return {0: pairs[0], **{m: chip_send(m, pairs[m]) for m in near}}

    def exchange_far(pairs, came):
        waits = [came[m] for m in near]
        rest = {m: chip_send(m, after(pairs[m], waits)) for m in far}
        return [rest[m] if m in rest else came[m] for m in range(cols)]

    def with_other(pairs):
        return [part for pair in pairs for part in (pair, to_core(pair))]

    def home_of(i):
        return lambda c, k, z: (c, z >> 1, (2 * k + (z & 1)) ^ i)

    def worker_of(i):
        return lambda c, k, z: (c, (z ^ i) >> 1, 2 * k + ((z ^ i) & 1))

    def step_bits(kk):
        return list(range(col_bits))[:: 1 - 2 * kk]

    def local(
        tokens,
        cotangent,
        token_ids,
        segments,
        hash_table,
        w_qkv,
        w_attn_out,
        norm_scale,
        norm_shift,
        w_in,
        w_out,
    ):
        seq_dev, rows_seq, width = tokens.shape
        rows = seq_dev * rows_seq
        slot_rows = 3 * rows // exp_size
        full_len = rows_seq * seq_size
        half = width // 2
        wide = 4 * half + LANES
        part_rows = w_qkv.shape[0]
        blocks = seq_size * 2 * cols
        w_in, w_out = w_in[0], w_out[0]
        exp_at = lax.axis_index("exp")
        z = lax.axis_index("seq")
        k = exp_at & 1
        is_one = k == 1
        z0 = z & 1
        at = jnp.stack([k, exp_at * seq_size + z, z0, z, exp_at, 2 * k + z0]).astype(jnp.int32)

        norms = jnp.concatenate([norm_scale, norm_shift], axis=1)
        norms = jnp.pad(norms, ((0, 0), (0, LANES - norms.shape[1])))
        pack = jnp.concatenate([w_qkv, w_attn_out, norms], axis=1)
        got = [pack] + [to_seq(pack, i) for i in range(1, seq_size)]
        seg_pair = jnp.where((z >> 1) == k, segments, to_core(segments))
        seg_row = jnp.where(z0 == 1, seg_pair[1:2], seg_pair[0:1])

        expert = hash_table[token_ids.reshape(-1)]
        order = jnp.arange(rows, dtype=jnp.int32)
        earlier = (expert[None, :] == expert[:, None]) & (order[None, :] < order[:, None])
        slot_rank = jnp.sum(earlier.astype(jnp.int32), axis=1)
        slots = exp_size * slot_rows
        slot_index = expert * slot_rows + slot_rank
        slot_near = (expert ^ exp_at) * slot_rows + slot_rank
        spread = (jnp.arange(slots, dtype=jnp.int32)[:, None] == slot_index[None, :]).astype(bf16)

        def swap(array):
            return lax.all_to_all(
                array.reshape(exp_size, slot_rows, width),
                "exp",
                split_axis=0,
                concat_axis=0,
                tiled=True,
            )

        grad_low = cotangent.reshape(rows, width)
        grad_packed = nn(spread, grad_low).astype(bf16)
        got, _ = lax.optimization_barrier((got, (grad_packed, slot_near, seg_row)))
        mine, other = single_call(
            functools.partial(split_kernel, half=half, parts=seq_size),
            at,
            got,
            [shape(bf16, seq_size, part_rows, wide)] * 2,
            "split_cores",
        )
        pair = [jnp.where(z0 == 1, tokens[1 - i], tokens[i]) for i in range(2)]
        here = [send(pair[0], home_of(0)), send(pair[1], home_of(1))]
        x_half = jnp.concatenate(
            [jnp.where(z0 == 1, here[1 - i], here[i]) for i in range(2)], axis=0
        )
        pieces = [[mine], [to_core(other)]]
        x_other = None
        for step in range(col_bits):
            if step == 1:
                pieces, x_half = lax.optimization_barrier((pieces, x_half))
                x_other = to_core(x_half)
            pieces = [
                own + [to_col(piece, step_bits(kk)[step]) for piece in own]
                for kk, own in enumerate(pieces)
            ]
        ordered = []
        for kk in range(2):
            bits = step_bits(kk)
            by_place = {}
            for index, piece in enumerate(pieces[kk]):
                place = sum(1 << bits[step] for step in range(col_bits) if (index >> step) & 1)
                by_place[place] = piece
            ordered += [by_place[place] for place in range(cols)]
        wq, wo_own, norm_rows, hat, normed, qkv = single_call(
            functools.partial(norm_qkv_kernel, half=half, parts=seq_size, cols=cols),
            at,
            [*ordered, x_half, x_other],
            [
                shape(bf16, blocks, part_rows, 3 * half),
                shape(bf16, blocks, part_rows, half),
                shape(f32, 8, width),
                shape(bf16, full_len, width),
                shape(bf16, full_len, width),
                shape(bf16, full_len, 3 * half),
            ],
            "norm_qkv",
            flops=2 * full_len * width * 3 * half,
            scratch=[pltpu.VMEM((blocks, part_rows, LANES), f32)],
        )
        wq = wq.reshape(width, 3 * half)
        wo_own = wo_own.reshape(width, half)
        gain_one, gain_two, bias_two = norm_rows[0:1], norm_rows[1:2], norm_rows[3:4]
        grad_arrived = swap(after(grad_packed, qkv))
        att, lse, *chunks = attend(at, qkv, seg_row, seq_size)
        wo_other = to_core(wo_own)
        wo = jnp.concatenate(
            [jnp.where(is_one, wo_other, wo_own), jnp.where(is_one, wo_own, wo_other)], axis=1
        )
        quads = [send(chunks[i], home_of(i)) for i in range(seq_size)]
        quads, grad_arrived = lax.optimization_barrier((quads, grad_arrived))
        x_home = tokens.reshape(rows, width)
        att_home, middle, *packs = single_call(
            mix_kernel,
            at,
            [*quads, x_home, wo, gain_two, bias_two, slot_near[None, :]],
            [shape(bf16, rows, width), shape(f32, rows, width)]
            + [shape(bf16, 2, slot_rows, width)] * cols,
            "mix",
            flops=2 * rows * width * (width + slots),
        )

        arrived = exchange(packs)
        hidden = []
        for members in groups:
            pairs = [arrived[m] for m in members]
            if hidden:
                pairs = after(pairs, hidden[-1])
            earlier = hidden if len(hidden) == 2 else ()
            hidden.append(
                hidden_group(
                    at, with_other(pairs), grad_arrived, members, w_in, w_out, earlier
                )
            )
        grad_outer = hidden[2][4]
        hidden[2] = hidden[2][:4]
        acts, dpres, sents, grads = zip(*hidden)
        grad_w_out = lax.psum_scatter(grad_outer, "seq", scatter_dimension=0, tiled=True)
        dpres = after(dpres, grad_outer)
        grad_sents = {}
        for i in (1, 2, 0):
            parts = back_group(at, dpres[i], w_in, groups[i])
            grad_sents.update(zip(groups[i], parts))
            dpres = after(dpres, parts)
        grad_back = exchange([grad_sents[m] for m in range(cols)])
        expert_out = out_rows(at, after(acts, dpres), w_out, groups)
        grad_back = with_other(after(grad_back, expert_out))
        expert_out = after(expert_out, grad_back)
        returned_near = exchange_near(expert_out)

        outs = [
            *(shape(f32, rows, width), shape(bf16, rows, width), shape(f32, 8, width)),
            *[shape(bf16, rows_seq, half)] * seq_size,
        ]
        grad_middle, grad_branch, sums_two, *quads = kernel_call(
            functools.partial(mid_back_kernel, owners=exp_size),
            1,
            at,
            [*grad_back, middle, grad_low, wo, gain_two, slot_near[:, None]],
            pair_specs(exp_size, slot_rows, width) + [None] * 5,
            [None] * len(outs),
            outs,
            2 * rows * width * (width + slots),
            "mid_back",
            [pltpu.VMEM((slots, width), bf16), pltpu.VMEM((rows, width), bf16)],
        )

        quads, returned_near = lax.optimization_barrier((quads, returned_near))
        came = [send(quads[i], worker_of(i)) for i in range(seq_size)]
        returned = exchange_far(expert_out, returned_near)
        grad_inner = grad_in_weight(at, sents, after(dpres, quads))
        grad_w_in = lax.psum_scatter(
            after(grad_inner, came), "seq", scatter_dimension=1, tiled=True
        )
        grad_wo = tn(att_home, grad_branch)
        wo_halves = [grad_wo[:, :half], grad_wo[:, half:]]
        grad_wo = jnp.where(is_one, wo_halves[1], wo_halves[0]) + to_core(
            jnp.where(is_one, wo_halves[0], wo_halves[1]).astype(bf16)
        ).astype(f32)
        came = after(came, grad_wo)
        dqkv, own, other, sums_one = attend_back(at, qkv, att, lse, seg_row, hat, came, wq)
        other = to_core(other)
        small = jnp.stack([sums_one[0], sums_two[0], sums_one[1], sums_two[1]])
        small = jnp.pad(small, ((0, LANES - 4), (0, 0))).T
        orders = [
            sorted(range(cols), key=lambda m, kk=kk: [(m >> bit) & 1 for bit in step_bits(kk)])
            for kk in range(2)
        ]
        stay_go = single_call(
            functools.partial(grad_shared_kernel, orders=orders),
            at,
            [normed, dqkv, grad_wo, small],
            [shape(bf16, cols // 2, seq_size, part_rows, wide)] * 4,
            "grad_shared",
            flops=2 * full_len * width * 3 * half,
            scratch=[pltpu.VMEM((blocks, part_rows, wide), f32)],
        )
        returned = with_other(returned)
        stay_go, returned = lax.optimization_barrier((stay_go, returned))
        wide_w_out = grad_w_out.astype(f32)[None]
        sums = []
        for kk in range(2):
            stay, go = stay_go[2 * kk], stay_go[2 * kk + 1]
            for step in range(col_bits):
                came = to_col(go, step_bits(kk)[step])
                if step == 0:
                    came = after(came, wide_w_out)
                both = stay.astype(f32) + came.astype(f32)
                if step + 1 < col_bits:
                    count = both.shape[0] // 2
                    stay, go = both[:count], both[count:].astype(bf16)
            sums.append(both[0])
        lined = jnp.stack([sums[0].astype(bf16), to_core(sums[1].astype(bf16))], axis=1)
        own_late, lined = lax.optimization_barrier((own, lined))
        parts = [lined[0]] + [to_seq(lined[i], i) for i in range(1, seq_size)]
        back_a, back_b = single_call(
            home_rows_kernel,
            at,
            [own_late, other, x_half, gain_one],
            [shape(bf16, rows_seq, width)] * 2,
            "home_rows",
        )
        layer_out = kernel_call(
            functools.partial(layer_out_kernel, owners=exp_size),
            1,
            at,
            [*returned, middle, slot_near[:, None]],
            pair_specs(exp_size, slot_rows, width) + [None, None],
            [None],
            [shape(bf16, rows, width)],
            2 * rows * width * slots,
            "layer_out",
            [pltpu.VMEM((slots, width), bf16)],
        )[0]
        wide_w_in = grad_w_in.astype(f32)[None]
        (grad_tokens,) = single_call(
            tokens_kernel,
            at,
            [
                *[send(part, home_of(i)) for i, part in enumerate((back_a, back_b))],
                after(grad_middle, wide_w_in),
            ],
            [shape(f32, rows, width)],
            "tokens",
        )

        grad_w_qkv, grad_w_attn_out, grad_norm_scale, grad_norm_shift = single_call(
            functools.partial(final_shared_kernel, half=half),
            at,
            parts,
            [
                shape(f32, part_rows, 6 * half),
                shape(f32, part_rows, 2 * half),
                shape(f32, 2, part_rows),
                shape(f32, 2, part_rows),
            ],
            "final_shared",
        )
        return (
            layer_out.reshape(seq_dev, rows_seq, width),
            grad_tokens.reshape(seq_dev, rows_seq, width),
            grad_w_qkv,
            grad_w_attn_out,
            grad_norm_scale.T,
            grad_norm_shift.T,
            wide_w_in,
            wide_w_out,
        )

    return local


def solution(mesh):
    return jax.shard_map(
        make_local(mesh.shape["exp"], mesh.shape["seq"]),
        mesh=mesh,
        in_specs=(
            P("exp", "seq", None),
            P("exp", "seq", None),
            P("exp", "seq"),
            P("exp", None),
            P(),
            P(("exp", "seq"), None),
            P(("exp", "seq"), None),
            P(("exp", "seq"), None),
            P(("exp", "seq"), None),
            P("exp", None, None),
            P("exp", None, None),
        ),
        out_specs=(
            P("exp", "seq", None),
            P("exp", "seq", None),
            P(("exp", "seq"), None),
            P(("exp", "seq"), None),
            P(("exp", "seq"), None),
            P(("exp", "seq"), None),
            P("exp", None, "seq"),
            P("exp", "seq", None),
        ),
        check_vma=False,
    )
```
